512 devices in a mesh: angle: 16 (over z_lo, core), slab: 4 (over x), tile: 8 (over y, z_hi).
Axes of the slice: x: 4, y: 4, z: 16 (z_hi: 2, z_lo: 8; z = z_hi * 8 + z_lo), core: 2. Of those that a mesh axis runs over, the one named last changes fastest.
Arguments:
- volume: bfloat16 [2, 4, 1536, 1536], P(None, 'slab', 'tile'), may hold values from -2 to 2
- probe_wave: float32 [2, 256, 256], replicated, may hold values from -6 to 6
- amplitudes: bfloat16 [16, 8, 4, 2, 256, 256], P('angle', 'tile', 'slab'), may hold values from 0.099609375 to 3
- offsets: int32 [16, 8, 4, 2], P('angle', 'tile', 'slab'), may hold values from 0 to 128
- column_starts: int32 [16, 8, 4, 2], P('angle', 'tile', 'slab'), may hold values from 0 to 1280
- counts: int32 [16, 8, 4], P('angle', 'tile', 'slab'), may hold values from 1 to 2, as said below
- angle_ids: int32 [16], P('angle'), may hold values from 0 to 1199
Outputs:
- new_volume: float32 [2, 4, 1536, 1536], P(None, 'slab', 'tile')
The draws below stay inside these ranges and needn't reach their ends.
Inputs may be any that keep to these rules, and one draw needn't show every extreme that they name: counts gives the live slots of one device; slots at or beyond it are ignored; in every draw some device has 2.
All inputs are finite; a program needn't handle non-finite values.
Results may differ from the reference program's by a relative error of at most 0.04.
Values may be sent and summed in bfloat16 or wider, within the bound.
No kernel may reach another device: no remote copies, remote signals or barrier semaphores. Data moves between devices by JAX's collectives and lax.ppermute only.
A program may use at most 64 MiB of HBM per device.

```python
import math
import jax
import jax.numpy as jnp
from jax import lax

PATCH = 256
COLS = 1536
TILE_ROWS = 192
POS_CAP = 2
ANGLES = 16
TILES = 8
SLABS = 4
DEPTH = 4
ROWS = 1536


def draw_counts(key, part):
    key = jax.random.fold_in(key, 7)
    uniform_draw = jax.random.randint(key, (ANGLES, TILES, SLABS), 0, POS_CAP)
    live_count = 1 + uniform_draw * uniform_draw // POS_CAP
    return live_count.at[0, 0, 0].set(POS_CAP).astype(jnp.int32)


def with_ends(values, stream_key, least, largest):
    longest = values.shape.index(max(values.shape))
    spots = []
    for shift in (0, 1):
        where = [jax.random.randint(jax.random.fold_in(stream_key, axis), (), 0, length) for axis, length in enumerate(values.shape)]
        where[longest] = (where[longest] + shift) % values.shape[longest]
        spots.append(tuple(where))
    return values.at[spots[0]].set(least).at[spots[1]].set(largest)


def shard_levels(rng, dims, cuts, smallest, high):
    def one(position, parts):
        steps = jax.random.uniform(jax.random.fold_in(jax.random.fold_in(rng, 6), position), (parts,), jnp.float32, smallest / len(cuts), high / len(cuts))
        return jnp.repeat(jnp.exp(steps), dims[position] // parts).reshape((-1,) + (1,) * (len(dims) - position - 1))

    level = one(*cuts[0])
    for cut in cuts[1:]:
        level = level * one(*cut)
    return level


def centred(key, extent, spread, bound, cuts=(), held_as=jnp.bfloat16):
    values = jax.random.normal(key, extent, jnp.float32) * spread
    if len(cuts) > 0:
        values = shard_levels(key, extent, cuts, -0.22, 0.18) * values
    return jnp.clip(values, min=-bound, max=bound).astype(held_as)


def setup_inputs(seed: int = 0) -> dict:
    seeds = jax.random.split(jax.random.key(seed), 8)
    return {
        "volume": centred(seeds[0], (2, DEPTH, ROWS, COLS), 0.25, 2.0, ((1, 4), (2, 8))),
        "probe_wave": centred(seeds[1], (2, PATCH, PATCH), 1.0, 6.0, (), jnp.float32),
        "amplitudes": jnp.clip(jnp.exp(math.log(3.0) - 3.4051113 * jax.random.uniform(seeds[2], (ANGLES, TILES, SLABS, POS_CAP, PATCH, PATCH), jnp.float32) ** shard_levels(seeds[2], (ANGLES, TILES, SLABS, POS_CAP, PATCH, PATCH), ((0, 16), (1, 8), (2, 4)), -0.2, 0.2)), 0.099609375, 3.0).astype(jnp.bfloat16),
        "offsets": with_ends(jax.random.randint(seeds[3], (ANGLES, TILES, SLABS, POS_CAP), 0, min(TILE_ROWS, 2 * TILE_ROWS - PATCH + 1)), jax.random.fold_in(seeds[3], 1), 0, (min(TILE_ROWS, 2 * TILE_ROWS - PATCH + 1)) - 1).astype(jnp.int32),
        "column_starts": with_ends(jax.random.randint(seeds[4], (ANGLES, TILES, SLABS, POS_CAP), 0, COLS - PATCH + 1), jax.random.fold_in(seeds[4], 1), 0, COLS - PATCH).astype(jnp.int32),
        "counts": draw_counts(jax.random.fold_in(seeds[7], 71), 0),
        "angle_ids": with_ends(jax.random.randint(seeds[6], (ANGLES,), 0, 1200), jax.random.fold_in(seeds[6], 1), 0, 1199).astype(jnp.int32),
    }


angle_center = 600
shear_divisor = 64
step_size = 0.03
floor_square = 0.25

def dft_tables(plane_width):
    index_line = jnp.arange(plane_width, dtype=jnp.int32)
    product_mod = jnp.mod(index_line[:, None] * index_line[None, :], plane_width)
    phase_table = product_mod.astype(jnp.float32) * (2.0 * 3.141592653589793 / plane_width)
    scale_factor = plane_width ** (-0.5)
    table_real = (jnp.cos(phase_table) * scale_factor).astype(jnp.bfloat16)
    table_imag = (-jnp.sin(phase_table) * scale_factor).astype(jnp.bfloat16)
    return (table_real, table_imag)

def shear_shifts(angle_value, first_layer, layer_count, total_depth, column_count):
    layer_index = first_layer + jnp.arange(layer_count, dtype=jnp.int32)
    offset_layer = layer_index - total_depth // 2
    sheared = jnp.floor_divide((angle_value - angle_center) * offset_layer, shear_divisor)
    return jnp.mod(sheared, column_count).astype(jnp.int32)

def twodot(left_matrix, right_matrix):
    return jnp.dot(left_matrix, right_matrix, preferred_element_type=jnp.float32)

def patch_gradient(window, probe_wave, pattern, table_real, table_imag):
    window_wide = window.astype(jnp.float32)
    trans_mag = jnp.exp(-window_wide[1])
    trans_real = trans_mag * jnp.cos(window_wide[0])
    trans_imag = trans_mag * jnp.sin(window_wide[0])
    wave_real = (probe_wave[0] * trans_real - probe_wave[1] * trans_imag).astype(jnp.bfloat16)
    wave_imag = (probe_wave[0] * trans_imag + probe_wave[1] * trans_real).astype(jnp.bfloat16)
    left_real = (twodot(table_real, wave_real) - twodot(table_imag, wave_imag)).astype(jnp.bfloat16)
    left_imag = (twodot(table_real, wave_imag) + twodot(table_imag, wave_real)).astype(jnp.bfloat16)
    far_real = twodot(left_real, table_real) - twodot(left_imag, table_imag)
    far_imag = twodot(left_real, table_imag) + twodot(left_imag, table_real)
    ratio = pattern.astype(jnp.float32) / jnp.sqrt(far_real * far_real + far_imag * far_imag + floor_square)
    keeping = 1.0 - ratio
    resid_real = (far_real * keeping).astype(jnp.bfloat16)
    resid_imag = (far_imag * keeping).astype(jnp.bfloat16)
    back_real = (twodot(table_real, resid_real) + twodot(table_imag, resid_imag)).astype(jnp.bfloat16)
    back_imag = (twodot(table_real, resid_imag) - twodot(table_imag, resid_real)).astype(jnp.bfloat16)
    exit_real = twodot(back_real, table_real) + twodot(back_imag, table_imag)
    exit_imag = twodot(back_imag, table_real) - twodot(back_real, table_imag)
    mixed_real = probe_wave[0] * exit_real + probe_wave[1] * exit_imag
    mixed_imag = probe_wave[0] * exit_imag - probe_wave[1] * exit_real
    final_real = trans_real * mixed_real + trans_imag * mixed_imag
    final_imag = trans_real * mixed_imag - trans_imag * mixed_real
    return jnp.stack([final_imag, -final_real])

def slot_update(buffer, extended, start_row, start_column, pattern, probe_wave, table_real, table_imag):
    plane_width = pattern.shape[-1]
    zero_index = jnp.zeros((), jnp.int32)
    corner = (zero_index, start_row.astype(jnp.int32), start_column.astype(jnp.int32))
    window = lax.dynamic_slice(extended, corner, (2, plane_width, plane_width))
    gradient = patch_gradient(window, probe_wave, pattern, table_real, table_imag)
    previous = lax.dynamic_slice(buffer, corner, (2, plane_width, plane_width))
    return lax.dynamic_update_slice(buffer, previous + gradient, corner)

def keep_buffer(buffer):
    return buffer

def reference(volume, probe_wave, amplitudes, offsets, column_starts, counts, angle_ids):
    total_depth = volume.shape[1]
    row_count = volume.shape[2]
    column_count = volume.shape[3]
    plane_width = amplitudes.shape[-1]
    tile_count = counts.shape[1]
    slab_count = counts.shape[2]
    capacity = offsets.shape[3]
    tile_rows = row_count // tile_count
    layer_count = total_depth // slab_count
    slot_total = tile_count * capacity
    table_real, table_imag = dft_tables(plane_width)

    def one_angle(gradient_sum, inputs):
        angle_value, patterns, row_starts, col_starts, live_counts = inputs
        shifts = shear_shifts(angle_value, 0, total_depth, total_depth, column_count)

        def slab_partial(slab_index):

            def add_layer(running, within):
                layer_index = slab_index * layer_count + within
                layer_field = lax.dynamic_index_in_dim(volume, layer_index, 1, keepdims=False)
                rolled = jnp.roll(layer_field, -shifts[layer_index], axis=-1)
                return (running + rolled.astype(jnp.float32), None)
            partial_value, _ = lax.scan(add_layer, jnp.zeros((2, row_count, column_count), jnp.float32), jnp.arange(layer_count, dtype=jnp.int32))
            return partial_value.astype(jnp.bfloat16)

        def add_partial(running, slab_index):
            return (running + slab_partial(slab_index).astype(jnp.float32), None)
        projection_wide, _ = lax.scan(add_partial, jnp.zeros((2, row_count, column_count), jnp.float32), jnp.arange(slab_count, dtype=jnp.int32))
        projection = projection_wide.astype(jnp.bfloat16)
        extended = jnp.concatenate([projection, jnp.zeros((2, tile_rows, column_count), jnp.bfloat16)], axis=1)

        def one_slab(plane_sum, slab_index):
            slab_patterns = lax.dynamic_index_in_dim(patterns, slab_index, 1, keepdims=False)
            slab_patterns = slab_patterns.reshape(slot_total, plane_width, plane_width)
            slab_rows = lax.dynamic_index_in_dim(row_starts, slab_index, 1, keepdims=False).reshape(slot_total)
            slab_cols = lax.dynamic_index_in_dim(col_starts, slab_index, 1, keepdims=False).reshape(slot_total)
            slab_live = lax.dynamic_index_in_dim(live_counts, slab_index, 1, keepdims=False)

            def one_slot(buffer, slot_index):
                tile_index = slot_index // capacity
                within = slot_index % capacity
                is_live = within < slab_live[tile_index]
                start_row = (tile_index * tile_rows + slab_rows[slot_index]).astype(jnp.int32)

                def add_patch(current):
                    return slot_update(current, extended, start_row, slab_cols[slot_index], slab_patterns[slot_index], probe_wave, table_real, table_imag)
                return (lax.cond(is_live, add_patch, keep_buffer, buffer), None)
            buffer, _ = lax.scan(one_slot, jnp.zeros(extended.shape, jnp.float32), jnp.arange(slot_total, dtype=jnp.int32))
            rounded = buffer[:, :row_count].astype(jnp.bfloat16)
            return (plane_sum + rounded.astype(jnp.float32), None)
        plane_gradient, _ = lax.scan(one_slab, jnp.zeros((2, row_count, column_count), jnp.float32), jnp.arange(slab_count, dtype=jnp.int32))
        layer_gradient = jax.vmap(lambda amount: jnp.roll(plane_gradient, amount, axis=-1))(shifts)
        return (gradient_sum + jnp.moveaxis(layer_gradient, 0, 1), None)
    gradient_sum, _ = lax.scan(one_angle, jnp.zeros(volume.shape, jnp.float32), (angle_ids, amplitudes, offsets, column_starts, counts))
    return volume.astype(jnp.float32) - step_size * gradient_sum
```

```python
import functools

import jax
import jax.numpy as jnp
import ml_dtypes
import numpy as np
from jax import lax
from jax.experimental import pallas as pl
from jax.experimental.pallas import tpu as pltpu
from jax.sharding import PartitionSpec as P

angle_center = 600
shear_divisor = 64
step_size = 0.03
floor_square = 0.25

LANE = 128
HALO = 64
SMEM = pl.BlockSpec(memory_space=pltpu.SMEM)
VMEM = pl.BlockSpec(memory_space=pltpu.VMEM)


def dft_tables(plane_width):
    index_line = np.arange(plane_width, dtype=np.int32)
    product_mod = np.mod(index_line[:, None] * index_line[None, :], plane_width)
    phase_table = product_mod.astype(np.float32) * np.float32(2.0 * 3.141592653589793 / plane_width)
    scale_factor = np.float32(plane_width ** (-0.5))
    table_real = (np.cos(phase_table) * scale_factor).astype(ml_dtypes.bfloat16)
    table_imag = (-np.sin(phase_table) * scale_factor).astype(ml_dtypes.bfloat16)
    return table_real, table_imag


def dot(left, right):
    return jnp.dot(left, right, preferred_element_type=jnp.float32)


def one_hot(rows, columns, down):
    row = lax.broadcasted_iota(jnp.int32, (rows, columns), 0)
    column = lax.broadcasted_iota(jnp.int32, (rows, columns), 1)
    return (row - column == down).astype(jnp.float32).astype(jnp.bfloat16)


def call(body, out_shape, in_specs, scratch=()):
    return pl.pallas_call(
        body,
        out_shape=out_shape,
        in_specs=in_specs,
        out_specs=jax.tree.map(lambda _: VMEM, out_shape),
        scratch_shapes=scratch,
        compiler_params=pltpu.CompilerParams(vmem_limit_bytes=48 * 1024 * 1024),
    )


def cut_body(columns, place_ref, volume_ref, *outs):
    rows, width = outs[0].shape[1:]
    blocks = columns // LANE

    for n, out in enumerate(outs):
        top, left, live = (place_ref[3 * n + i] for i in range(3))

        @pl.when(live > 0)
        def _():
            block, inside = left // LANE, left % LANE
            pick_rows = one_hot(rows, volume_ref.shape[1], -top)
            pick_columns = one_hot(width + LANE, width, inside)
            for part in range(2):
                pieces = []
                for i in range(width // LANE + 1):
                    start = pl.multiple_of(lax.rem(block + i, blocks) * LANE, LANE)
                    pieces.append(volume_ref[part, :, pl.ds(start, LANE)])
                narrow = dot(jnp.concatenate(pieces, axis=1), pick_columns).astype(jnp.bfloat16)
                out[part] = dot(pick_rows, narrow).astype(jnp.bfloat16)

        @pl.when(live == 0)
        def _():
            out[...] = jnp.zeros_like(out)


def cut_windows(place, layer, count, rows, width):
    shape = jax.ShapeDtypeStruct((2, rows, width), jnp.bfloat16)
    return call(
        functools.partial(cut_body, layer.shape[2]), [shape] * count, [SMEM, VMEM]
    )(place, layer)


def patch_body(
    live_ref, upper0, upper1, upper2, upper3, lower, probe, pattern, wr_ref, wi_ref, up_out, low_out
):
    @pl.when(live_ref[0] > 0)
    def _():
        rows = upper0.shape[1]
        f32, bf16 = jnp.float32, jnp.bfloat16

        def window(part):
            above = sum(u[part].astype(f32) for u in (upper0, upper1, upper2, upper3))
            above = above.astype(bf16).astype(f32)
            below = lower[part].astype(f32)
            return jnp.concatenate(
                [above[:HALO], above[HALO:] + below[: rows - HALO], below[rows - HALO :]], axis=0
            )

        phase, absorption = window(0), window(1)
        magnitude = jnp.exp(-absorption)
        trans_real = magnitude * jnp.cos(phase)
        trans_imag = magnitude * jnp.sin(phase)
        probe_real, probe_imag = probe[0], probe[1]
        wr, wi = wr_ref[...], wi_ref[...]
        wave_real = (probe_real * trans_real - probe_imag * trans_imag).astype(bf16)
        wave_imag = (probe_real * trans_imag + probe_imag * trans_real).astype(bf16)
        left_real = (dot(wr, wave_real) - dot(wi, wave_imag)).astype(bf16)
        left_imag = (dot(wr, wave_imag) + dot(wi, wave_real)).astype(bf16)
        far_real = dot(left_real, wr) - dot(left_imag, wi)
        far_imag = dot(left_real, wi) + dot(left_imag, wr)
        power = far_real * far_real + far_imag * far_imag + floor_square
        keeping = 1.0 - pattern[...].astype(f32) * lax.rsqrt(power)
        resid_real = (far_real * keeping).astype(bf16)
        resid_imag = (far_imag * keeping).astype(bf16)
        back_real = (dot(wr, resid_real) + dot(wi, resid_imag)).astype(bf16)
        back_imag = (dot(wr, resid_imag) - dot(wi, resid_real)).astype(bf16)
        exit_real = dot(back_real, wr) + dot(back_imag, wi)
        exit_imag = dot(back_imag, wr) - dot(back_real, wi)
        mixed_real = probe_real * exit_real + probe_imag * exit_imag
        mixed_imag = probe_real * exit_imag - probe_imag * exit_real
        final_real = trans_real * mixed_real + trans_imag * mixed_imag
        final_imag = trans_real * mixed_imag - trans_imag * mixed_real
        for part, value in enumerate((final_imag, -final_real)):
            value = value.astype(bf16)
            up_out[part] = value[:rows]
            low_out[part] = value[HALO:]

    @pl.when(live_ref[0] == 0)
    def _():
        up_out[...] = jnp.zeros_like(up_out)
        low_out[...] = jnp.zeros_like(low_out)


def patch_gradient(live, uppers, lower, probe_wave, pattern, tables):
    shape = jax.ShapeDtypeStruct(lower.shape, jnp.bfloat16)
    return call(patch_body, [shape] * 2, [SMEM] + [VMEM] * 9)(
        live, *uppers, lower, probe_wave, pattern, *tables
    )


def place_body(count, place_ref, *refs):
    windows, (keep_out, send_out, total) = refs[:count], refs[count:]
    rows, width = windows[0].shape[1:]
    blocks = total.shape[2] // LANE
    total[...] = jnp.zeros_like(total)
    for n, window in enumerate(windows):
        top, left, live = (place_ref[3 * n + i] for i in range(3))

        @pl.when(live > 0)
        def _():
            block, inside = left // LANE, left % LANE
            put_rows = one_hot(total.shape[1], rows, top)
            put_columns = one_hot(width, width + LANE, -inside)
            for part in range(2):
                moved = dot(put_rows, window[part]).astype(jnp.bfloat16)
                wide = dot(moved, put_columns)
                for i in range(width // LANE + 1):
                    start = pl.multiple_of(lax.rem(block + i, blocks) * LANE, LANE)
                    total[part, :, pl.ds(start, LANE)] += wide[:, i * LANE : (i + 1) * LANE]

    core = place_ref[3 * count]
    keep_out[...] = total[core]
    send_out[...] = total[1 - core].astype(jnp.bfloat16)


def place_windows(place, windows, tile_rows, columns):
    shapes = [
        jax.ShapeDtypeStruct((tile_rows, columns), jnp.float32),
        jax.ShapeDtypeStruct((tile_rows, columns), jnp.bfloat16),
    ]
    return call(
        functools.partial(place_body, len(windows)),
        shapes,
        [SMEM] + [VMEM] * len(windows),
        [pltpu.VMEM((2, tile_rows, columns), jnp.float32)],
    )(place, *windows)


def step_body(where_ref, volume_ref, *refs):
    out = refs[-1]
    core, group = where_ref[0], where_ref[1]
    blocks = (len(refs) - 1) // 2
    for n, ref in enumerate(refs[:-1]):
        part = core if n < blocks else 1 - core
        rows = ref.shape[0]
        start = pl.multiple_of((group ^ (n % blocks)) * rows, 16)
        old = volume_ref[part, pl.ds(start, rows), :].astype(jnp.float32)
        out[part, pl.ds(start, rows), :] = old - step_size * ref[...].astype(jnp.float32)


def step(where, layer, blocks):
    return call(
        step_body,
        jax.ShapeDtypeStruct(layer.shape, jnp.float32),
        [SMEM] + [VMEM] * (1 + len(blocks)),
    )(where, layer, *blocks)


def to_slab(value, by):
    count = lax.axis_size("slab")
    return lax.ppermute(value, "slab", [(i, (i + by) % count) for i in range(count)])


def to_tile(value, by):
    count = lax.axis_size("tile")
    pairs = [(i, i + by) for i in range(count) if 0 <= i + by < count]
    return lax.ppermute(value, "tile", pairs)


def to_next_tile_and_slab(value, by):
    tiles, slabs = lax.axis_size("tile"), lax.axis_size("slab")
    pairs = [
        (s * tiles + t, (s + by) % slabs * tiles + t + 1) for t in range(tiles - 1) for s in range(slabs)
    ]
    return lax.ppermute(value, ("slab", "tile"), pairs)


def swap_angle(value, mask):
    return lax.ppermute(value, "angle", [(i, i ^ mask) for i in range(lax.axis_size("angle"))])


def per_device(volume, probe_wave, amplitudes, offsets, column_starts, counts, angle_ids):
    layer = volume.reshape(volume.shape[0], *volume.shape[2:])
    tile_rows, columns = layer.shape[1:]
    width = amplitudes.shape[-1]
    capacity = offsets.shape[3]
    slabs = lax.axis_size("slab")
    slab = lax.axis_index("slab")
    angle = lax.axis_index("angle")
    core, group, far = angle & 1, (angle >> 1) & 3, angle >> 3
    f32, bf16 = jnp.float32, jnp.bfloat16
    tables = dft_tables(width)
    window_rows = width - HALO
    patterns = amplitudes.reshape(capacity, width, width)

    sheared = jnp.floor_divide((angle_ids[0] - angle_center) * (slab - slabs // 2), shear_divisor)
    shift = jnp.mod(sheared, columns)
    live = (jnp.arange(capacity) < counts.reshape(1)).astype(jnp.int32)
    meta = jnp.stack([offsets.reshape(capacity), column_starts.reshape(capacity), live], axis=1)
    own_meta = [meta] + [to_slab(meta, -k) for k in range(1, slabs)]
    before_meta = [to_next_tile_and_slab(meta, -k) for k in range(slabs)]

    def place(metas, down):
        table = jnp.stack(metas)
        top = table[..., 0] + down
        left = jnp.mod(table[..., 1] + shift, columns)
        return jnp.stack([top, left, table[..., 2]], axis=-1)

    below = HALO - tile_rows
    lower_cuts = cut_windows(
        place(before_meta, below).transpose(1, 0, 2).reshape(-1), layer, capacity * slabs, window_rows, width
    )
    upper_cuts = cut_windows(
        place(own_meta, 0).transpose(1, 0, 2).reshape(-1), layer, capacity * slabs, window_rows, width
    )

    def exchanged(cuts):
        return [cuts[0]] + [to_slab(cuts[k], k) for k in range(1, slabs)]

    lowers = []
    for slot in range(capacity):
        partials = exchanged(lower_cuts[slot * slabs : (slot + 1) * slabs])
        summed = sum(p.astype(f32) for p in partials).astype(bf16)
        lowers.append(to_tile(summed, -1))
    uppers = [exchanged(upper_cuts[slot * slabs : (slot + 1) * slabs]) for slot in range(capacity)]

    own_grads, before_grads = [], []
    for slot in range(capacity):
        up, low = patch_gradient(
            live[slot : slot + 1], uppers[slot], lowers[slot], probe_wave, patterns[slot], tables
        )
        own_grads.append([up] + [to_slab(up, k) for k in range(1, slabs)])
        low = to_tile(low, 1)
        before_grads.append([low] + [to_slab(low, k) for k in range(1, slabs)])

    order = [(slabs - k) % slabs for k in range(slabs)]
    places = [
        place([own_meta[k] for k in order], 0).transpose(1, 0, 2).reshape(-1),
        place([before_meta[k] for k in order], below).transpose(1, 0, 2).reshape(-1),
        core.reshape(1),
    ]
    kept, sent = place_windows(
        jnp.concatenate(places).astype(jnp.int32),
        [w for slot in own_grads for w in slot] + [w for slot in before_grads for w in slot],
        tile_rows,
        columns,
    )

    kept = kept + swap_angle(sent, 1).astype(f32)
    kept = kept.reshape(4, tile_rows // 4, columns)
    block = lambda k: lax.dynamic_index_in_dim(kept, group ^ k, 0, keepdims=False)
    arrived = [swap_angle(block(k).astype(bf16), k << 1) for k in range(1, 4)]
    mine = sum((a.astype(f32) for a in arrived), block(0))
    mine = mine.reshape(2, tile_rows // 8, columns)
    half = lambda k: lax.dynamic_index_in_dim(mine, far ^ k, 0, keepdims=False)
    done = (half(0) + swap_angle(half(1).astype(bf16), 8).astype(f32)).astype(bf16)

    other = swap_angle(done, 8)
    first = jnp.where(far == 0, done, other)
    second = jnp.where(far == 0, other, done)
    block0 = jnp.concatenate([first, second], axis=0)
    blocks = [block0] + [swap_angle(block0, k << 1) for k in range(1, 4)]
    blocks = blocks + [swap_angle(b, 1) for b in blocks]
    new = step(jnp.stack([core, group]).astype(jnp.int32), layer, blocks)
    return new.reshape(volume.shape)


def solution(mesh):
    in_specs = (
        P(None, "slab", "tile", None),
        P(),
        P("angle", "tile", "slab", None, None, None),
        P("angle", "tile", "slab", None),
        P("angle", "tile", "slab", None),
        P("angle", "tile", "slab"),
        P("angle"),
    )
    out_specs = P(None, "slab", "tile", None)
    return jax.shard_map(
        per_device, mesh=mesh, in_specs=in_specs, out_specs=out_specs, check_vma=False
    )
```

```python
import functools

import jax
import jax.numpy as jnp
import ml_dtypes
import numpy as np
from jax import lax
from jax.experimental import pallas as pl
from jax.experimental.pallas import tpu as pltpu
from jax.sharding import PartitionSpec as P

angle_center = 600
shear_divisor = 64
step_size = 0.03
floor_square = 0.25

LANE = 128
HALO = 64


def dft_tables(plane_width):
    index_line = np.arange(plane_width, dtype=np.int32)
    product_mod = np.mod(index_line[:, None] * index_line[None, :], plane_width)
    phase_table = product_mod.astype(np.float32) * np.float32(2.0 * 3.141592653589793 / plane_width)
    scale_factor = np.float32(plane_width ** (-0.5))
    table_real = (np.cos(phase_table) * scale_factor).astype(ml_dtypes.bfloat16)
    table_imag = (-np.sin(phase_table) * scale_factor).astype(ml_dtypes.bfloat16)
    return table_real, table_imag


def dot(left, right):
    return jnp.dot(left, right, preferred_element_type=jnp.float32)


def one_hot(rows, columns, down):
    row = lax.broadcasted_iota(jnp.int32, (rows, columns), 0)
    column = lax.broadcasted_iota(jnp.int32, (rows, columns), 1)
    return (row - column == down).astype(jnp.float32).astype(jnp.bfloat16)


def call(body, out_shape, scratch, *args):
    def spec(x):
        if x.dtype == jnp.int32:
            return pl.BlockSpec(memory_space=pltpu.SMEM)
        return pl.BlockSpec(x.shape, functools.partial(lambda rank, i: (0,) * rank, len(x.shape)))

    return pl.pallas_call(
        body,
        grid=(1,),
        out_shape=out_shape,
        in_specs=[spec(x) for x in args],
        out_specs=[spec(x) for x in out_shape],
        scratch_shapes=scratch,
        compiler_params=pltpu.CompilerParams(vmem_limit_bytes=56 * 1024 * 1024),
    )(*args)


def column_blocks(left, width, columns):
    blocks = columns // LANE
    return [
        pl.multiple_of(lax.rem(left // LANE + i, blocks) * LANE, LANE) for i in range(width // LANE + 1)
    ]


def cut_body(slabs, slots, place_ref, first_ref, second_ref, *outs):
    rows, width = outs[0].shape[2:]
    tile_rows, columns = first_ref.shape
    first_part = place_ref[3 * slabs * slots]
    for slab in range(slabs):
        for slot in range(slots):
            top, left, live = (place_ref[3 * (slab * slots + slot) + i] for i in range(3))
            out = outs[slot]

            @pl.when(live > 0)
            def _():
                pick_rows = one_hot(rows, tile_rows, -top)
                pick_columns = one_hot(width + LANE, width, lax.rem(left, LANE))
                starts = column_blocks(left, width, columns)
                for turn, ref in enumerate((first_ref, second_ref)):
                    pieces = [ref[:, pl.ds(start, LANE)] for start in starts]
                    narrow = dot(jnp.concatenate(pieces, axis=1), pick_columns).astype(jnp.bfloat16)
                    out[slab, first_part ^ turn] = dot(pick_rows, narrow).astype(jnp.bfloat16)

            @pl.when(live == 0)
            def _():
                out[slab] = jnp.zeros(out.shape[1:], out.dtype)


def cut_windows(place, first_part, first, second, rows, width):
    slabs, slots = place.shape[:2]
    shape = jax.ShapeDtypeStruct((slabs, 2, rows, width), jnp.bfloat16)
    scalars = jnp.concatenate([place.reshape(-1), first_part.reshape(1)]).astype(jnp.int32)
    return call(
        functools.partial(cut_body, slabs, slots), [shape] * slots, [], scalars, first, second
    )


def patch_body(slots, live_ref, *refs):
    uppers, lowers = refs[:slots], refs[slots : 2 * slots]
    probe, patterns, wr_ref, wi_ref = refs[2 * slots : 2 * slots + 4]
    outs = refs[2 * slots + 4 :]
    rows = uppers[0].shape[2]
    f32, bf16 = jnp.float32, jnp.bfloat16

    def window(slot, part):
        def projected(ref):
            return sum(ref[slab, part].astype(f32) for slab in range(ref.shape[0])).astype(bf16).astype(f32)

        above, below = projected(uppers[slot]), projected(lowers[slot])
        return jnp.concatenate(
            [above[:HALO], above[HALO:] + below[: rows - HALO], below[rows - HALO :]], axis=0
        )

    for slot in range(slots):

        @pl.when(live_ref[slot] > 0)
        def _():
            phase, absorption = window(slot, 0), window(slot, 1)
            magnitude = jnp.exp(-absorption)
            trans_real = magnitude * jnp.cos(phase)
            trans_imag = magnitude * jnp.sin(phase)
            probe_real, probe_imag = probe[0], probe[1]
            wr, wi = wr_ref[...], wi_ref[...]
            wave_real = (probe_real * trans_real - probe_imag * trans_imag).astype(bf16)
            wave_imag = (probe_real * trans_imag + probe_imag * trans_real).astype(bf16)
            left_real = (dot(wr, wave_real) - dot(wi, wave_imag)).astype(bf16)
            left_imag = (dot(wr, wave_imag) + dot(wi, wave_real)).astype(bf16)
            far_real = dot(left_real, wr) - dot(left_imag, wi)
            far_imag = dot(left_real, wi) + dot(left_imag, wr)
            power = far_real * far_real + far_imag * far_imag + floor_square
            keeping = 1.0 - patterns[slot].astype(f32) * lax.rsqrt(power)
            resid_real = (far_real * keeping).astype(bf16)
            resid_imag = (far_imag * keeping).astype(bf16)
            back_real = (dot(wr, resid_real) + dot(wi, resid_imag)).astype(bf16)
            back_imag = (dot(wr, resid_imag) - dot(wi, resid_real)).astype(bf16)
            exit_real = dot(back_real, wr) + dot(back_imag, wi)
            exit_imag = dot(back_imag, wr) - dot(back_real, wi)
            mixed_real = probe_real * exit_real + probe_imag * exit_imag
            mixed_imag = probe_real * exit_imag - probe_imag * exit_real
            final_real = trans_real * mixed_real + trans_imag * mixed_imag
            final_imag = trans_real * mixed_imag - trans_imag * mixed_real
            for part, value in enumerate((final_imag, -final_real)):
                value = value.astype(bf16)
                for slab in range(outs[slot].shape[0]):
                    outs[slot][slab, part] = value

        @pl.when(live_ref[slot] == 0)
        def _():
            outs[slot][...] = jnp.zeros(outs[slot].shape, bf16)


def patch_gradients(live, uppers, lowers, probe_wave, patterns, tables):
    slots, width = patterns.shape[:2]
    shape = jax.ShapeDtypeStruct((uppers[0].shape[0], 2, width, width), jnp.bfloat16)
    return call(
        functools.partial(patch_body, slots),
        [shape] * slots,
        [],
        live,
        *uppers,
        *lowers,
        probe_wave,
        patterns,
        *tables,
    )


def place_body(slots, pieces, place_ref, *refs):
    windows, (keep_out, send_out, total) = refs[:slots], refs[slots:]
    slabs, _, width, _ = windows[0].shape
    tile_rows, columns = keep_out.shape[1:]
    total[...] = jnp.zeros_like(total)

    stored = lax.broadcasted_iota(jnp.int32, (2 * tile_rows, width), 0)
    size = tile_rows // pieces
    piece = sum((stored >= tile_rows + k * size).astype(jnp.int32) for k in range(1, pieces))
    true_row = jnp.where(stored < tile_rows, stored, stored + (pieces - 1 - 2 * piece) * size)
    patch_row = true_row - lax.broadcasted_iota(jnp.int32, (2 * tile_rows, width), 1)

    for slab in range(slabs):
        for slot in range(slots):
            top, left, live = (place_ref[3 * (slab * slots + slot) + i] for i in range(3))

            @pl.when(live > 0)
            def _():
                put_rows = (patch_row == top).astype(jnp.float32).astype(jnp.bfloat16)
                put_columns = one_hot(width, width + LANE, -lax.rem(left, LANE))
                starts = column_blocks(left, width, columns)
                for part in range(2):
                    moved = dot(put_rows, windows[slot][slab, part]).astype(jnp.bfloat16)
                    wide = dot(moved, put_columns)
                    for i, start in enumerate(starts):
                        total[part, :, pl.ds(start, LANE)] += wide[:, i * LANE : (i + 1) * LANE]

    core = place_ref[3 * slabs * slots]
    for which in range(2):
        rows = slice(which * tile_rows, (which + 1) * tile_rows)
        keep_out[which] = total[core, rows]
        send_out[which] = total[1 - core, rows].astype(jnp.bfloat16)


def place_windows(place, core, windows, pieces, tile_rows, columns):
    shape = (2, tile_rows, columns)
    scalars = jnp.concatenate([place.reshape(-1), core.reshape(1)]).astype(jnp.int32)
    return call(
        functools.partial(place_body, len(windows), pieces),
        [jax.ShapeDtypeStruct(shape, jnp.float32), jax.ShapeDtypeStruct(shape, jnp.bfloat16)],
        [pltpu.VMEM((2, 2 * tile_rows, columns), jnp.float32)],
        scalars,
        *windows,
    )


def step_body(core_ref, layer_ref, mine_ref, other_ref, out):
    core = core_ref[0]
    for turn, ref in enumerate((mine_ref, other_ref)):
        part = core ^ turn
        out[part] = layer_ref[part].astype(jnp.float32) - step_size * ref[...].astype(jnp.float32)


def step(core, layer, mine, other):
    shape = jax.ShapeDtypeStruct(layer.shape, jnp.float32)
    return call(step_body, [shape], [], core.reshape(1).astype(jnp.int32), layer, mine, other)[0]


def per_device(volume, probe_wave, amplitudes, offsets, column_starts, counts, angle_ids):
    layer = volume.reshape(volume.shape[0], *volume.shape[2:])
    tile_rows, columns = layer.shape[1:]
    width = amplitudes.shape[-1]
    slots = offsets.shape[3]
    angles, slabs, tiles = (lax.axis_size(axis) for axis in ("angle", "slab", "tile"))
    slab, angle = lax.axis_index("slab"), lax.axis_index("angle")
    f32, bf16 = jnp.float32, jnp.bfloat16
    tables = dft_tables(width)
    window_rows = width - HALO
    patterns = amplitudes.reshape(slots, width, width)

    fours = angles // 8
    core, far = angle % 2, angle // 8
    four_groups = [[8 * f + 2 * q + c for q in range(4)] for f in range(fours) for c in range(2)]
    pieces = 4 * fours
    piece_rows = tile_rows // pieces

    def swap(value, by):
        return lax.ppermute(value, "angle", [(i, i ^ by) for i in range(angles)])

    def mirrored(value, by):
        pairs = [
            (a * tiles + t, (angles - 2 - (a - a % 2) + a % 2) * tiles + t + by)
            for a in range(angles)
            for t in range(tiles)
            if 0 <= t + by < tiles
        ]
        return lax.ppermute(value, ("angle", "tile"), pairs)

    def to_slabs(value):
        return lax.all_to_all(value, "slab", 0, 0, tiled=True)

    def to_four(value):
        return lax.all_to_all(value, "angle", 0, 0, axis_index_groups=four_groups, tiled=True)

    def spread(piece):
        other = swap(piece, 8)
        pair = jnp.concatenate([jnp.where(far == 0, piece, other), jnp.where(far == 0, other, piece)])
        return to_four(jnp.broadcast_to(pair, (4, *pair.shape))).reshape(tile_rows, columns)

    def summed(blocks):
        total = jnp.sum(to_four(blocks).astype(f32), axis=0).reshape(fours, piece_rows, columns)
        here = lax.dynamic_index_in_dim(total, far, 0, keepdims=False)
        there = lax.dynamic_index_in_dim(total, 1 - far, 0, keepdims=False).astype(bf16)
        return here + swap(there, 8).astype(f32)

    place_z = angles // 2 - 1 - angle // 2
    first_row = (place_z % 4) * (piece_rows * fours) + place_z // 4 * piece_rows
    own_part = lax.dynamic_index_in_dim(layer, core, 0, keepdims=False)
    after = mirrored(lax.dynamic_slice(own_part, (first_row, 0), (piece_rows, columns)), -1)

    live = (jnp.arange(slots) < counts.reshape(1)).astype(jnp.int32)
    meta = jnp.stack([offsets.reshape(slots), column_starts.reshape(slots), live], axis=1)
    group = to_slabs(jnp.broadcast_to(meta, (slabs, *meta.shape)))
    more = jnp.max(group[:, 1:, 2]) > 0
    sheared = jnp.floor_divide((angle_ids[0] - angle_center) * (slab - slabs // 2), shear_divisor)
    lefts = jnp.mod(group[..., 1] + jnp.mod(sheared, columns), columns)

    def place(down):
        return jnp.stack([group[..., 0] + down, lefts, group[..., 2]], axis=-1)

    def exchanged(first, *others):
        return lax.cond(
            more,
            lambda values: tuple(to_slabs(v) for v in values),
            lambda values: (to_slabs(values[0]), *values[1:]),
            (first, *others),
        )

    zero = jnp.zeros((), jnp.int32)
    uppers = cut_windows(place(0), zero, layer[0], layer[1], window_rows, width)
    uppers = [to_slabs(u) for u in uppers]
    after = spread(after)
    lowers = cut_windows(
        place(HALO - tile_rows), core, after, swap(after, 1), window_rows, width
    )
    lowers = exchanged(*lowers)

    gradients = patch_gradients(live, uppers, lowers, probe_wave, patterns, tables)
    gradients = exchanged(*gradients)
    kept, sent = place_windows(place(0), core, gradients, pieces, tile_rows, columns)

    kept = (kept + swap(sent, 1).astype(f32)).astype(bf16).reshape(2, 4, tile_rows // 4, columns)
    spilled = mirrored(summed(kept[1]).astype(bf16), 1)
    total = (summed(kept[0]) + spilled.astype(f32)).astype(bf16)

    total = spread(total)
    return step(core, layer, total, swap(total, 1)).reshape(volume.shape)


def solution(mesh):
    in_specs = (
        P(None, "slab", "tile", None),
        P(),
        P("angle", "tile", "slab", None, None, None),
        P("angle", "tile", "slab", None),
        P("angle", "tile", "slab", None),
        P("angle", "tile", "slab"),
        P("angle"),
    )
    out_specs = P(None, "slab", "tile", None)
    return jax.shard_map(
        per_device, mesh=mesh, in_specs=in_specs, out_specs=out_specs, check_vma=False
    )
```

```python
import functools

import jax
import jax.numpy as jnp
import ml_dtypes
import numpy as np
from jax import lax
from jax.experimental import pallas as pl
from jax.experimental.pallas import tpu as pltpu
from jax.sharding import PartitionSpec as P

angle_center = 600
shear_divisor = 64
step_size = 0.03
floor_square = 0.25

LANE = 128
HALO = 64


def dft_tables(plane_width):
    index_line = np.arange(plane_width, dtype=np.int32)
    product_mod = np.mod(index_line[:, None] * index_line[None, :], plane_width)
    phase_table = product_mod.astype(np.float32) * np.float32(2.0 * 3.141592653589793 / plane_width)
    scale_factor = np.float32(plane_width ** (-0.5))
    table_real = (np.cos(phase_table) * scale_factor).astype(ml_dtypes.bfloat16)
    table_imag = (-np.sin(phase_table) * scale_factor).astype(ml_dtypes.bfloat16)
    return table_real, table_imag


def dot(left, right):
    return jnp.dot(left, right, preferred_element_type=jnp.float32)


def one_hot(rows, columns, down):
    row = lax.broadcasted_iota(jnp.int32, (rows, columns), 0)
    column = lax.broadcasted_iota(jnp.int32, (rows, columns), 1)
    return (row - column == down).astype(jnp.float32).astype(jnp.bfloat16)


def call(body, out_shape, scratch, *args):
    def spec(x):
        if x.dtype == jnp.int32:
            return pl.BlockSpec(memory_space=pltpu.SMEM)
        return pl.BlockSpec(x.shape, functools.partial(lambda rank, i: (0,) * rank, len(x.shape)))

    return pl.pallas_call(
        body,
        grid=(1,),
        out_shape=out_shape,
        in_specs=[spec(x) for x in args],
        out_specs=[spec(x) for x in out_shape],
        scratch_shapes=scratch,
        compiler_params=pltpu.CompilerParams(vmem_limit_bytes=56 * 1024 * 1024),
    )(*args)


def column_blocks(left, width, columns):
    blocks = columns // LANE
    return [
        pl.multiple_of(lax.rem(left // LANE + i, blocks) * LANE, LANE) for i in range(width // LANE + 1)
    ]


def cut_body(place_ref, first_ref, second_ref, out):
    rows, width = out.shape[3:]
    slabs, slots = out.shape[:2]
    tile_rows, columns = first_ref.shape
    first_part = place_ref[3 * slabs * slots]
    for slab in range(slabs):
        for slot in range(slots):
            top, left, live = (place_ref[3 * (slab * slots + slot) + i] for i in range(3))

            @pl.when(live > 0)
            def _():
                pick_rows = one_hot(rows, tile_rows, -top)
                pick_columns = one_hot(width + LANE, width, lax.rem(left, LANE))
                starts = column_blocks(left, width, columns)
                for turn, ref in enumerate((first_ref, second_ref)):
                    pieces = [ref[:, pl.ds(start, LANE)] for start in starts]
                    narrow = dot(jnp.concatenate(pieces, axis=1), pick_columns).astype(jnp.bfloat16)
                    out[slab, slot, first_part ^ turn] = dot(pick_rows, narrow).astype(jnp.bfloat16)

            @pl.when(live == 0)
            def _():
                out[slab, slot] = jnp.zeros(out.shape[2:], out.dtype)


def cut_windows(place, first_part, first, second, rows, width):
    shape = jax.ShapeDtypeStruct((*place.shape[:2], 2, rows, width), jnp.bfloat16)
    scalars = jnp.concatenate([place.reshape(-1), first_part.reshape(1)]).astype(jnp.int32)
    return call(cut_body, [shape], [], scalars, first, second)[0]


def patch_body(live_ref, uppers, lowers, probe, patterns, wr_ref, wi_ref, out):
    slabs, slots, _, rows, _ = uppers.shape
    f32, bf16 = jnp.float32, jnp.bfloat16

    def window(slot, part):
        def projected(ref):
            return sum(ref[slab, slot, part].astype(f32) for slab in range(slabs)).astype(bf16).astype(f32)

        above, below = projected(uppers), projected(lowers)
        return jnp.concatenate(
            [above[:HALO], above[HALO:] + below[: rows - HALO], below[rows - HALO :]], axis=0
        )

    for slot in range(slots):

        @pl.when(live_ref[slot] > 0)
        def _():
            phase, absorption = window(slot, 0), window(slot, 1)
            magnitude = jnp.exp(-absorption)
            trans_real = magnitude * jnp.cos(phase)
            trans_imag = magnitude * jnp.sin(phase)
            probe_real, probe_imag = probe[0], probe[1]
            wr, wi = wr_ref[...], wi_ref[...]
            wave_real = (probe_real * trans_real - probe_imag * trans_imag).astype(bf16)
            wave_imag = (probe_real * trans_imag + probe_imag * trans_real).astype(bf16)
            left_real = (dot(wr, wave_real) - dot(wi, wave_imag)).astype(bf16)
            left_imag = (dot(wr, wave_imag) + dot(wi, wave_real)).astype(bf16)
            far_real = dot(left_real, wr) - dot(left_imag, wi)
            far_imag = dot(left_real, wi) + dot(left_imag, wr)
            power = far_real * far_real + far_imag * far_imag + floor_square
            keeping = 1.0 - patterns[slot].astype(f32) * lax.rsqrt(power)
            resid_real = (far_real * keeping).astype(bf16)
            resid_imag = (far_imag * keeping).astype(bf16)
            back_real = (dot(wr, resid_real) + dot(wi, resid_imag)).astype(bf16)
            back_imag = (dot(wr, resid_imag) - dot(wi, resid_real)).astype(bf16)
            exit_real = dot(back_real, wr) + dot(back_imag, wi)
            exit_imag = dot(back_imag, wr) - dot(back_real, wi)
            mixed_real = probe_real * exit_real + probe_imag * exit_imag
            mixed_imag = probe_real * exit_imag - probe_imag * exit_real
            final_real = trans_real * mixed_real + trans_imag * mixed_imag
            final_imag = trans_real * mixed_imag - trans_imag * mixed_real
            for part, value in enumerate((final_imag, -final_real)):
                value = value.astype(bf16)
                for slab in range(slabs):
                    out[slab, slot, part] = value

        @pl.when(live_ref[slot] == 0)
        def _():
            for slab in range(slabs):
                out[slab, slot] = jnp.zeros(out.shape[2:], bf16)


def patch_gradients(live, uppers, lowers, probe_wave, patterns, tables):
    slots, width = patterns.shape[:2]
    shape = jax.ShapeDtypeStruct((uppers.shape[0], slots, 2, width, width), jnp.bfloat16)
    return call(patch_body, [shape], [], live, uppers, lowers, probe_wave, patterns, *tables)[0]


def place_body(pieces, place_ref, windows, keep_out, send_out, total):
    slabs, slots, _, width, _ = windows.shape
    tile_rows, columns = keep_out.shape[1:]
    total[...] = jnp.zeros_like(total)

    stored = lax.broadcasted_iota(jnp.int32, (2 * tile_rows, width), 0)
    size = tile_rows // pieces
    piece = sum((stored >= tile_rows + k * size).astype(jnp.int32) for k in range(1, pieces))
    true_row = jnp.where(stored < tile_rows, stored, stored + (pieces - 1 - 2 * piece) * size)
    patch_row = true_row - lax.broadcasted_iota(jnp.int32, (2 * tile_rows, width), 1)

    for slab in range(slabs):
        for slot in range(slots):
            top, left, live = (place_ref[3 * (slab * slots + slot) + i] for i in range(3))

            @pl.when(live > 0)
            def _():
                put_rows = (patch_row == top).astype(jnp.float32).astype(jnp.bfloat16)
                put_columns = one_hot(width, width + LANE, -lax.rem(left, LANE))
                starts = column_blocks(left, width, columns)
                for part in range(2):
                    moved = dot(put_rows, windows[slab, slot, part]).astype(jnp.bfloat16)
                    wide = dot(moved, put_columns)
                    for i, start in enumerate(starts):
                        total[part, :, pl.ds(start, LANE)] += wide[:, i * LANE : (i + 1) * LANE]

    core = place_ref[3 * slabs * slots]
    for which in range(2):
        rows = slice(which * tile_rows, (which + 1) * tile_rows)
        keep_out[which] = total[core, rows]
        send_out[which] = total[1 - core, rows].astype(jnp.bfloat16)


def place_windows(place, core, windows, pieces, tile_rows, columns):
    shape = (2, tile_rows, columns)
    scalars = jnp.concatenate([place.reshape(-1), core.reshape(1)]).astype(jnp.int32)
    return call(
        functools.partial(place_body, pieces),
        [jax.ShapeDtypeStruct(shape, jnp.float32), jax.ShapeDtypeStruct(shape, jnp.bfloat16)],
        [pltpu.VMEM((2, 2 * tile_rows, columns), jnp.float32)],
        scalars,
        windows,
    )


def step_body(core_ref, layer_ref, mine_ref, other_ref, out):
    core = core_ref[0]
    for turn, ref in enumerate((mine_ref, other_ref)):
        part = core ^ turn
        out[part] = layer_ref[part].astype(jnp.float32) - step_size * ref[...].astype(jnp.float32)


def step(core, layer, mine, other):
    shape = jax.ShapeDtypeStruct(layer.shape, jnp.float32)
    return call(step_body, [shape], [], core.reshape(1).astype(jnp.int32), layer, mine, other)[0]


def per_device(volume, probe_wave, amplitudes, offsets, column_starts, counts, angle_ids):
    layer = volume.reshape(volume.shape[0], *volume.shape[2:])
    tile_rows, columns = layer.shape[1:]
    width = amplitudes.shape[-1]
    slots = offsets.shape[3]
    angles, slabs, tiles = (lax.axis_size(axis) for axis in ("angle", "slab", "tile"))
    slab, angle = lax.axis_index("slab"), lax.axis_index("angle")
    f32, bf16 = jnp.float32, jnp.bfloat16
    tables = dft_tables(width)
    window_rows = width - HALO
    patterns = amplitudes.reshape(slots, width, width)

    fours = angles // 8
    core, far = angle % 2, angle // 8
    four_groups = [[8 * f + 2 * q + c for q in range(4)] for f in range(fours) for c in range(2)]
    pieces = 4 * fours
    piece_rows = tile_rows // pieces

    def swap(value, by):
        return lax.ppermute(value, "angle", [(i, i ^ by) for i in range(angles)])

    def mirrored(value, by):
        pairs = [
            (a * tiles + t, (angles - 2 - (a - a % 2) + a % 2) * tiles + t + by)
            for a in range(angles)
            for t in range(tiles)
            if 0 <= t + by < tiles
        ]
        return lax.ppermute(value, ("angle", "tile"), pairs)

    def to_slabs(value):
        return lax.all_to_all(value, "slab", 0, 0, tiled=True)

    def to_four(value):
        return lax.all_to_all(value, "angle", 0, 0, axis_index_groups=four_groups, tiled=True)

    def paired(piece, other):
        return jnp.concatenate([jnp.where(far == 0, piece, other), jnp.where(far == 0, other, piece)])

    def spread(pair):
        return to_four(jnp.broadcast_to(pair, (4, *pair.shape))).reshape(tile_rows, columns)

    def summed(blocks):
        total = jnp.sum(blocks.astype(f32), axis=0).reshape(fours, piece_rows, columns)
        here = lax.dynamic_index_in_dim(total, far, 0, keepdims=False)
        there = lax.dynamic_index_in_dim(total, 1 - far, 0, keepdims=False).astype(bf16)
        return here + swap(there, 8).astype(f32)

    place_z = angles // 2 - 1 - angle // 2
    first_row = (place_z % 4) * (piece_rows * fours) + place_z // 4 * piece_rows
    own_part = lax.dynamic_index_in_dim(layer, core, 0, keepdims=False)
    after = mirrored(lax.dynamic_slice(own_part, (first_row, 0), (piece_rows, columns)), -1)

    live = (jnp.arange(slots) < counts.reshape(1)).astype(jnp.int32)
    meta = jnp.stack([offsets.reshape(slots), column_starts.reshape(slots), live], axis=1)
    group = to_slabs(jnp.broadcast_to(meta, (slabs, *meta.shape)))
    after, group = lax.optimization_barrier((after, group))
    more = jnp.max(group[:, 1:, 2]) > 0
    sheared = jnp.floor_divide((angle_ids[0] - angle_center) * (slab - slabs // 2), shear_divisor)
    lefts = jnp.mod(group[..., 1] + jnp.mod(sheared, columns), columns)

    def place(down):
        return jnp.stack([group[..., 0] + down, lefts, group[..., 2]], axis=-1)

    def exchanged(values):
        return lax.cond(
            more,
            to_slabs,
            lambda v: jnp.concatenate([to_slabs(v[:, :1]), v[:, 1:]], axis=1),
            values,
        )

    zero = jnp.zeros((), jnp.int32)
    uppers = cut_windows(place(0), zero, layer[0], layer[1], window_rows, width)
    after, uppers = lax.optimization_barrier((paired(after, swap(after, 8)), uppers))
    uppers, after = to_slabs(uppers), spread(after)
    after, after_too, uppers = lax.optimization_barrier((after, swap(after, 1), uppers))
    lowers = cut_windows(place(HALO - tile_rows), core, after, after_too, window_rows, width)
    lowers = exchanged(lowers)

    gradients = exchanged(patch_gradients(live, uppers, lowers, probe_wave, patterns, tables))
    kept, sent = place_windows(place(0), core, gradients, pieces, tile_rows, columns)

    kept = (kept + swap(sent, 1).astype(f32)).astype(bf16).reshape(2, 4, tile_rows // 4, columns)
    spill, own = to_four(kept[1]), to_four(kept[0])
    spill, own = lax.optimization_barrier((summed(spill).astype(bf16), own))
    spill = mirrored(spill, 1)
    total = (summed(own) + spill.astype(f32)).astype(bf16)

    total = spread(paired(total, swap(total, 8)))
    return step(core, layer, total, swap(total, 1)).reshape(volume.shape)


def solution(mesh):
    in_specs = (
        P(None, "slab", "tile", None),
        P(),
        P("angle", "tile", "slab", None, None, None),
        P("angle", "tile", "slab", None),
        P("angle", "tile", "slab", None),
        P("angle", "tile", "slab"),
        P("angle"),
    )
    out_specs = P(None, "slab", "tile", None)
    return jax.shard_map(
        per_device, mesh=mesh, in_specs=in_specs, out_specs=out_specs, check_vma=False
    )
```

```python
import functools

import jax
import jax.numpy as jnp
import ml_dtypes
import numpy as np
from jax import lax
from jax.experimental import pallas as pl
from jax.experimental.pallas import tpu as pltpu
from jax.sharding import PartitionSpec as P

angle_center = 600
shear_divisor = 64
step_size = 0.03
floor_square = 0.25

LANE = 128
HALO = 64


def dft_tables(plane_width):
    index_line = np.arange(plane_width, dtype=np.int32)
    product_mod = np.mod(index_line[:, None] * index_line[None, :], plane_width)
    phase_table = product_mod.astype(np.float32) * np.float32(2.0 * 3.141592653589793 / plane_width)
    scale_factor = np.float32(plane_width ** (-0.5))
    table_real = (np.cos(phase_table) * scale_factor).astype(ml_dtypes.bfloat16)
    table_imag = (-np.sin(phase_table) * scale_factor).astype(ml_dtypes.bfloat16)
    return table_real, table_imag


def dot(left, right):
    return jnp.dot(left, right, preferred_element_type=jnp.float32)


def one_hot(rows, columns, down):
    row = lax.broadcasted_iota(jnp.int32, (rows, columns), 0)
    column = lax.broadcasted_iota(jnp.int32, (rows, columns), 1)
    return (row - column == down).astype(jnp.float32).astype(jnp.bfloat16)


def call(body, out_shape, scratch, *args):
    def spec(x):
        if x.dtype == jnp.int32:
            return pl.BlockSpec(memory_space=pltpu.SMEM)
        return pl.BlockSpec(x.shape, functools.partial(lambda rank, i: (0,) * rank, len(x.shape)))

    return pl.pallas_call(
        body,
        grid=(1,),
        out_shape=out_shape,
        in_specs=[spec(x) for x in args],
        out_specs=[spec(x) for x in out_shape],
        scratch_shapes=scratch,
        compiler_params=pltpu.CompilerParams(vmem_limit_bytes=56 * 1024 * 1024),
    )(*args)


def column_blocks(left, width, columns):
    blocks = columns // LANE
    return [
        pl.multiple_of(lax.rem(left // LANE + i, blocks) * LANE, LANE) for i in range(width // LANE + 1)
    ]


def cut_body(place_ref, *refs):
    blocks, (out, rows_held) = refs[:-2], refs[-2:]
    slabs, slots, _, rows, width = out.shape
    tile_rows, columns = rows_held.shape[1:]
    first_part, first_block = (place_ref[3 * slabs * slots + i] for i in range(2))
    each = len(blocks) // 2
    for n, block in enumerate(blocks):
        size = tile_rows // each
        start = pl.multiple_of((first_block ^ (n % each)) * size, size)
        rows_held[first_part ^ (n // each), pl.ds(start, size), :] = block[...]

    for slab in range(slabs):
        for slot in range(slots):
            top, left, live = (place_ref[3 * (slab * slots + slot) + i] for i in range(3))

            @pl.when(live > 0)
            def _():
                pick_rows = one_hot(rows, tile_rows, -top)
                pick_columns = one_hot(width + LANE, width, lax.rem(left, LANE))
                starts = column_blocks(left, width, columns)
                for part in range(2):
                    pieces = [rows_held[part, :, pl.ds(start, LANE)] for start in starts]
                    narrow = dot(jnp.concatenate(pieces, axis=1), pick_columns).astype(jnp.bfloat16)
                    out[slab, slot, part] = dot(pick_rows, narrow).astype(jnp.bfloat16)

            @pl.when(live == 0)
            def _():
                out[slab, slot] = jnp.zeros(out.shape[2:], out.dtype)


def cut_windows(place, firsts, blocks, rows, width):
    shape = jax.ShapeDtypeStruct((*place.shape[:2], 2, rows, width), jnp.bfloat16)
    scalars = jnp.concatenate([place.reshape(-1), jnp.stack(firsts)]).astype(jnp.int32)
    each = len(blocks) // 2
    held = pltpu.VMEM((2, each * blocks[0].shape[0], blocks[0].shape[1]), jnp.bfloat16)
    return call(cut_body, [shape], [held], scalars, *blocks)[0]


def patch_body(live_ref, uppers, lowers, probe, patterns, wr_ref, wi_ref, out):
    slabs, slots, _, rows, _ = uppers.shape
    f32, bf16 = jnp.float32, jnp.bfloat16

    def window(slot, part):
        def projected(ref):
            return sum(ref[slab, slot, part].astype(f32) for slab in range(slabs)).astype(bf16).astype(f32)

        above, below = projected(uppers), projected(lowers)
        return jnp.concatenate(
            [above[:HALO], above[HALO:] + below[: rows - HALO], below[rows - HALO :]], axis=0
        )

    for slot in range(slots):

        @pl.when(live_ref[slot] > 0)
        def _():
            phase, absorption = window(slot, 0), window(slot, 1)
            magnitude = jnp.exp(-absorption)
            trans_real = magnitude * jnp.cos(phase)
            trans_imag = magnitude * jnp.sin(phase)
            probe_real, probe_imag = probe[0], probe[1]
            wr, wi = wr_ref[...], wi_ref[...]
            wave_real = (probe_real * trans_real - probe_imag * trans_imag).astype(bf16)
            wave_imag = (probe_real * trans_imag + probe_imag * trans_real).astype(bf16)
            left_real = (dot(wr, wave_real) - dot(wi, wave_imag)).astype(bf16)
            left_imag = (dot(wr, wave_imag) + dot(wi, wave_real)).astype(bf16)
            far_real = dot(left_real, wr) - dot(left_imag, wi)
            far_imag = dot(left_real, wi) + dot(left_imag, wr)
            power = far_real * far_real + far_imag * far_imag + floor_square
            keeping = 1.0 - patterns[slot].astype(f32) * lax.rsqrt(power)
            resid_real = (far_real * keeping).astype(bf16)
            resid_imag = (far_imag * keeping).astype(bf16)
            back_real = (dot(wr, resid_real) + dot(wi, resid_imag)).astype(bf16)
            back_imag = (dot(wr, resid_imag) - dot(wi, resid_real)).astype(bf16)
            exit_real = dot(back_real, wr) + dot(back_imag, wi)
            exit_imag = dot(back_imag, wr) - dot(back_real, wi)
            mixed_real = probe_real * exit_real + probe_imag * exit_imag
            mixed_imag = probe_real * exit_imag - probe_imag * exit_real
            final_real = trans_real * mixed_real + trans_imag * mixed_imag
            final_imag = trans_real * mixed_imag - trans_imag * mixed_real
            for part, value in enumerate((final_imag, -final_real)):
                value = value.astype(bf16)
                for slab in range(slabs):
                    out[slab, slot, part] = value

        @pl.when(live_ref[slot] == 0)
        def _():
            for slab in range(slabs):
                out[slab, slot] = jnp.zeros(out.shape[2:], bf16)


def patch_gradients(live, uppers, lowers, probe_wave, patterns, tables):
    slots, width = patterns.shape[:2]
    shape = jax.ShapeDtypeStruct((uppers.shape[0], slots, 2, width, width), jnp.bfloat16)
    return call(patch_body, [shape], [], live, uppers, lowers, probe_wave, patterns, *tables)[0]


def place_body(blocks, place_ref, windows, own_out, next_out, send_out, total):
    slabs, slots, _, width, _ = windows.shape
    tile_rows, columns = own_out.shape
    total[...] = jnp.zeros_like(total)
    for slab in range(slabs):
        for slot in range(slots):
            top, left, live = (place_ref[3 * (slab * slots + slot) + i] for i in range(3))

            @pl.when(live > 0)
            def _():
                put_rows = one_hot(2 * tile_rows, width, top)
                put_columns = one_hot(width, width + LANE, -lax.rem(left, LANE))
                starts = column_blocks(left, width, columns)
                for part in range(2):
                    moved = dot(put_rows, windows[slab, slot, part]).astype(jnp.bfloat16)
                    wide = dot(moved, put_columns)
                    for i, start in enumerate(starts):
                        total[part, :, pl.ds(start, LANE)] += wide[:, i * LANE : (i + 1) * LANE]

    core = place_ref[3 * slabs * slots]
    own_out[...] = total[core, :tile_rows]
    send_out[1] = total[1 - core, :tile_rows].astype(jnp.bfloat16)
    size = tile_rows // blocks
    for block in range(blocks):
        to = slice(block * size, (block + 1) * size)
        rows = slice(2 * tile_rows - (block + 1) * size, 2 * tile_rows - block * size)
        next_out[to] = total[core, rows]
        send_out[0, to] = total[1 - core, rows].astype(jnp.bfloat16)


def place_windows(place, core, windows, blocks, tile_rows, columns):
    kept = jax.ShapeDtypeStruct((tile_rows, columns), jnp.float32)
    scalars = jnp.concatenate([place.reshape(-1), core.reshape(1)]).astype(jnp.int32)
    return call(
        functools.partial(place_body, blocks),
        [kept, kept, jax.ShapeDtypeStruct((2, tile_rows, columns), jnp.bfloat16)],
        [pltpu.VMEM((2, 2 * tile_rows, columns), jnp.float32)],
        scalars,
        windows,
    )


def step_body(core_ref, layer_ref, mine_ref, other_ref, out):
    core = core_ref[0]
    for turn, ref in enumerate((mine_ref, other_ref)):
        part = core ^ turn
        out[part] = layer_ref[part].astype(jnp.float32) - step_size * ref[...].astype(jnp.float32)


def step(core, layer, mine, other):
    shape = jax.ShapeDtypeStruct(layer.shape, jnp.float32)
    return call(step_body, [shape], [], core.reshape(1).astype(jnp.int32), layer, mine, other)[0]


def per_device(volume, probe_wave, amplitudes, offsets, column_starts, counts, angle_ids):
    layer = volume.reshape(volume.shape[0], *volume.shape[2:])
    tile_rows, columns = layer.shape[1:]
    width = amplitudes.shape[-1]
    slots = offsets.shape[3]
    angles, slabs, tiles = (lax.axis_size(axis) for axis in ("angle", "slab", "tile"))
    slab, angle = lax.axis_index("slab"), lax.axis_index("angle")
    f32, bf16 = jnp.float32, jnp.bfloat16
    tables = dft_tables(width)
    window_rows = width - HALO
    patterns = amplitudes.reshape(slots, width, width)

    core, place_z = angle % 2, angle // 2 % 4
    four_groups = [[8 * f + 2 * q + c for q in range(4)] for f in range(angles // 8) for c in range(2)]
    block_rows = tile_rows // 4

    def swap(value, by):
        return lax.ppermute(value, "angle", [(i, i ^ by) for i in range(angles)])

    def mirrored(value, by):
        pairs = [
            (a * tiles + t, (angles - 2 - (a - a % 2) + a % 2) * tiles + t + by)
            for a in range(angles)
            for t in range(tiles)
            if 0 <= t + by < tiles
        ]
        return lax.ppermute(value, ("angle", "tile"), pairs)

    def to_slabs(value):
        return lax.all_to_all(value, "slab", 0, 0, tiled=True)

    def to_four(value):
        return lax.all_to_all(value, "angle", 0, 0, axis_index_groups=four_groups, tiled=True)

    def added(blocks):
        return jnp.sum(to_four(blocks).astype(f32), axis=0)

    own_part = lax.dynamic_index_in_dim(layer, core, 0, keepdims=False)
    after = mirrored(
        lax.dynamic_slice(own_part, ((3 - place_z) * block_rows, 0), (block_rows, columns)), -1
    )

    live = (jnp.arange(slots) < counts.reshape(1)).astype(jnp.int32)
    meta = jnp.stack([offsets.reshape(slots), column_starts.reshape(slots), live], axis=1)
    group = to_slabs(jnp.broadcast_to(meta, (slabs, *meta.shape)))
    after, group = lax.optimization_barrier((after, group))
    more = jnp.max(group[:, 1:, 2]) > 0
    sheared = jnp.floor_divide((angle_ids[0] - angle_center) * (slab - slabs // 2), shear_divisor)
    lefts = jnp.mod(group[..., 1] + jnp.mod(sheared, columns), columns)

    def place(down):
        return jnp.stack([group[..., 0] + down, lefts, group[..., 2]], axis=-1)

    def exchanged(values):
        return lax.cond(
            more,
            to_slabs,
            lambda v: jnp.concatenate([to_slabs(v[:, :1]), v[:, 1:]], axis=1),
            values,
        )

    zero = jnp.zeros((), jnp.int32)
    uppers = cut_windows(place(0), [zero, zero], [layer[0], layer[1]], window_rows, width)
    after, uppers = lax.optimization_barrier((after, uppers))
    uppers = to_slabs(uppers)
    mine = [after] + [swap(after, k << 1) for k in range(1, 4)]
    afters = mine + [swap(block, 1) for block in mine]
    afters, uppers = lax.optimization_barrier((afters, uppers))
    lowers = cut_windows(place(HALO - tile_rows), [core, place_z], afters, window_rows, width)
    lowers = exchanged(lowers)

    gradients = exchanged(patch_gradients(live, uppers, lowers, probe_wave, patterns, tables))
    own, spill, sent = place_windows(place(0), core, gradients, 4, tile_rows, columns)

    sent = swap(sent, 1).astype(f32)
    spill = (spill + sent[0]).astype(bf16).reshape(4, block_rows, columns)
    own = (own + sent[1]).astype(bf16).reshape(4, block_rows, columns)
    spill, own = lax.optimization_barrier((added(spill).astype(bf16), own))
    spill = mirrored(spill, 1)
    total = lax.optimization_barrier((added(own) + spill.astype(f32)).astype(bf16))
    total = (total.astype(f32) + swap(total, 8).astype(f32)).astype(bf16)

    total = to_four(jnp.broadcast_to(total, (4, *total.shape))).reshape(tile_rows, columns)
    return step(core, layer, total, swap(total, 1)).reshape(volume.shape)


def solution(mesh):
    in_specs = (
        P(None, "slab", "tile", None),
        P(),
        P("angle", "tile", "slab", None, None, None),
        P("angle", "tile", "slab", None),
        P("angle", "tile", "slab", None),
        P("angle", "tile", "slab"),
        P("angle"),
    )
    out_specs = P(None, "slab", "tile", None)
    return jax.shard_map(
        per_device, mesh=mesh, in_specs=in_specs, out_specs=out_specs, check_vma=False
    )
```

```python
import functools

import jax
import jax.numpy as jnp
import ml_dtypes
import numpy as np
from jax import lax
from jax.experimental import pallas as pl
from jax.experimental.pallas import tpu as pltpu
from jax.sharding import PartitionSpec as P

angle_center = 600
shear_divisor = 64
step_size = 0.03
floor_square = 0.25

LANE = 128
HALO = 64


def dft_tables(plane_width):
    index_line = np.arange(plane_width, dtype=np.int32)
    product_mod = np.mod(index_line[:, None] * index_line[None, :], plane_width)
    phase_table = product_mod.astype(np.float32) * np.float32(2.0 * 3.141592653589793 / plane_width)
    scale_factor = np.float32(plane_width ** (-0.5))
    table_real = (np.cos(phase_table) * scale_factor).astype(ml_dtypes.bfloat16)
    table_imag = (-np.sin(phase_table) * scale_factor).astype(ml_dtypes.bfloat16)
    return table_real, table_imag


def dot(left, right):
    return jnp.dot(left, right, preferred_element_type=jnp.float32)


def one_hot(rows, columns, down):
    row = lax.broadcasted_iota(jnp.int32, (rows, columns), 0)
    column = lax.broadcasted_iota(jnp.int32, (rows, columns), 1)
    return (row - column == down).astype(jnp.float32).astype(jnp.bfloat16)


HBM = pl.BlockSpec(memory_space=pltpu.HBM)


def call(body, out_shape, scratch, facts, *args):
    return pl.pallas_call(
        body,
        out_shape=out_shape,
        in_specs=[pl.BlockSpec(memory_space=pltpu.SMEM)] + [HBM] * len(args),
        out_specs=[HBM] * len(out_shape),
        scratch_shapes=scratch,
        compiler_params=pltpu.CompilerParams(vmem_limit_bytes=56 * 1024 * 1024),
    )(facts, *args)


class Facts:
    def __init__(self, ref, slabs, slots):
        self.ref, self.slots = ref, slots
        self.shift, self.core, self.place_z = (ref[3 * slabs * slots + i] for i in range(3))

    def slot(self, slab, slot):
        return tuple(self.ref[3 * (slab * self.slots + slot) + i] for i in range(3))


def column_blocks(left, width, columns):
    blocks = columns // LANE
    return [
        pl.multiple_of(lax.rem(left // LANE + i, blocks) * LANE, LANE) for i in range(width // LANE + 1)
    ]


def cut_body(down, facts_ref, *refs):
    blocks, (out, held, made, in_sems, out_sems) = refs[:-5], refs[-5:]
    slabs, slots, _, rows, width = out.shape
    tile_rows, columns = held.shape[1:]
    facts = Facts(facts_ref, slabs, slots)
    if len(blocks) == 1:
        copies = [pltpu.make_async_copy(blocks[0], held, in_sems.at[0])]
    else:
        *mine, other = blocks
        size = tile_rows // len(mine)
        copies = []
        for k, block in enumerate(mine):
            at = pl.ds(pl.multiple_of((facts.place_z ^ k) * size, size), size)
            copies.append(pltpu.make_async_copy(block, held.at[facts.core, at], in_sems.at[2 * k]))
            copies.append(
                pltpu.make_async_copy(other.at[k], held.at[1 - facts.core, at], in_sems.at[2 * k + 1])
            )
    for copy in copies:
        copy.start()
    for copy in copies:
        copy.wait()

    def written(slab, slot):
        return pltpu.make_async_copy(
            made.at[slab, slot], out.at[slab, slot], out_sems.at[slab, slot]
        )

    each = [(slab, slot) for slot in range(slots) for slab in range(slabs)]
    for slab, slot in each:
        row, column, live = facts.slot(slab, slot)

        @pl.when(live > 0)
        def _():
            left = lax.rem(column + facts.shift, columns)
            pick_rows = one_hot(rows, tile_rows, -(row + down))
            pick_columns = one_hot(width + LANE, width, lax.rem(left, LANE))
            wide = jnp.concatenate(
                [held[:, :, pl.ds(start, LANE)] for start in column_blocks(left, width, columns)], axis=2
            )
            narrow = dot(wide.reshape(2 * tile_rows, width + LANE), pick_columns).astype(jnp.bfloat16)
            for part in range(2):
                picked = dot(pick_rows, narrow[part * tile_rows : (part + 1) * tile_rows])
                made[slab, slot, part] = picked.astype(jnp.bfloat16)
            written(slab, slot).start()

    for slab, slot in each:

        @pl.when(facts.slot(slab, slot)[2] > 0)
        def _():
            written(slab, slot).wait()


def cut_windows(facts, slabs, slots, down, blocks, rows, width):
    shape = (slabs, slots, 2, rows, width)
    columns = blocks[0].shape[-1]
    tile_rows = blocks[0].shape[1] if len(blocks) == 1 else blocks[0].shape[0] * (len(blocks) - 1)
    scratch = [
        pltpu.VMEM((2, tile_rows, columns), jnp.bfloat16),
        pltpu.VMEM(shape, jnp.bfloat16),
        pltpu.SemaphoreType.DMA((2 * len(blocks),)),
        pltpu.SemaphoreType.DMA((slabs, slots)),
    ]
    out = jax.ShapeDtypeStruct(shape, jnp.bfloat16)
    return call(functools.partial(cut_body, down), [out], scratch, facts, *blocks)[0]


def cos_sin(angle):
    turns = jnp.round(angle * 0.6366197723675814)
    rest = angle - turns * 1.5703125
    rest = rest - turns * 4.837512969970703e-4
    rest = rest - turns * 7.549789948768648e-8
    square = rest * rest
    sine = (-1.9515295891e-4 * square + 8.3321608736e-3) * square - 1.6666654611e-1
    sine = sine * square * rest + rest
    cosine = (2.443315711809948e-5 * square - 1.388731625493765e-3) * square + 4.166664568298827e-2
    cosine = cosine * square * square - 0.5 * square + 1.0
    quarter = turns.astype(jnp.int32)
    odd = (quarter & 1) == 1
    first, second = jnp.where(odd, sine, cosine), jnp.where(odd, cosine, sine)
    return (
        jnp.where(((quarter + 1) & 2) == 2, -first, first),
        jnp.where((quarter & 2) == 2, -second, second),
    )


def patch_body(
    live_ref, uppers, lowers, probe_in, patterns_in, wr_in, wi_in,
    out, upper, lower, probe, patterns, wr_ref, wi_ref, made, in_sems, slot_sems, out_sems,
):
    slabs, slots, _, rows, _ = uppers.shape
    f32, bf16 = jnp.float32, jnp.bfloat16

    def arrive(slot):
        return [
            pltpu.make_async_copy(ref.at[:, slot], to.at[slot], slot_sems.at[slot, n])
            for n, (ref, to) in enumerate(((uppers, upper), (lowers, lower)))
        ] + [pltpu.make_async_copy(patterns_in.at[slot], patterns.at[slot], slot_sems.at[slot, 2])]

    def leave(slot):
        return [
            pltpu.make_async_copy(made.at[slot], out.at[slab, slot], out_sems.at[slab, slot])
            for slab in range(slabs)
        ]

    common = [
        pltpu.make_async_copy(ref, to, in_sems.at[n])
        for n, (ref, to) in enumerate(((probe_in, probe), (wr_in, wr_ref), (wi_in, wi_ref)))
    ]
    for slot in range(slots):

        @pl.when(live_ref[slot] > 0)
        def _():
            for copy in arrive(slot):
                copy.start()

        if slot == 0:
            for copy in common:
                copy.start()
    for copy in common:
        copy.wait()

    def window(slot, part):
        def projected(ref):
            return sum(ref[slot, slab, part].astype(f32) for slab in range(slabs)).astype(bf16).astype(f32)

        above, below = projected(upper), projected(lower)
        return jnp.concatenate(
            [above[:HALO], above[HALO:] + below[: rows - HALO], below[rows - HALO :]], axis=0
        )

    for slot in range(slots):

        @pl.when(live_ref[slot] > 0)
        def _():
            for copy in arrive(slot):
                copy.wait()
            phase, absorption = window(slot, 0), window(slot, 1)
            magnitude = jnp.exp(-absorption)
            cosine, sine = cos_sin(phase)
            trans_real = magnitude * cosine
            trans_imag = magnitude * sine
            probe_real, probe_imag = probe[0], probe[1]
            wr, wi = wr_ref[...], wi_ref[...]
            wave_real = (probe_real * trans_real - probe_imag * trans_imag).astype(bf16)
            wave_imag = (probe_real * trans_imag + probe_imag * trans_real).astype(bf16)
            left_real = (dot(wr, wave_real) - dot(wi, wave_imag)).astype(bf16)
            left_imag = (dot(wr, wave_imag) + dot(wi, wave_real)).astype(bf16)
            far_real = dot(left_real, wr) - dot(left_imag, wi)
            far_imag = dot(left_real, wi) + dot(left_imag, wr)
            power = far_real * far_real + far_imag * far_imag + floor_square
            keeping = 1.0 - patterns[slot].astype(f32) * lax.rsqrt(power)
            resid_real = (far_real * keeping).astype(bf16)
            resid_imag = (far_imag * keeping).astype(bf16)
            back_real = (dot(wr, resid_real) + dot(wi, resid_imag)).astype(bf16)
            back_imag = (dot(wr, resid_imag) - dot(wi, resid_real)).astype(bf16)
            exit_real = dot(back_real, wr) + dot(back_imag, wi)
            exit_imag = dot(back_imag, wr) - dot(back_real, wi)
            mixed_real = probe_real * exit_real + probe_imag * exit_imag
            mixed_imag = probe_real * exit_imag - probe_imag * exit_real
            made[slot, 0] = (trans_real * mixed_imag - trans_imag * mixed_real).astype(bf16)
            made[slot, 1] = (-(trans_real * mixed_real + trans_imag * mixed_imag)).astype(bf16)
            for copy in leave(slot):
                copy.start()

    for slot in range(slots):

        @pl.when(live_ref[slot] > 0)
        def _():
            for copy in leave(slot):
                copy.wait()


def patch_gradients(live, uppers, lowers, probe_wave, patterns, tables):
    slabs, slots, _, rows, width = uppers.shape
    bf16 = jnp.bfloat16
    scratch = [
        pltpu.VMEM((slots, slabs, 2, rows, width), bf16),
        pltpu.VMEM((slots, slabs, 2, rows, width), bf16),
        pltpu.VMEM(probe_wave.shape, jnp.float32),
        pltpu.VMEM(patterns.shape, bf16),
        pltpu.VMEM((width, width), bf16),
        pltpu.VMEM((width, width), bf16),
        pltpu.VMEM((slots, 2, width, width), bf16),
        pltpu.SemaphoreType.DMA((3,)),
        pltpu.SemaphoreType.DMA((slots, 3)),
        pltpu.SemaphoreType.DMA((slabs, slots)),
    ]
    out = jax.ShapeDtypeStruct((slabs, slots, 2, width, width), bf16)
    return call(patch_body, [out], scratch, live, uppers, lowers, probe_wave, patterns, *tables)[0]


def place_body(
    first_row, reverse, facts_ref, windows, keep_out, send_out, total, patches, send, in_sems, out_sems
):
    slabs, slots, _, width, _ = windows.shape
    rows = patches.shape[3]
    tile_rows, columns = keep_out.shape
    facts = Facts(facts_ref, slabs, slots)
    down = first_row - (tile_rows if first_row else 0)
    each = [(slab, slot) for slot in range(slots) for slab in range(slabs)]

    def arrive(slab, slot):
        return pltpu.make_async_copy(
            windows.at[slab, slot, :, pl.ds(first_row, rows)], patches.at[slab, slot], in_sems.at[slab, slot]
        )

    for slab, slot in each:

        @pl.when(facts.slot(slab, slot)[2] > 0)
        def _():
            arrive(slab, slot).start()

    total[...] = jnp.zeros_like(total)
    for slab, slot in each:
        row, column, live = facts.slot(slab, slot)

        @pl.when(live > 0)
        def _():
            arrive(slab, slot).wait()
            left = lax.rem(column + facts.shift, columns)
            put_rows = one_hot(tile_rows, rows, row + down)
            put_columns = one_hot(width, width + LANE, -lax.rem(left, LANE))
            moved = [dot(put_rows, patches[slab, slot, part]).astype(jnp.bfloat16) for part in range(2)]
            wide = dot(jnp.concatenate(moved, axis=0), put_columns)
            wide = wide.reshape(2, tile_rows, width + LANE)
            for i, start in enumerate(column_blocks(left, width, columns)):
                total[:, :, pl.ds(start, LANE)] += wide[:, :, i * LANE : (i + 1) * LANE]

    send[...] = total[1 - facts.core].astype(jnp.bfloat16)
    blocks = 4 if reverse else 1
    size = tile_rows // blocks
    copies = []
    for block in range(blocks):
        here, there = pl.ds(block * size, size), pl.ds((blocks - 1 - block) * size, size)
        copies.append(pltpu.make_async_copy(send.at[here], send_out.at[there], out_sems.at[0, block]))
        copies.append(
            pltpu.make_async_copy(total.at[facts.core, here], keep_out.at[there], out_sems.at[1, block])
        )
    for copy in copies:
        copy.start()
    for copy in copies:
        copy.wait()


def place_windows(facts, windows, first_row, reverse, rows, tile_rows, columns):
    slabs, slots, _, width, _ = windows.shape
    scratch = [
        pltpu.VMEM((2, tile_rows, columns), jnp.float32),
        pltpu.VMEM((slabs, slots, 2, rows, width), jnp.bfloat16),
        pltpu.VMEM((tile_rows, columns), jnp.bfloat16),
        pltpu.SemaphoreType.DMA((slabs, slots)),
        pltpu.SemaphoreType.DMA((2, 4)),
    ]
    shapes = [jax.ShapeDtypeStruct((tile_rows, columns), t) for t in (jnp.float32, jnp.bfloat16)]
    return call(functools.partial(place_body, first_row, reverse), shapes, scratch, facts, windows)


def step_body(part_ref, layer_ref, gradient_ref, *refs):
    refs[-1][...] = layer_ref[...].astype(jnp.float32) - step_size * gradient_ref[...].astype(jnp.float32)


def step(part, layer, gradient, *stepped):
    block = gradient.shape[0] // 4
    columns = gradient.shape[1]
    of_part = pl.BlockSpec((None, block, columns), lambda i, part_ref: (part_ref[0], i, 0))
    return pl.pallas_call(
        step_body,
        grid_spec=pltpu.PrefetchScalarGridSpec(
            num_scalar_prefetch=1,
            grid=(4,),
            in_specs=[of_part, pl.BlockSpec((block, columns), lambda i, part_ref: (i, 0))]
            + [pl.BlockSpec(memory_space=pl.ANY)] * len(stepped),
            out_specs=of_part,
        ),
        out_shape=jax.ShapeDtypeStruct(layer.shape, jnp.float32),
        input_output_aliases={3: 0} if stepped else {},
    )(part.reshape(1).astype(jnp.int32), layer, gradient, *stepped)


def per_device(volume, probe_wave, amplitudes, offsets, column_starts, counts, angle_ids):
    layer = volume.reshape(volume.shape[0], *volume.shape[2:])
    tile_rows, columns = layer.shape[1:]
    width = amplitudes.shape[-1]
    slots = offsets.shape[3]
    angles, slabs, tiles = (lax.axis_size(axis) for axis in ("angle", "slab", "tile"))
    slab, angle = lax.axis_index("slab"), lax.axis_index("angle")
    f32, bf16 = jnp.float32, jnp.bfloat16
    tables = dft_tables(width)
    window_rows = width - HALO
    patterns = amplitudes.reshape(slots, width, width)

    core, place_z = angle % 2, angle // 2 % 4
    four_groups = [[8 * f + 2 * q + c for q in range(4)] for f in range(angles // 8) for c in range(2)]
    block_rows = tile_rows // 4

    def swap(value, by):
        return lax.ppermute(value, "angle", [(i, i ^ by) for i in range(angles)])

    def mirrored(value, by):
        pairs = [
            (a * tiles + t, (angles - 2 - (a - a % 2) + a % 2) * tiles + t + by)
            for a in range(angles)
            for t in range(tiles)
            if 0 <= t + by < tiles
        ]
        return lax.ppermute(value, ("angle", "tile"), pairs)

    def to_slabs(value):
        return lax.all_to_all(value, "slab", 0, 0, tiled=True)

    def to_four(value):
        return lax.all_to_all(value, "angle", 0, 0, axis_index_groups=four_groups, tiled=True)

    def added(blocks):
        return jnp.sum(to_four(blocks).astype(f32), axis=0)

    own_part = lax.dynamic_index_in_dim(layer, core, 0, keepdims=False)
    after = lax.dynamic_slice(own_part, ((3 - place_z) * block_rows, 0), (block_rows, columns))
    live = (jnp.arange(slots) < counts.reshape(1)).astype(jnp.int32)
    meta = jnp.stack([offsets.reshape(slots), column_starts.reshape(slots), live], axis=1)
    after, meta = lax.optimization_barrier((after, jnp.broadcast_to(meta, (slabs, *meta.shape))))
    after = mirrored(after, -1)
    group = to_slabs(meta)
    more = jnp.max(group[:, 1:, 2]) > 0
    sheared = jnp.floor_divide((angle_ids[0] - angle_center) * (slab - slabs // 2), shear_divisor)
    others = jnp.stack([jnp.mod(sheared, columns), core, place_z])
    facts = jnp.concatenate([group.reshape(-1), others]).astype(jnp.int32)

    def exchanged(values):
        return lax.cond(
            more,
            to_slabs,
            lambda v: jnp.concatenate([to_slabs(v[:, :1]), v[:, 1:]], axis=1),
            values,
        )

    uppers = cut_windows(facts, slabs, slots, 0, [layer], window_rows, width)
    after, uppers = lax.optimization_barrier((after, uppers))
    uppers = to_slabs(uppers)
    mine = [after] + [swap(after, k << 1) for k in range(1, 4)]
    afters = mine + [swap(jnp.stack(mine), 1)]
    afters, uppers = lax.optimization_barrier((afters, uppers))
    lowers = cut_windows(facts, slabs, slots, HALO - tile_rows, afters, window_rows, width)
    lowers = exchanged(lowers)

    gradients = exchanged(patch_gradients(live, uppers, lowers, probe_wave, patterns, tables))

    def placed(first_row, reverse):
        keep, send = place_windows(facts, gradients, first_row, reverse, window_rows, tile_rows, columns)
        return (keep + swap(send, 1).astype(f32)).astype(bf16).reshape(4, block_rows, columns)

    spill, own = placed(HALO, True), placed(0, False)
    spill, own = lax.optimization_barrier((added(spill).astype(bf16), own))
    spill = mirrored(spill, 1)
    total = lax.optimization_barrier((added(own) + spill.astype(f32)).astype(bf16))
    total = (total.astype(f32) + swap(total, 8).astype(f32)).astype(bf16)

    total = to_four(jnp.broadcast_to(total, (4, *total.shape))).reshape(tile_rows, columns)
    new = step(core, layer, total)
    return step(1 - core, layer, swap(total, 1), new).reshape(volume.shape)


def solution(mesh):
    in_specs = (
        P(None, "slab", "tile", None),
        P(),
        P("angle", "tile", "slab", None, None, None),
        P("angle", "tile", "slab", None),
        P("angle", "tile", "slab", None),
        P("angle", "tile", "slab"),
        P("angle"),
    )
    out_specs = P(None, "slab", "tile", None)
    return jax.shard_map(
        per_device, mesh=mesh, in_specs=in_specs, out_specs=out_specs, check_vma=False
    )
```

```python
import functools

import jax
import jax.numpy as jnp
import ml_dtypes
import numpy as np
from jax import lax
from jax.experimental import pallas as pl
from jax.experimental.pallas import tpu as pltpu
from jax.sharding import PartitionSpec as P

angle_center = 600
shear_divisor = 64
step_size = 0.03
floor_square = 0.25

LANE = 128
HALO = 64


def dft_tables(plane_width):
    index_line = np.arange(plane_width, dtype=np.int32)
    product_mod = np.mod(index_line[:, None] * index_line[None, :], plane_width)
    phase_table = product_mod.astype(np.float32) * np.float32(2.0 * 3.141592653589793 / plane_width)
    scale_factor = np.float32(plane_width ** (-0.5))
    table_real = (np.cos(phase_table) * scale_factor).astype(ml_dtypes.bfloat16)
    table_imag = (-np.sin(phase_table) * scale_factor).astype(ml_dtypes.bfloat16)
    return table_real, table_imag


def dot(left, right):
    return jnp.dot(left, right, preferred_element_type=jnp.float32)


def one_hot(rows, columns, down):
    row = lax.broadcasted_iota(jnp.int32, (rows, columns), 0)
    column = lax.broadcasted_iota(jnp.int32, (rows, columns), 1)
    return (row - column == down).astype(jnp.float32).astype(jnp.bfloat16)


VMEM = pl.BlockSpec(memory_space=pltpu.VMEM)


def call(body, out_shape, scratch, facts, *args):
    return pl.pallas_call(
        body,
        out_shape=out_shape,
        in_specs=[pl.BlockSpec(memory_space=pltpu.SMEM)] + [VMEM] * len(args),
        out_specs=[VMEM] * len(out_shape),
        scratch_shapes=scratch,
        compiler_params=pltpu.CompilerParams(vmem_limit_bytes=24 * 1024 * 1024),
    )(facts, *args)


class Facts:
    def __init__(self, ref, slabs, slots):
        self.ref, self.slots = ref, slots
        self.shift, self.core, self.place_z = (ref[3 * slabs * slots + i] for i in range(3))

    def slot(self, slab, slot):
        return tuple(self.ref[3 * (slab * self.slots + slot) + i] for i in range(3))


def column_blocks(left, width, columns):
    blocks = columns // LANE
    return [
        pl.multiple_of(lax.rem(left // LANE + i, blocks) * LANE, LANE) for i in range(width // LANE + 1)
    ]


def cut_body(down, facts_ref, *refs):
    blocks, (out, held) = refs[:-2], refs[-2:]
    slabs, slots, _, rows, width = out.shape
    facts = Facts(facts_ref, slabs, slots)
    if len(blocks) == 1:
        held = blocks[0]
    else:
        *mine, other = blocks
        size = mine[0].shape[0]
        for k, block in enumerate(mine):
            at = pl.ds(pl.multiple_of((facts.place_z ^ k) * size, size), size)
            held[facts.core, at] = block[...]
            held[1 - facts.core, at] = other[k]
    tile_rows, columns = held.shape[1:]

    for slot in range(slots):
        for slab in range(slabs):
            row, column, live = facts.slot(slab, slot)

            @pl.when(live > 0)
            def _():
                left = lax.rem(column + facts.shift, columns)
                pick_rows = one_hot(rows, tile_rows, -(row + down))
                pick_columns = one_hot(width + LANE, width, lax.rem(left, LANE))
                wide = jnp.concatenate(
                    [held[:, :, pl.ds(start, LANE)] for start in column_blocks(left, width, columns)], axis=2
                )
                narrow = dot(wide.reshape(2 * tile_rows, width + LANE), pick_columns).astype(jnp.bfloat16)
                for part in range(2):
                    picked = dot(pick_rows, narrow[part * tile_rows : (part + 1) * tile_rows])
                    out[slab, slot, part] = picked.astype(jnp.bfloat16)


def cut_windows(facts, slabs, slots, down, blocks, rows, width):
    out = jax.ShapeDtypeStruct((slabs, slots, 2, rows, width), jnp.bfloat16)
    size, columns = blocks[0].shape[-2:]
    held = pltpu.VMEM((2, size * max(1, len(blocks) - 1), columns), jnp.bfloat16)
    return call(functools.partial(cut_body, down), [out], [held], facts, *blocks)[0]


def cos_sin(angle):
    turns = jnp.round(angle * 0.6366197723675814)
    rest = angle - turns * 1.5703125
    rest = rest - turns * 4.837512969970703e-4
    rest = rest - turns * 7.549789948768648e-8
    square = rest * rest
    sine = (-1.9515295891e-4 * square + 8.3321608736e-3) * square - 1.6666654611e-1
    sine = sine * square * rest + rest
    cosine = (2.443315711809948e-5 * square - 1.388731625493765e-3) * square + 4.166664568298827e-2
    cosine = cosine * square * square - 0.5 * square + 1.0
    quarter = turns.astype(jnp.int32)
    odd = (quarter & 1) == 1
    first, second = jnp.where(odd, sine, cosine), jnp.where(odd, cosine, sine)
    return (
        jnp.where(((quarter + 1) & 2) == 2, -first, first),
        jnp.where((quarter & 2) == 2, -second, second),
    )


def patch_body(live_ref, uppers, lowers, probe, patterns, wr_ref, wi_ref, out):
    slabs, slots, _, rows, _ = uppers.shape
    f32, bf16 = jnp.float32, jnp.bfloat16

    def window(slot, part):
        def projected(ref):
            return sum(ref[slab, slot, part].astype(f32) for slab in range(slabs)).astype(bf16).astype(f32)

        above, below = projected(uppers), projected(lowers)
        return jnp.concatenate(
            [above[:HALO], above[HALO:] + below[: rows - HALO], below[rows - HALO :]], axis=0
        )

    for slot in range(slots):

        @pl.when(live_ref[slot] > 0)
        def _():
            phase, absorption = window(slot, 0), window(slot, 1)
            magnitude = jnp.exp(-absorption)
            cosine, sine = cos_sin(phase)
            trans_real = magnitude * cosine
            trans_imag = magnitude * sine
            probe_real, probe_imag = probe[0], probe[1]
            wr, wi = wr_ref[...], wi_ref[...]
            wave_real = (probe_real * trans_real - probe_imag * trans_imag).astype(bf16)
            wave_imag = (probe_real * trans_imag + probe_imag * trans_real).astype(bf16)
            left_real = (dot(wr, wave_real) - dot(wi, wave_imag)).astype(bf16)
            left_imag = (dot(wr, wave_imag) + dot(wi, wave_real)).astype(bf16)
            far_real = dot(left_real, wr) - dot(left_imag, wi)
            far_imag = dot(left_real, wi) + dot(left_imag, wr)
            power = far_real * far_real + far_imag * far_imag + floor_square
            keeping = 1.0 - patterns[slot].astype(f32) * lax.rsqrt(power)
            resid_real = (far_real * keeping).astype(bf16)
            resid_imag = (far_imag * keeping).astype(bf16)
            back_real = (dot(wr, resid_real) + dot(wi, resid_imag)).astype(bf16)
            back_imag = (dot(wr, resid_imag) - dot(wi, resid_real)).astype(bf16)
            exit_real = dot(back_real, wr) + dot(back_imag, wi)
            exit_imag = dot(back_imag, wr) - dot(back_real, wi)
            mixed_real = probe_real * exit_real + probe_imag * exit_imag
            mixed_imag = probe_real * exit_imag - probe_imag * exit_real
            phase_out = (trans_real * mixed_imag - trans_imag * mixed_real).astype(bf16)
            absorption_out = (-(trans_real * mixed_real + trans_imag * mixed_imag)).astype(bf16)
            for slab in range(slabs):
                out[slab, slot, 0] = phase_out
                out[slab, slot, 1] = absorption_out


def patch_gradients(live, uppers, lowers, probe_wave, patterns, tables):
    slabs, slots, _, _, width = uppers.shape
    out = jax.ShapeDtypeStruct((slabs, slots, 2, width, width), jnp.bfloat16)
    return call(patch_body, [out], [], live, uppers, lowers, probe_wave, patterns, *tables)[0]


def place_body(first_row, rows, reverse, facts_ref, windows, keep_out, send_out, total):
    slabs, slots, _, width, _ = windows.shape
    tile_rows, columns = keep_out.shape
    facts = Facts(facts_ref, slabs, slots)
    down = first_row - (tile_rows if first_row else 0)
    total[...] = jnp.zeros_like(total)
    for slot in range(slots):
        for slab in range(slabs):
            row, column, live = facts.slot(slab, slot)

            @pl.when(live > 0)
            def _():
                left = lax.rem(column + facts.shift, columns)
                put_rows = one_hot(tile_rows, rows, row + down)
                put_columns = one_hot(width, width + LANE, -lax.rem(left, LANE))
                moved = [
                    dot(put_rows, windows[slab, slot, part, first_row : first_row + rows]) for part in range(2)
                ]
                wide = dot(jnp.concatenate(moved, axis=0).astype(jnp.bfloat16), put_columns)
                wide = wide.reshape(2, tile_rows, width + LANE)
                for i, start in enumerate(column_blocks(left, width, columns)):
                    total[:, :, pl.ds(start, LANE)] += wide[:, :, i * LANE : (i + 1) * LANE]

    blocks = 4 if reverse else 1
    size = tile_rows // blocks
    for block in range(blocks):
        here = slice(block * size, (block + 1) * size)
        there = slice((blocks - 1 - block) * size, (blocks - block) * size)
        keep_out[there] = total[facts.core, here]
        send_out[there] = total[1 - facts.core, here].astype(jnp.bfloat16)


def place_windows(facts, windows, first_row, reverse, rows, tile_rows, columns):
    shapes = [jax.ShapeDtypeStruct((tile_rows, columns), t) for t in (jnp.float32, jnp.bfloat16)]
    total = pltpu.VMEM((2, tile_rows, columns), jnp.float32)
    return call(functools.partial(place_body, first_row, rows, reverse), shapes, [total], facts, windows)


def step_body(part_ref, layer, gradient, *refs):
    out, made, sems = refs[-3:]
    part = part_ref[0]
    size = gradient.shape[0] // 4
    copies = []
    for n in range(4):
        rows = slice(n * size, (n + 1) * size)
        made[rows] = layer[part, rows].astype(jnp.float32) - step_size * gradient[rows].astype(jnp.float32)
        copies.append(
            pltpu.make_async_copy(made.at[pl.ds(n * size, size)], out.at[part, pl.ds(n * size, size)], sems.at[n])
        )
        copies[-1].start()
    for copy in copies:
        copy.wait()


def step(part, layer, gradient, *stepped):
    return pl.pallas_call(
        step_body,
        out_shape=jax.ShapeDtypeStruct(layer.shape, jnp.float32),
        in_specs=[pl.BlockSpec(memory_space=pltpu.SMEM), VMEM, VMEM]
        + [pl.BlockSpec(memory_space=pltpu.HBM)] * len(stepped),
        out_specs=pl.BlockSpec(memory_space=pltpu.HBM),
        scratch_shapes=[pltpu.VMEM(gradient.shape, jnp.float32), pltpu.SemaphoreType.DMA((4,))],
        input_output_aliases={3: 0} if stepped else {},
        compiler_params=pltpu.CompilerParams(vmem_limit_bytes=24 * 1024 * 1024),
    )(part.reshape(1).astype(jnp.int32), layer, gradient, *stepped)


def per_device(volume, probe_wave, amplitudes, offsets, column_starts, counts, angle_ids):
    layer = volume.reshape(volume.shape[0], *volume.shape[2:])
    tile_rows, columns = layer.shape[1:]
    width = amplitudes.shape[-1]
    slots = offsets.shape[3]
    angles, slabs, tiles = (lax.axis_size(axis) for axis in ("angle", "slab", "tile"))
    slab, angle = lax.axis_index("slab"), lax.axis_index("angle")
    f32, bf16 = jnp.float32, jnp.bfloat16
    tables = dft_tables(width)
    window_rows = width - HALO
    patterns = amplitudes.reshape(slots, width, width)

    core, place_z = angle % 2, angle // 2 % 4
    four_groups = [[8 * f + 2 * q + c for q in range(4)] for f in range(angles // 8) for c in range(2)]
    block_rows = tile_rows // 4

    def swap(value, by):
        return lax.ppermute(value, "angle", [(i, i ^ by) for i in range(angles)])

    def mirrored(value, by):
        pairs = [
            (a * tiles + t, (angles - 2 - (a - a % 2) + a % 2) * tiles + t + by)
            for a in range(angles)
            for t in range(tiles)
            if 0 <= t + by < tiles
        ]
        return lax.ppermute(value, ("angle", "tile"), pairs)

    def to_slabs(value):
        return lax.all_to_all(value, "slab", 0, 0, tiled=True)

    def to_four(value):
        return lax.all_to_all(value, "angle", 0, 0, axis_index_groups=four_groups, tiled=True)

    def added(blocks):
        return jnp.sum(to_four(blocks).astype(f32), axis=0)

    own_part = lax.dynamic_index_in_dim(layer, core, 0, keepdims=False)
    after = lax.dynamic_slice(own_part, ((3 - place_z) * block_rows, 0), (block_rows, columns))
    after, counts = lax.optimization_barrier((after, counts))
    after = mirrored(after, -1)
    live = (jnp.arange(slots) < counts.reshape(1)).astype(jnp.int32)
    meta = jnp.stack([offsets.reshape(slots), column_starts.reshape(slots), live], axis=1)
    group = to_slabs(jnp.broadcast_to(meta, (slabs, *meta.shape)))
    more = jnp.max(group[:, 1:, 2]) > 0
    sheared = jnp.floor_divide((angle_ids[0] - angle_center) * (slab - slabs // 2), shear_divisor)
    others = jnp.stack([jnp.mod(sheared, columns), core, place_z])
    facts = jnp.concatenate([group.reshape(-1), others]).astype(jnp.int32)

    def exchanged(values):
        return lax.cond(
            more,
            to_slabs,
            lambda v: jnp.concatenate([to_slabs(v[:, :1]), v[:, 1:]], axis=1),
            values,
        )

    uppers = cut_windows(facts, slabs, slots, 0, [layer], window_rows, width)
    after, uppers = lax.optimization_barrier((after, uppers))
    uppers = to_slabs(uppers)
    mine = [after] + [swap(after, k << 1) for k in range(1, 4)]
    afters = mine + [swap(jnp.stack(mine), 1)]
    afters, uppers = lax.optimization_barrier((afters, uppers))
    lowers = cut_windows(facts, slabs, slots, HALO - tile_rows, afters, window_rows, width)
    lowers = exchanged(lowers)

    gradients = exchanged(patch_gradients(live, uppers, lowers, probe_wave, patterns, tables))

    def placed(first_row, reverse):
        keep, send = place_windows(facts, gradients, first_row, reverse, window_rows, tile_rows, columns)
        return (keep + swap(send, 1).astype(f32)).astype(bf16).reshape(4, block_rows, columns)

    spill, own = placed(HALO, True), placed(0, False)
    spill, own = lax.optimization_barrier((added(spill).astype(bf16), own))
    spill = mirrored(spill, 1)
    total = lax.optimization_barrier((added(own) + spill.astype(f32)).astype(bf16))
    total = (total.astype(f32) + swap(total, 8).astype(f32)).astype(bf16)

    total = to_four(jnp.broadcast_to(total, (4, *total.shape))).reshape(tile_rows, columns)
    new = step(core, layer, total)
    return step(1 - core, layer, swap(total, 1), new).reshape(volume.shape)


def solution(mesh):
    in_specs = (
        P(None, "slab", "tile", None),
        P(),
        P("angle", "tile", "slab", None, None, None),
        P("angle", "tile", "slab", None),
        P("angle", "tile", "slab", None),
        P("angle", "tile", "slab"),
        P("angle"),
    )
    out_specs = P(None, "slab", "tile", None)
    return jax.shard_map(
        per_device, mesh=mesh, in_specs=in_specs, out_specs=out_specs, check_vma=False
    )
```

```python
import functools

import jax
import jax.numpy as jnp
import ml_dtypes
import numpy as np
from jax import lax
from jax.experimental import pallas as pl
from jax.experimental.pallas import tpu as pltpu
from jax.sharding import PartitionSpec as P

angle_center = 600
shear_divisor = 64
step_size = 0.03
floor_square = 0.25

LANE = 128


def dft_tables(plane_width):
    index_line = np.arange(plane_width, dtype=np.int32)
    product_mod = np.mod(index_line[:, None] * index_line[None, :], plane_width)
    phase_table = product_mod.astype(np.float32) * np.float32(2.0 * 3.141592653589793 / plane_width)
    scale_factor = np.float32(plane_width ** (-0.5))
    table_real = (np.cos(phase_table) * scale_factor).astype(ml_dtypes.bfloat16)
    table_imag = (-np.sin(phase_table) * scale_factor).astype(ml_dtypes.bfloat16)
    return table_real, table_imag


def dot(left, right):
    return jnp.dot(left, right, preferred_element_type=jnp.float32)


def one_hot(rows, columns, down):
    row = lax.broadcasted_iota(jnp.int32, (rows, columns), 0)
    column = lax.broadcasted_iota(jnp.int32, (rows, columns), 1)
    return (row - column == down).astype(jnp.float32).astype(jnp.bfloat16)


VMEM = pl.BlockSpec(memory_space=pltpu.VMEM)


def call(body, out_shape, scratch, facts, *args):
    return pl.pallas_call(
        body,
        out_shape=out_shape,
        in_specs=[pl.BlockSpec(memory_space=pltpu.SMEM)] + [VMEM] * len(args),
        out_specs=[VMEM] * len(out_shape),
        scratch_shapes=scratch,
        compiler_params=pltpu.CompilerParams(vmem_limit_bytes=24 * 1024 * 1024),
    )(facts, *args)


class Facts:
    def __init__(self, ref, slots, slabs, columns):
        self.ref, self.slots, self.slabs, self.columns = ref, slots, slabs, columns
        self.stride = 3 * slots + 1

    def slot(self, angle, slot):
        return tuple(self.ref[self.stride * angle + 3 * slot + i] for i in range(3))

    def columns_of(self, angle, slot, step):
        layer = lax.rem(self.ref[8 * self.stride] + self.slabs + step, self.slabs)
        index = self.ref[self.stride * angle + self.stride - 1]
        shift = ((index - angle_center) * (layer - self.slabs // 2)) >> (shear_divisor.bit_length() - 1)
        shift = lax.rem(lax.rem(shift, self.columns) + self.columns, self.columns)
        left = lax.rem(self.slot(angle, slot)[1] + shift, self.columns)
        blocks = self.columns // LANE
        starts = [pl.multiple_of(lax.rem(left // LANE + i, blocks) * LANE, LANE) for i in range(3)]
        return starts, lax.rem(left, LANE)


def cut_body(slabs, facts_ref, *refs):
    blocks, out = refs[:-1], refs[-1]
    angles, slots, rows, width = out.shape
    facts = Facts(facts_ref, slots, slabs, blocks[0].shape[1])
    lane = lax.broadcasted_iota(jnp.int32, (rows, LANE), 1)
    for slot in range(slots):
        for angle in range(angles):

            @pl.when(facts.slot(angle, slot)[2] > 0)
            def _():
                total = [jnp.zeros((rows, LANE), jnp.float32)] * 2
                for k, block in enumerate(blocks):
                    starts, inside = facts.columns_of(angle, slot, -k)
                    turned = [
                        pltpu.roll(block[:, pl.ds(start, LANE)].astype(jnp.float32), (LANE - inside) % LANE, 1)
                        for start in starts
                    ]
                    here = lane < LANE - inside
                    total = [t + jnp.where(here, turned[i], turned[i + 1]) for i, t in enumerate(total)]
                out[angle, slot] = jnp.concatenate(total, axis=1).astype(jnp.bfloat16)


def cut_windows(facts, blocks, angles, slots, width):
    out = jax.ShapeDtypeStruct((angles, slots, blocks[0].shape[0], width), jnp.bfloat16)
    return call(functools.partial(cut_body, len(blocks)), [out], [], facts, *blocks)[0]


def cos_sin(angle):
    turns = jnp.round(angle * 0.6366197723675814)
    rest = angle - turns * 1.5703125
    rest = rest - turns * 4.837512969970703e-4
    rest = rest - turns * 7.549789948768648e-8
    square = rest * rest
    sine = (-1.9515295891e-4 * square + 8.3321608736e-3) * square - 1.6666654611e-1
    sine = sine * square * rest + rest
    cosine = (2.443315711809948e-5 * square - 1.388731625493765e-3) * square + 4.166664568298827e-2
    cosine = cosine * square * square - 0.5 * square + 1.0
    quarter = turns.astype(jnp.int32)
    odd = (quarter & 1) == 1
    first, second = jnp.where(odd, sine, cosine), jnp.where(odd, cosine, sine)
    return (
        jnp.where(((quarter + 1) & 2) == 2, -first, first),
        jnp.where((quarter & 2) == 2, -second, second),
    )


def patch_body(slot_ref, own_in, next_in, probe, patterns, wr_ref, wi_ref, own_out, next_out):
    angles, slots, rows, width = own_in.shape
    f32, bf16 = jnp.float32, jnp.bfloat16
    blocks = angles // 2
    tall = 2 * blocks * rows
    for slot in range(slots):
        row, live = slot_ref[2 * slot], slot_ref[2 * slot + 1]

        @pl.when(live > 0)
        def _():
            pick = one_hot(width, tall, -row)
            window = []
            for part in range(2):
                held = [ref[2 * k + part, slot] for ref in (own_in, next_in) for k in range(blocks)]
                window.append(dot(pick, jnp.concatenate(held, axis=0)))
            phase, absorption = window
            magnitude = jnp.exp(-absorption)
            cosine, sine = cos_sin(phase)
            trans_real = magnitude * cosine
            trans_imag = magnitude * sine
            probe_real, probe_imag = probe[0], probe[1]
            wr, wi = wr_ref[...], wi_ref[...]
            wave_real = (probe_real * trans_real - probe_imag * trans_imag).astype(bf16)
            wave_imag = (probe_real * trans_imag + probe_imag * trans_real).astype(bf16)
            left_real = (dot(wr, wave_real) - dot(wi, wave_imag)).astype(bf16)
            left_imag = (dot(wr, wave_imag) + dot(wi, wave_real)).astype(bf16)
            far_real = dot(left_real, wr) - dot(left_imag, wi)
            far_imag = dot(left_real, wi) + dot(left_imag, wr)
            power = far_real * far_real + far_imag * far_imag + floor_square
            keeping = 1.0 - patterns[slot].astype(f32) * lax.rsqrt(power)
            resid_real = (far_real * keeping).astype(bf16)
            resid_imag = (far_imag * keeping).astype(bf16)
            back_real = (dot(wr, resid_real) + dot(wi, resid_imag)).astype(bf16)
            back_imag = (dot(wr, resid_imag) - dot(wi, resid_real)).astype(bf16)
            exit_real = dot(back_real, wr) + dot(back_imag, wi)
            exit_imag = dot(back_imag, wr) - dot(back_real, wi)
            mixed_real = probe_real * exit_real + probe_imag * exit_imag
            mixed_imag = probe_real * exit_imag - probe_imag * exit_real
            final_real = trans_real * mixed_real + trans_imag * mixed_imag
            final_imag = trans_real * mixed_imag - trans_imag * mixed_real
            put = one_hot(tall, width, row)
            for part, value in enumerate((final_imag, -final_real)):
                placed = dot(put, value.astype(bf16)).astype(bf16)
                for k in range(blocks):
                    own_out[2 * k + part, slot] = placed[k * rows : (k + 1) * rows]
                    below = placed[(blocks + k) * rows : (blocks + k + 1) * rows]
                    next_out[2 * (blocks - 1 - k) + part, slot] = below


def patch_gradients(slot_facts, own, after, probe_wave, patterns, tables):
    out = jax.ShapeDtypeStruct(own.shape, jnp.bfloat16)
    return call(patch_body, [out, out], [], slot_facts, own, after, probe_wave, patterns, *tables)


def place_body(facts_ref, windows, *refs):
    outs, total = refs[:-1], refs[-1]
    angles, slots, rows, width = windows.shape
    facts = Facts(facts_ref, slots, len(outs), total.shape[2])
    lane = lax.broadcasted_iota(jnp.int32, (rows, LANE), 1)
    total[...] = jnp.zeros_like(total)
    for slot in range(slots):
        for angle in range(angles):

            @pl.when(facts.slot(angle, slot)[2] > 0)
            def _():
                window = windows[angle, slot].astype(jnp.float32)
                for k in range(len(outs)):
                    starts, inside = facts.columns_of(angle, slot, k)
                    first, second = (pltpu.roll(window[:, i * LANE : (i + 1) * LANE], inside, 1) for i in range(2))
                    there = lane < inside
                    total[k, :, pl.ds(starts[0], LANE)] += jnp.where(there, 0.0, first)
                    total[k, :, pl.ds(starts[1], LANE)] += jnp.where(there, first, second)
                    total[k, :, pl.ds(starts[2], LANE)] += jnp.where(there, second, 0.0)
    for k, out in enumerate(outs):
        out[...] = total[k].astype(out.dtype)


def place_windows(facts, windows, slabs, columns):
    shape = (windows.shape[2], columns)
    outs = [jax.ShapeDtypeStruct(shape, jnp.bfloat16 if k else jnp.float32) for k in range(slabs)]
    return call(place_body, outs, [pltpu.VMEM((slabs, *shape), jnp.float32)], facts, windows)


def step_body(part_ref, layer, gradient, *refs):
    out, made, sems = refs[-3:]
    part = part_ref[0]
    size = gradient.shape[0] // 4
    copies = []
    for n in range(4):
        rows = slice(n * size, (n + 1) * size)
        made[rows] = layer[part, rows].astype(jnp.float32) - step_size * gradient[rows].astype(jnp.float32)
        copies.append(
            pltpu.make_async_copy(made.at[pl.ds(n * size, size)], out.at[part, pl.ds(n * size, size)], sems.at[n])
        )
        copies[-1].start()
    for copy in copies:
        copy.wait()


def step(part, layer, gradient, *stepped):
    return pl.pallas_call(
        step_body,
        out_shape=jax.ShapeDtypeStruct(layer.shape, jnp.float32),
        in_specs=[pl.BlockSpec(memory_space=pltpu.SMEM), VMEM, VMEM]
        + [pl.BlockSpec(memory_space=pltpu.HBM)] * len(stepped),
        out_specs=pl.BlockSpec(memory_space=pltpu.HBM),
        scratch_shapes=[pltpu.VMEM(gradient.shape, jnp.float32), pltpu.SemaphoreType.DMA((4,))],
        input_output_aliases={3: 0} if stepped else {},
        compiler_params=pltpu.CompilerParams(vmem_limit_bytes=24 * 1024 * 1024),
    )(part.reshape(1).astype(jnp.int32), layer, gradient, *stepped)


def per_device(volume, probe_wave, amplitudes, offsets, column_starts, counts, angle_ids):
    layer = volume.reshape(volume.shape[0], *volume.shape[2:])
    tile_rows, columns = layer.shape[1:]
    width = amplitudes.shape[-1]
    slots = offsets.shape[3]
    angles, slabs, tiles = (lax.axis_size(axis) for axis in ("angle", "slab", "tile"))
    slab, angle = lax.axis_index("slab"), lax.axis_index("angle")
    f32, bf16 = jnp.float32, jnp.bfloat16
    tables = dft_tables(width)
    patterns = amplitudes.reshape(slots, width, width)

    core, place_z = angle % 2, angle // 2 % 4
    eight_groups = [[8 * f + i for i in range(8)] for f in range(angles // 8)]
    four_groups = [[8 * f + 2 * q + c for q in range(4)] for f in range(angles // 8) for c in range(2)]
    block_rows = tile_rows // 4

    def swap(value, by):
        return lax.ppermute(value, "angle", [(i, i ^ by) for i in range(angles)])

    def mirrored(value, by):
        pairs = [
            (a * tiles + t, (angles - 2 - (a - a % 2) + a % 2) * tiles + t + by)
            for a in range(angles)
            for t in range(tiles)
            if 0 <= t + by < tiles
        ]
        return lax.ppermute(value, ("angle", "tile"), pairs)

    def to_slab(value, by):
        return lax.ppermute(value, "slab", [(i, (i + by) % slabs) for i in range(slabs)])

    def to_eight(value):
        return lax.all_to_all(value, "angle", 0, 0, axis_index_groups=eight_groups, tiled=True)

    def to_four(value):
        return lax.all_to_all(value, "angle", 0, 0, axis_index_groups=four_groups, tiled=True)

    def of_slabs(block):
        return [block] + [to_slab(block, k) for k in range(1, slabs)]

    def over_slabs(kept, *sent):
        return sum((to_slab(block, k + 1).astype(f32) for k, block in enumerate(sent)), kept)

    own_part = lax.dynamic_index_in_dim(layer, core, 0, keepdims=False)

    def rows_of(block):
        return lax.dynamic_slice(own_part, (block * block_rows, 0), (block_rows, columns))

    after, own, counts = lax.optimization_barrier((rows_of(3 - place_z), rows_of(place_z), counts))
    after, own = mirrored(after, -1), of_slabs(own)

    live = (jnp.arange(slots) < counts.reshape(1)).astype(jnp.int32)
    meta = jnp.stack([offsets.reshape(slots), column_starts.reshape(slots), live], axis=1)
    eight = to_eight(jnp.broadcast_to(jnp.concatenate([meta.reshape(-1), angle_ids]), (8, 3 * slots + 1)))
    facts = jnp.concatenate([eight.reshape(-1), slab.reshape(1)]).astype(jnp.int32)
    slot_facts = jnp.stack([offsets.reshape(slots), live], axis=1).reshape(-1)

    own = cut_windows(facts, own, 8, slots, width)
    after, own = lax.optimization_barrier((after, own))
    after, own = lax.optimization_barrier((of_slabs(after), to_eight(own)))
    after = to_eight(cut_windows(facts, after, 8, slots, width))

    own, after = patch_gradients(slot_facts, own, after, probe_wave, patterns, tables)
    after = place_windows(facts, to_eight(after), slabs, columns)
    after, own = lax.optimization_barrier((after, own))
    spill = mirrored(over_slabs(*after).astype(bf16), 1)
    own = over_slabs(*place_windows(facts, to_eight(own), slabs, columns))

    total = lax.optimization_barrier((own + spill.astype(f32)).astype(bf16))
    total = (total.astype(f32) + swap(total, 8).astype(f32)).astype(bf16)

    total = to_four(jnp.broadcast_to(total, (4, *total.shape))).reshape(tile_rows, columns)
    new = step(core, layer, total)
    return step(1 - core, layer, swap(total, 1), new).reshape(volume.shape)


def solution(mesh):
    in_specs = (
        P(None, "slab", "tile", None),
        P(),
        P("angle", "tile", "slab", None, None, None),
        P("angle", "tile", "slab", None),
        P("angle", "tile", "slab", None),
        P("angle", "tile", "slab"),
        P("angle"),
    )
    out_specs = P(None, "slab", "tile", None)
    return jax.shard_map(
        per_device, mesh=mesh, in_specs=in_specs, out_specs=out_specs, check_vma=False
    )
```

```python
import functools

import jax
import jax.numpy as jnp
import ml_dtypes
import numpy as np
from jax import lax
from jax.experimental import pallas as pl
from jax.experimental.pallas import tpu as pltpu
from jax.sharding import PartitionSpec as P

angle_center = 600
shear_divisor = 64
step_size = 0.03
floor_square = 0.25

LANE = 128


def dft_tables(plane_width):
    index_line = np.arange(plane_width, dtype=np.int32)
    product_mod = np.mod(index_line[:, None] * index_line[None, :], plane_width)
    phase_table = product_mod.astype(np.float32) * np.float32(2.0 * 3.141592653589793 / plane_width)
    scale_factor = np.float32(plane_width ** (-0.5))
    table_real = (np.cos(phase_table) * scale_factor).astype(ml_dtypes.bfloat16)
    table_imag = (-np.sin(phase_table) * scale_factor).astype(ml_dtypes.bfloat16)
    return table_real, table_imag


def dot(left, right):
    return jnp.dot(left, right, preferred_element_type=jnp.float32)


def one_hot(rows, columns, down):
    row = lax.broadcasted_iota(jnp.int32, (rows, columns), 0)
    column = lax.broadcasted_iota(jnp.int32, (rows, columns), 1)
    return (row - column == down).astype(jnp.float32).astype(jnp.bfloat16)


VMEM = pl.BlockSpec(memory_space=pltpu.VMEM)


def call(body, out_shape, scratch, *args):
    smem = pl.BlockSpec(memory_space=pltpu.SMEM)
    return pl.pallas_call(
        body,
        out_shape=out_shape,
        in_specs=[smem if x.dtype == jnp.int32 else VMEM for x in args],
        out_specs=[VMEM] * len(out_shape),
        scratch_shapes=scratch,
        compiler_params=pltpu.CompilerParams(vmem_limit_bytes=24 * 1024 * 1024),
    )(*args)


def facts_body(rows_ref, columns_ref, count_ref, index_ref, out):
    values = []
    for slot in range(rows_ref.shape[0]):
        values += [rows_ref[slot], columns_ref[slot], (slot < count_ref[0]).astype(jnp.int32)]
    lane = lax.broadcasted_iota(jnp.int32, out.shape, 1)
    line = jnp.zeros(out.shape, jnp.int32)
    for n, value in enumerate(values + [index_ref[0]]):
        line = jnp.where(lane == n, value, line)
    out[...] = line


class Facts:
    def __init__(self, ref, slab_ref, slots, slabs, columns):
        self.ref, self.slab, self.slots, self.slabs, self.columns = ref, slab_ref[0], slots, slabs, columns

    def slot(self, angle, slot):
        return tuple(self.ref[angle, 3 * slot + i] for i in range(3))

    def layer(self, step):
        layer = self.slab + step
        layer = jnp.where(layer < 0, layer + self.slabs, layer)
        return jnp.where(layer >= self.slabs, layer - self.slabs, layer)

    def columns_of(self, angle, slot, layer):
        index = self.ref[angle, 3 * self.slots]
        shift = ((index - angle_center) * (layer - self.slabs // 2)) >> (shear_divisor.bit_length() - 1)
        left = self.slot(angle, slot)[1] + shift
        left = jnp.where(left < 0, left + self.columns, left)
        left = jnp.where(left >= self.columns, left - self.columns, left)
        starts = []
        for i in range(3):
            start = (left & -LANE) + i * LANE
            start = jnp.where(start >= self.columns, start - self.columns, start)
            starts.append(pl.multiple_of(start, LANE))
        return starts, left & (LANE - 1)


def cut_body(absolute, facts_ref, slab_ref, *refs):
    blocks, out = refs[:-1], refs[-1]
    angles, slots, rows, width = out.shape
    facts = Facts(facts_ref, slab_ref, slots, len(blocks), blocks[0].shape[1])
    lane = lax.broadcasted_iota(jnp.int32, (rows, LANE), 1)
    for slot in range(slots):
        for angle in range(angles):

            @pl.when(facts.slot(angle, slot)[2] > 0)
            def _():
                total = [jnp.zeros((rows, LANE), jnp.float32)] * 2
                for k, block in enumerate(blocks):
                    layer = k if absolute else facts.layer(-k)
                    starts, inside = facts.columns_of(angle, slot, layer)
                    turned = [
                        pltpu.roll(block[:, pl.ds(start, LANE)].astype(jnp.float32), (LANE - inside) & (LANE - 1), 1)
                        for start in starts
                    ]
                    here = lane < LANE - inside
                    total = [t + jnp.where(here, turned[i], turned[i + 1]) for i, t in enumerate(total)]
                out[angle, slot] = jnp.concatenate(total, axis=1).astype(jnp.bfloat16)


def cut_windows(facts, blocks, angles, slots, width):
    out = jax.ShapeDtypeStruct((angles, slots, blocks[0].shape[0], width), jnp.bfloat16)
    return call(functools.partial(cut_body, False), [out], [], *facts, *blocks)[0]


def cut_rest(facts, blocks, done, which):
    angles, slots, rows, width = done.shape
    out = jax.ShapeDtypeStruct((angles, 2, slots, rows, width), jnp.bfloat16)

    def body(facts_ref, slab_ref, blocks, done, out):
        out[:, 1 - which] = done[...]
        cut_body(True, facts_ref, slab_ref, *(blocks.at[k] for k in range(blocks.shape[0])), out.at[:, which])

    return call(body, [out], [], *facts, blocks, done)[0]


def cos_sin(angle):
    turns = jnp.round(angle * 0.6366197723675814)
    rest = angle - turns * 1.5703125
    rest = rest - turns * 4.837512969970703e-4
    rest = rest - turns * 7.549789948768648e-8
    square = rest * rest
    sine = (-1.9515295891e-4 * square + 8.3321608736e-3) * square - 1.6666654611e-1
    sine = sine * square * rest + rest
    cosine = (2.443315711809948e-5 * square - 1.388731625493765e-3) * square + 4.166664568298827e-2
    cosine = cosine * square * square - 0.5 * square + 1.0
    quarter = turns.astype(jnp.int32)
    odd = (quarter & 1) == 1
    first, second = jnp.where(odd, sine, cosine), jnp.where(odd, cosine, sine)
    return (
        jnp.where(((quarter + 1) & 2) == 2, -first, first),
        jnp.where((quarter & 2) == 2, -second, second),
    )


def patch_body(row_ref, count_ref, windows, probe, patterns, wr_ref, wi_ref, own_out, next_out):
    angles, _, slots, rows, width = windows.shape
    f32, bf16 = jnp.float32, jnp.bfloat16
    blocks = angles // 2
    tall = 2 * blocks * rows
    for slot in range(slots):
        row = row_ref[slot]

        @pl.when(slot < count_ref[0])
        def _():
            pick = one_hot(width, tall, -row)
            window = []
            for part in range(2):
                held = [windows[2 * k + part, tile, slot] for tile in range(2) for k in range(blocks)]
                window.append(dot(pick, jnp.concatenate(held, axis=0)))
            phase, absorption = window
            magnitude = jnp.exp(-absorption)
            cosine, sine = cos_sin(phase)
            trans_real = magnitude * cosine
            trans_imag = magnitude * sine
            probe_real, probe_imag = probe[0], probe[1]
            wr, wi = wr_ref[...], wi_ref[...]
            wave_real = (probe_real * trans_real - probe_imag * trans_imag).astype(bf16)
            wave_imag = (probe_real * trans_imag + probe_imag * trans_real).astype(bf16)
            left_real = (dot(wr, wave_real) - dot(wi, wave_imag)).astype(bf16)
            left_imag = (dot(wr, wave_imag) + dot(wi, wave_real)).astype(bf16)
            far_real = dot(left_real, wr) - dot(left_imag, wi)
            far_imag = dot(left_real, wi) + dot(left_imag, wr)
            power = far_real * far_real + far_imag * far_imag + floor_square
            keeping = 1.0 - patterns[slot].astype(f32) * lax.rsqrt(power)
            resid_real = (far_real * keeping).astype(bf16)
            resid_imag = (far_imag * keeping).astype(bf16)
            back_real = (dot(wr, resid_real) + dot(wi, resid_imag)).astype(bf16)
            back_imag = (dot(wr, resid_imag) - dot(wi, resid_real)).astype(bf16)
            exit_real = dot(back_real, wr) + dot(back_imag, wi)
            exit_imag = dot(back_imag, wr) - dot(back_real, wi)
            mixed_real = probe_real * exit_real + probe_imag * exit_imag
            mixed_imag = probe_real * exit_imag - probe_imag * exit_real
            final_real = trans_real * mixed_real + trans_imag * mixed_imag
            final_imag = trans_real * mixed_imag - trans_imag * mixed_real
            put = one_hot(tall, width, row)
            for part, value in enumerate((final_imag, -final_real)):
                placed = dot(put, value.astype(bf16)).astype(bf16)
                for k in range(blocks):
                    own_out[2 * k + part, slot] = placed[k * rows : (k + 1) * rows]
                    below = placed[(blocks + k) * rows : (blocks + k + 1) * rows]
                    next_out[2 * (blocks - 1 - k) + part, slot] = below


def patch_gradients(slot_rows, count, windows, probe_wave, patterns, tables):
    angles, _, slots, rows, width = windows.shape
    out = jax.ShapeDtypeStruct((angles, slots, rows, width), jnp.bfloat16)
    return call(patch_body, [out, out], [], slot_rows, count, windows, probe_wave, patterns, *tables)


def place_body(facts_ref, slab_ref, windows, *refs):
    outs, total = refs[:-1], refs[-1]
    angles, slots, rows, width = windows.shape
    slabs = total.shape[0]
    facts = Facts(facts_ref, slab_ref, slots, slabs, total.shape[2])
    lane = lax.broadcasted_iota(jnp.int32, (rows, LANE), 1)
    total[...] = jnp.zeros_like(total)
    for slot in range(slots):
        for angle in range(angles):

            @pl.when(facts.slot(angle, slot)[2] > 0)
            def _():
                window = windows[angle, slot].astype(jnp.float32)
                for k in range(slabs):
                    layer = facts.layer(k) if len(outs) > 1 else k
                    starts, inside = facts.columns_of(angle, slot, layer)
                    first, second = (pltpu.roll(window[:, i * LANE : (i + 1) * LANE], inside, 1) for i in range(2))
                    there = lane < inside
                    total[k, :, pl.ds(starts[0], LANE)] += jnp.where(there, 0.0, first)
                    total[k, :, pl.ds(starts[1], LANE)] += jnp.where(there, first, second)
                    total[k, :, pl.ds(starts[2], LANE)] += jnp.where(there, second, 0.0)
    for k, out in enumerate(outs):
        out[...] = (total[k] if len(outs) > 1 else total[...]).astype(out.dtype)


def place_windows(facts, windows, slabs, columns, together=False):
    shape = (windows.shape[2], columns)
    outs = [jax.ShapeDtypeStruct(shape, jnp.bfloat16 if k else jnp.float32) for k in range(slabs)]
    if together:
        outs = [jax.ShapeDtypeStruct((slabs, *shape), jnp.bfloat16)]
    return call(place_body, outs, [pltpu.VMEM((slabs, *shape), jnp.float32)], *facts, windows)


def step_body(part_ref, layer, gradient, *refs):
    out, made, sems = refs[-3:]
    part = part_ref[0]
    size = gradient.shape[0] // 4
    copies = []
    for n in range(4):
        rows = slice(n * size, (n + 1) * size)
        made[rows] = layer[part, rows].astype(jnp.float32) - step_size * gradient[rows].astype(jnp.float32)
        copies.append(
            pltpu.make_async_copy(made.at[pl.ds(n * size, size)], out.at[part, pl.ds(n * size, size)], sems.at[n])
        )
        copies[-1].start()
    for copy in copies:
        copy.wait()


def step(part, layer, gradient, *stepped):
    return pl.pallas_call(
        step_body,
        out_shape=jax.ShapeDtypeStruct(layer.shape, jnp.float32),
        in_specs=[pl.BlockSpec(memory_space=pltpu.SMEM), VMEM, VMEM]
        + [pl.BlockSpec(memory_space=pltpu.HBM)] * len(stepped),
        out_specs=pl.BlockSpec(memory_space=pltpu.HBM),
        scratch_shapes=[pltpu.VMEM(gradient.shape, jnp.float32), pltpu.SemaphoreType.DMA((4,))],
        input_output_aliases={3: 0} if stepped else {},
        compiler_params=pltpu.CompilerParams(vmem_limit_bytes=24 * 1024 * 1024),
    )(part.reshape(1).astype(jnp.int32), layer, gradient, *stepped)


def per_device(volume, probe_wave, amplitudes, offsets, column_starts, counts, angle_ids):
    layer = volume.reshape(volume.shape[0], *volume.shape[2:])
    tile_rows, columns = layer.shape[1:]
    width = amplitudes.shape[-1]
    slots = offsets.shape[3]
    angles, slabs, tiles = (lax.axis_size(axis) for axis in ("angle", "slab", "tile"))
    slab, angle = lax.axis_index("slab"), lax.axis_index("angle")
    f32, bf16 = jnp.float32, jnp.bfloat16
    tables = dft_tables(width)
    patterns = amplitudes.reshape(slots, width, width)

    core, place_z = angle % 2, angle // 2 % 4
    eight_groups = [[8 * f + i for i in range(8)] for f in range(angles // 8)]
    four_groups = [[8 * f + 2 * q + c for q in range(4)] for f in range(angles // 8) for c in range(2)]
    block_rows = tile_rows // 4

    def swap(value, by):
        return lax.ppermute(value, "angle", [(i, i ^ by) for i in range(angles)])

    def mirrored(value, by):
        pairs = [
            (a * tiles + t, (angles - 2 - (a - a % 2) + a % 2) * tiles + t + by)
            for a in range(angles)
            for t in range(tiles)
            if 0 <= t + by < tiles
        ]
        return lax.ppermute(value, ("angle", "tile"), pairs)

    def to_slab(value, by):
        return lax.ppermute(value, "slab", [(i, (i + by) % slabs) for i in range(slabs)])

    def to_eight(value):
        return lax.all_to_all(value, "angle", 0, 0, axis_index_groups=eight_groups, tiled=True)

    def to_four(value):
        return lax.all_to_all(value, "angle", 0, 0, axis_index_groups=four_groups, tiled=True)

    def to_slabs(value):
        return lax.all_to_all(value, "slab", 0, 0, tiled=True)

    def of_slabs(block):
        return [block] + [to_slab(block, k) for k in range(1, slabs)]

    def over_slabs(kept, *sent):
        return sum((to_slab(block, k + 1).astype(f32) for k, block in enumerate(sent)), kept)

    own_part = lax.dynamic_index_in_dim(layer, core, 0, keepdims=False)

    def rows_of(block):
        return lax.dynamic_slice(own_part, (block * block_rows, 0), (block_rows, columns))

    after, own, counts = lax.optimization_barrier((rows_of(3 - place_z), rows_of(place_z), counts))
    after = mirrored(after, -1)

    slot_rows, count = offsets.reshape(slots), counts.reshape(1)
    line = jax.ShapeDtypeStruct((8, LANE), jnp.int32)
    meta = call(facts_body, [line], [], slot_rows, column_starts.reshape(slots), count, angle_ids)[0]
    eight = to_eight(meta)
    eight, own = lax.optimization_barrier((eight, own))
    facts = (eight, slab.reshape(1).astype(jnp.int32))
    own = of_slabs(own)
    after, own = lax.optimization_barrier((after, own))
    own = cut_windows(facts, own, 8, slots, width)
    after = to_slabs(jnp.broadcast_to(after, (slabs, *after.shape)))
    after, own = lax.optimization_barrier((after, own))
    windows = to_eight(cut_rest(facts, after, own, 1))

    own, after = patch_gradients(slot_rows, count, windows, probe_wave, patterns, tables)
    after, own = lax.optimization_barrier((to_eight(after), own))
    own = to_eight(own)
    spill = mirrored(over_slabs(*place_windows(facts, after, slabs, columns)).astype(bf16), 1)
    own = to_slabs(place_windows(facts, own, slabs, columns, together=True)[0])
    own = jnp.sum(own.astype(f32), axis=0)

    total = lax.optimization_barrier((own + spill.astype(f32)).astype(bf16))
    total = (total.astype(f32) + swap(total, 8).astype(f32)).astype(bf16)

    total = to_four(jnp.broadcast_to(total, (4, *total.shape))).reshape(tile_rows, columns)
    new = step(core, layer, total)
    return step(1 - core, layer, swap(total, 1), new).reshape(volume.shape)


def solution(mesh):
    in_specs = (
        P(None, "slab", "tile", None),
        P(),
        P("angle", "tile", "slab", None, None, None),
        P("angle", "tile", "slab", None),
        P("angle", "tile", "slab", None),
        P("angle", "tile", "slab"),
        P("angle"),
    )
    out_specs = P(None, "slab", "tile", None)
    return jax.shard_map(
        per_device, mesh=mesh, in_specs=in_specs, out_specs=out_specs, check_vma=False
    )
```

```python
import functools

import jax
import jax.numpy as jnp
import ml_dtypes
import numpy as np
from jax import lax
from jax.experimental import pallas as pl
from jax.experimental.pallas import tpu as pltpu
from jax.sharding import PartitionSpec as P

angle_center = 600
shear_divisor = 64
step_size = 0.03
floor_square = 0.25

LANE = 128


def dft_tables(plane_width):
    index_line = np.arange(plane_width, dtype=np.int32)
    product_mod = np.mod(index_line[:, None] * index_line[None, :], plane_width)
    phase_table = product_mod.astype(np.float32) * np.float32(2.0 * 3.141592653589793 / plane_width)
    scale_factor = np.float32(plane_width ** (-0.5))
    table_real = (np.cos(phase_table) * scale_factor).astype(ml_dtypes.bfloat16)
    table_imag = (-np.sin(phase_table) * scale_factor).astype(ml_dtypes.bfloat16)
    return table_real, table_imag


def dot(left, right):
    return jnp.dot(left, right, preferred_element_type=jnp.float32)


def one_hot(rows, columns, down):
    row = lax.broadcasted_iota(jnp.int32, (rows, columns), 0)
    column = lax.broadcasted_iota(jnp.int32, (rows, columns), 1)
    return (row - column == down).astype(jnp.float32).astype(jnp.bfloat16)


VMEM = pl.BlockSpec(memory_space=pltpu.VMEM)


def call(body, out_shape, scratch, *args):
    smem = pl.BlockSpec(memory_space=pltpu.SMEM)
    return pl.pallas_call(
        body,
        out_shape=out_shape,
        in_specs=[smem if x.dtype == jnp.int32 else VMEM for x in args],
        out_specs=[VMEM] * len(out_shape),
        scratch_shapes=scratch,
        compiler_params=pltpu.CompilerParams(vmem_limit_bytes=24 * 1024 * 1024),
    )(*args)


def facts_body(rows_ref, columns_ref, count_ref, index_ref, out):
    values = []
    for slot in range(rows_ref.shape[0]):
        values += [rows_ref[slot], columns_ref[slot], (slot < count_ref[0]).astype(jnp.int32)]
    lane = lax.broadcasted_iota(jnp.int32, out.shape, 1)
    line = jnp.zeros(out.shape, jnp.int32)
    for n, value in enumerate(values + [index_ref[0]]):
        line = jnp.where(lane == n, value, line)
    out[...] = line


class Facts:
    def __init__(self, ref, slab_ref, slots, slabs, columns):
        self.ref, self.slab, self.slots, self.slabs, self.columns = ref, slab_ref[0], slots, slabs, columns

    def slot(self, angle, slot):
        return tuple(self.ref[angle, 3 * slot + i] for i in range(3))

    def layer(self, step):
        layer = self.slab + step
        layer = jnp.where(layer < 0, layer + self.slabs, layer)
        return jnp.where(layer >= self.slabs, layer - self.slabs, layer)

    def columns_of(self, angle, slot, layer):
        index = self.ref[angle, 3 * self.slots]
        shift = ((index - angle_center) * (layer - self.slabs // 2)) >> (shear_divisor.bit_length() - 1)
        left = self.slot(angle, slot)[1] + shift
        left = jnp.where(left < 0, left + self.columns, left)
        left = jnp.where(left >= self.columns, left - self.columns, left)
        starts = []
        for i in range(3):
            start = (left & -LANE) + i * LANE
            start = jnp.where(start >= self.columns, start - self.columns, start)
            starts.append(pl.multiple_of(start, LANE))
        return starts, left & (LANE - 1)


def cut_body(absolute, facts_ref, slab_ref, *refs):
    blocks, out = refs[:-1], refs[-1]
    angles, slots, rows, width = out.shape
    facts = Facts(facts_ref, slab_ref, slots, len(blocks), blocks[0].shape[1])
    lane = lax.broadcasted_iota(jnp.int32, (rows, LANE), 1)
    for slot in range(slots):
        for angle in range(angles):

            @pl.when(facts.slot(angle, slot)[2] > 0)
            def _():
                total = [jnp.zeros((rows, LANE), jnp.float32)] * 2
                for k, block in enumerate(blocks):
                    layer = k if absolute else facts.layer(-k)
                    starts, inside = facts.columns_of(angle, slot, layer)
                    turned = [
                        pltpu.roll(block[:, pl.ds(start, LANE)].astype(jnp.float32), (LANE - inside) & (LANE - 1), 1)
                        for start in starts
                    ]
                    here = lane < LANE - inside
                    total = [t + jnp.where(here, turned[i], turned[i + 1]) for i, t in enumerate(total)]
                out[angle, slot] = jnp.concatenate(total, axis=1).astype(jnp.bfloat16)


def cut_windows(facts, blocks, angles, slots, width):
    out = jax.ShapeDtypeStruct((angles, slots, blocks[0].shape[0], width), jnp.bfloat16)
    return call(functools.partial(cut_body, False), [out], [], *facts, *blocks)[0]


def cut_rest(facts, blocks, done, which):
    angles, slots, rows, width = done.shape
    out = jax.ShapeDtypeStruct((angles, 2, slots, rows, width), jnp.bfloat16)

    def body(facts_ref, slab_ref, blocks, done, out):
        out[:, 1 - which] = done[...]
        cut_body(True, facts_ref, slab_ref, *(blocks.at[k] for k in range(blocks.shape[0])), out.at[:, which])

    return call(body, [out], [], *facts, blocks, done)[0]


def cos_sin(angle):
    turns = jnp.round(angle * 0.6366197723675814)
    rest = angle - turns * 1.5703125
    rest = rest - turns * 4.837512969970703e-4
    rest = rest - turns * 7.549789948768648e-8
    square = rest * rest
    sine = (-1.9515295891e-4 * square + 8.3321608736e-3) * square - 1.6666654611e-1
    sine = sine * square * rest + rest
    cosine = (2.443315711809948e-5 * square - 1.388731625493765e-3) * square + 4.166664568298827e-2
    cosine = cosine * square * square - 0.5 * square + 1.0
    quarter = turns.astype(jnp.int32)
    odd = (quarter & 1) == 1
    first, second = jnp.where(odd, sine, cosine), jnp.where(odd, cosine, sine)
    return (
        jnp.where(((quarter + 1) & 2) == 2, -first, first),
        jnp.where((quarter & 2) == 2, -second, second),
    )


def patch_body(row_ref, count_ref, windows, probe, patterns, wr_ref, wi_ref, own_out, next_out):
    angles, _, slots, rows, width = windows.shape
    f32, bf16 = jnp.float32, jnp.bfloat16
    blocks = angles // 2
    tall = 2 * blocks * rows
    for slot in range(slots):
        row = row_ref[slot]

        @pl.when(slot < count_ref[0])
        def _():
            pick = one_hot(width, tall, -row)
            window = []
            for part in range(2):
                held = [windows[2 * k + part, tile, slot] for tile in range(2) for k in range(blocks)]
                window.append(dot(pick, jnp.concatenate(held, axis=0)))
            phase, absorption = window
            magnitude = jnp.exp(-absorption)
            cosine, sine = cos_sin(phase)
            trans_real = magnitude * cosine
            trans_imag = magnitude * sine
            probe_real, probe_imag = probe[0], probe[1]
            wr, wi = wr_ref[...], wi_ref[...]
            wave_real = (probe_real * trans_real - probe_imag * trans_imag).astype(bf16)
            wave_imag = (probe_real * trans_imag + probe_imag * trans_real).astype(bf16)
            left_real = (dot(wr, wave_real) - dot(wi, wave_imag)).astype(bf16)
            left_imag = (dot(wr, wave_imag) + dot(wi, wave_real)).astype(bf16)
            far_real = dot(left_real, wr) - dot(left_imag, wi)
            far_imag = dot(left_real, wi) + dot(left_imag, wr)
            power = far_real * far_real + far_imag * far_imag + floor_square
            keeping = 1.0 - patterns[slot].astype(f32) * lax.rsqrt(power)
            resid_real = (far_real * keeping).astype(bf16)
            resid_imag = (far_imag * keeping).astype(bf16)
            back_real = (dot(wr, resid_real) + dot(wi, resid_imag)).astype(bf16)
            back_imag = (dot(wr, resid_imag) - dot(wi, resid_real)).astype(bf16)
            exit_real = dot(back_real, wr) + dot(back_imag, wi)
            exit_imag = dot(back_imag, wr) - dot(back_real, wi)
            mixed_real = probe_real * exit_real + probe_imag * exit_imag
            mixed_imag = probe_real * exit_imag - probe_imag * exit_real
            final_real = trans_real * mixed_real + trans_imag * mixed_imag
            final_imag = trans_real * mixed_imag - trans_imag * mixed_real
            put = one_hot(tall, width, row)
            for part, value in enumerate((final_imag, -final_real)):
                placed = dot(put, value.astype(bf16)).astype(bf16)
                for k in range(blocks):
                    own_out[2 * k + part, slot] = placed[k * rows : (k + 1) * rows]
                    below = placed[(blocks + k) * rows : (blocks + k + 1) * rows]
                    next_out[2 * (blocks - 1 - k) + part, slot] = below


def patch_gradients(slot_rows, count, windows, probe_wave, patterns, tables):
    angles, _, slots, rows, width = windows.shape
    out = jax.ShapeDtypeStruct((angles, slots, rows, width), jnp.bfloat16)
    return call(patch_body, [out, out], [], slot_rows, count, windows, probe_wave, patterns, *tables)


def place_body(facts_ref, slab_ref, windows, *refs):
    outs, total = refs[:-1], refs[-1]
    angles, slots, rows, width = windows.shape
    slabs = total.shape[0]
    facts = Facts(facts_ref, slab_ref, slots, slabs, total.shape[2])
    lane = lax.broadcasted_iota(jnp.int32, (rows, LANE), 1)
    total[...] = jnp.zeros_like(total)
    for slot in range(slots):
        for angle in range(angles):

            @pl.when(facts.slot(angle, slot)[2] > 0)
            def _():
                window = windows[angle, slot].astype(jnp.float32)
                for k in range(slabs):
                    layer = facts.layer(k) if len(outs) > 1 else k
                    starts, inside = facts.columns_of(angle, slot, layer)
                    first, second = (pltpu.roll(window[:, i * LANE : (i + 1) * LANE], inside, 1) for i in range(2))
                    there = lane < inside
                    total[k, :, pl.ds(starts[0], LANE)] += jnp.where(there, 0.0, first)
                    total[k, :, pl.ds(starts[1], LANE)] += jnp.where(there, first, second)
                    total[k, :, pl.ds(starts[2], LANE)] += jnp.where(there, second, 0.0)
    for k, out in enumerate(outs):
        out[...] = (total[k] if len(outs) > 1 else total[...]).astype(out.dtype)


def place_windows(facts, windows, slabs, columns, together=False):
    shape = (windows.shape[2], columns)
    outs = [jax.ShapeDtypeStruct(shape, jnp.bfloat16 if k else jnp.float32) for k in range(slabs)]
    if together:
        outs = [jax.ShapeDtypeStruct((slabs, *shape), jnp.bfloat16)]
    return call(place_body, outs, [pltpu.VMEM((slabs, *shape), jnp.float32)], *facts, windows)


def sum_body(*refs):
    *terms, out = refs
    total = sum(term[...].astype(jnp.float32) for term in terms).astype(out.dtype)
    for k in range(out.shape[0]):
        out[k] = total


def sum_copies(terms, copies):
    out = jax.ShapeDtypeStruct((copies, *terms[0].shape), jnp.bfloat16)
    return call(sum_body, [out], [], *terms)[0]


def step_body(part_ref, layer, gradient, *refs):
    out, made, sems = refs[-3:]
    part = part_ref[0]
    size = gradient.shape[0] // 4
    copies = []
    for n in range(4):
        rows = slice(n * size, (n + 1) * size)
        made[rows] = layer[part, rows].astype(jnp.float32) - step_size * gradient[rows].astype(jnp.float32)
        copies.append(
            pltpu.make_async_copy(made.at[pl.ds(n * size, size)], out.at[part, pl.ds(n * size, size)], sems.at[n])
        )
        copies[-1].start()
    for copy in copies:
        copy.wait()


def step(part, layer, gradient, *stepped):
    return pl.pallas_call(
        step_body,
        out_shape=jax.ShapeDtypeStruct(layer.shape, jnp.float32),
        in_specs=[pl.BlockSpec(memory_space=pltpu.SMEM), VMEM, VMEM]
        + [pl.BlockSpec(memory_space=pltpu.HBM)] * len(stepped),
        out_specs=pl.BlockSpec(memory_space=pltpu.HBM),
        scratch_shapes=[pltpu.VMEM(gradient.shape, jnp.float32), pltpu.SemaphoreType.DMA((4,))],
        input_output_aliases={3: 0} if stepped else {},
        compiler_params=pltpu.CompilerParams(vmem_limit_bytes=24 * 1024 * 1024),
    )(part.reshape(1).astype(jnp.int32), layer, gradient, *stepped)


def per_device(volume, probe_wave, amplitudes, offsets, column_starts, counts, angle_ids):
    layer = volume.reshape(volume.shape[0], *volume.shape[2:])
    tile_rows, columns = layer.shape[1:]
    width = amplitudes.shape[-1]
    slots = offsets.shape[3]
    angles, slabs, tiles = (lax.axis_size(axis) for axis in ("angle", "slab", "tile"))
    slab, angle = lax.axis_index("slab"), lax.axis_index("angle")
    f32, bf16 = jnp.float32, jnp.bfloat16
    tables = dft_tables(width)
    patterns = amplitudes.reshape(slots, width, width)

    core, place_z = angle % 2, angle // 2 % 4
    eight_groups = [[8 * f + i for i in range(8)] for f in range(angles // 8)]
    four_groups = [[8 * f + 2 * q + c for q in range(4)] for f in range(angles // 8) for c in range(2)]
    block_rows = tile_rows // 4

    def swap(value, by):
        return lax.ppermute(value, "angle", [(i, i ^ by) for i in range(angles)])

    def mirrored(value, by):
        pairs = [
            (a * tiles + t, (angles - 2 - (a - a % 2) + a % 2) * tiles + t + by)
            for a in range(angles)
            for t in range(tiles)
            if 0 <= t + by < tiles
        ]
        return lax.ppermute(value, ("angle", "tile"), pairs)

    def to_slab(value, by):
        return lax.ppermute(value, "slab", [(i, (i + by) % slabs) for i in range(slabs)])

    def to_eight(value):
        return lax.all_to_all(value, "angle", 0, 0, axis_index_groups=eight_groups, tiled=True)

    def to_four(value):
        return lax.all_to_all(value, "angle", 0, 0, axis_index_groups=four_groups, tiled=True)

    def to_slabs(value):
        return lax.all_to_all(value, "slab", 0, 0, tiled=True)

    def of_slabs(block):
        return [block] + [to_slab(block, k) for k in range(1, slabs)]

    def over_slabs(kept, *sent):
        return sum((to_slab(block, k + 1).astype(f32) for k, block in enumerate(sent)), kept)

    own_part = lax.dynamic_index_in_dim(layer, core, 0, keepdims=False)

    def rows_of(block):
        return lax.dynamic_slice(own_part, (block * block_rows, 0), (block_rows, columns))

    after = mirrored(rows_of(3 - place_z), -1)
    own = rows_of(place_z)

    slot_rows, count = offsets.reshape(slots), counts.reshape(1)
    line = jax.ShapeDtypeStruct((8, LANE), jnp.int32)
    meta = call(facts_body, [line], [], slot_rows, column_starts.reshape(slots), count, angle_ids)[0]
    eight = to_eight(meta)
    facts = (eight, slab.reshape(1).astype(jnp.int32))
    own = of_slabs(own)
    after, own = lax.optimization_barrier((after, own))
    own = cut_windows(facts, own, 8, slots, width)
    after = to_slabs(jnp.broadcast_to(after, (slabs, *after.shape)))
    after, own = lax.optimization_barrier((after, own))
    windows = to_eight(cut_rest(facts, after, own, 1))

    own, after = patch_gradients(slot_rows, count, windows, probe_wave, patterns, tables)
    after, own = lax.optimization_barrier((to_eight(after), own))
    own = to_eight(own)
    spill = mirrored(over_slabs(*place_windows(facts, after, slabs, columns)).astype(bf16), 1)
    own = to_slabs(place_windows(facts, own, slabs, columns, together=True)[0])
    own = jnp.sum(own.astype(f32), axis=0)

    total = lax.optimization_barrier((own + spill.astype(f32)).astype(bf16))
    total = to_four(sum_copies([total, swap(total, 8)], 4)).reshape(tile_rows, columns)
    new = step(core, layer, total)
    return step(1 - core, layer, swap(total, 1), new).reshape(volume.shape)


def solution(mesh):
    in_specs = (
        P(None, "slab", "tile", None),
        P(),
        P("angle", "tile", "slab", None, None, None),
        P("angle", "tile", "slab", None),
        P("angle", "tile", "slab", None),
        P("angle", "tile", "slab"),
        P("angle"),
    )
    out_specs = P(None, "slab", "tile", None)
    return jax.shard_map(
        per_device, mesh=mesh, in_specs=in_specs, out_specs=out_specs, check_vma=False
    )
```

```python
import functools

import jax
import jax.numpy as jnp
import ml_dtypes
import numpy as np
from jax import lax
from jax.experimental import pallas as pl
from jax.experimental.pallas import tpu as pltpu
from jax.sharding import PartitionSpec as P

angle_center = 600
shear_divisor = 64
step_size = 0.03
floor_square = 0.25

LANE = 128


def dft_tables(plane_width):
    index_line = np.arange(plane_width, dtype=np.int32)
    product_mod = np.mod(index_line[:, None] * index_line[None, :], plane_width)
    phase_table = product_mod.astype(np.float32) * np.float32(2.0 * 3.141592653589793 / plane_width)
    scale_factor = np.float32(plane_width ** (-0.5))
    table_real = (np.cos(phase_table) * scale_factor).astype(ml_dtypes.bfloat16)
    table_imag = (-np.sin(phase_table) * scale_factor).astype(ml_dtypes.bfloat16)
    return table_real, table_imag


def dot(left, right):
    return jnp.dot(left, right, preferred_element_type=jnp.float32)


def one_hot(rows, columns, down):
    row = lax.broadcasted_iota(jnp.int32, (rows, columns), 0)
    column = lax.broadcasted_iota(jnp.int32, (rows, columns), 1)
    return (row - column == down).astype(jnp.float32).astype(jnp.bfloat16)


VMEM = pl.BlockSpec(memory_space=pltpu.VMEM)


def call(body, out_shape, scratch, *args):
    smem = pl.BlockSpec(memory_space=pltpu.SMEM)
    return pl.pallas_call(
        body,
        out_shape=out_shape,
        in_specs=[smem if x.dtype == jnp.int32 else VMEM for x in args],
        out_specs=[VMEM] * len(out_shape),
        scratch_shapes=scratch,
        compiler_params=pltpu.CompilerParams(vmem_limit_bytes=24 * 1024 * 1024),
    )(*args)


def facts_body(rows_ref, columns_ref, count_ref, index_ref, out):
    values = []
    for slot in range(rows_ref.shape[0]):
        values += [rows_ref[slot], columns_ref[slot], (slot < count_ref[0]).astype(jnp.int32)]
    lane = lax.broadcasted_iota(jnp.int32, out.shape, 1)
    line = jnp.zeros(out.shape, jnp.int32)
    for n, value in enumerate(values + [index_ref[0]]):
        line = jnp.where(lane == n, value, line)
    out[...] = line


class Facts:
    def __init__(self, ref, slab_ref, slots, slabs, columns):
        self.ref, self.slab, self.slots, self.slabs, self.columns = ref, slab_ref[0], slots, slabs, columns

    def slot(self, angle, slot):
        return tuple(self.ref[angle, 3 * slot + i] for i in range(3))

    def layer(self, step):
        layer = self.slab + step
        layer = jnp.where(layer < 0, layer + self.slabs, layer)
        return jnp.where(layer >= self.slabs, layer - self.slabs, layer)

    def columns_of(self, angle, slot, layer):
        index = self.ref[angle, 3 * self.slots]
        shift = ((index - angle_center) * (layer - self.slabs // 2)) >> (shear_divisor.bit_length() - 1)
        left = self.slot(angle, slot)[1] + shift
        left = jnp.where(left < 0, left + self.columns, left)
        left = jnp.where(left >= self.columns, left - self.columns, left)
        starts = []
        for i in range(3):
            start = (left & -LANE) + i * LANE
            start = jnp.where(start >= self.columns, start - self.columns, start)
            starts.append(pl.multiple_of(start, LANE))
        return starts, left & (LANE - 1)


def cut_body(facts_ref, slab_ref, *refs):
    blocks, out = refs[:-1], refs[-1]
    angles, slots, rows, width = out.shape
    facts = Facts(facts_ref, slab_ref, slots, len(blocks), blocks[0].shape[1])
    lane = lax.broadcasted_iota(jnp.int32, (rows, LANE), 1)
    for slot in range(slots):
        for angle in range(angles):

            @pl.when(facts.slot(angle, slot)[2] > 0)
            def _():
                total = [jnp.zeros((rows, LANE), jnp.float32)] * 2
                for k, block in enumerate(blocks):
                    starts, inside = facts.columns_of(angle, slot, facts.layer(-k))
                    turned = [
                        pltpu.roll(block[:, pl.ds(start, LANE)].astype(jnp.float32), (LANE - inside) & (LANE - 1), 1)
                        for start in starts
                    ]
                    here = lane < LANE - inside
                    total = [t + jnp.where(here, turned[i], turned[i + 1]) for i, t in enumerate(total)]
                out[angle, slot] = jnp.concatenate(total, axis=1).astype(jnp.bfloat16)


def cut_windows(facts, blocks, angles, slots, width):
    out = jax.ShapeDtypeStruct((angles, slots, blocks[0].shape[0], width), jnp.bfloat16)
    return call(cut_body, [out], [], *facts, *blocks)[0]


def cos_sin(angle):
    turns = jnp.round(angle * 0.6366197723675814)
    rest = angle - turns * 1.5703125
    rest = rest - turns * 4.837512969970703e-4
    rest = rest - turns * 7.549789948768648e-8
    square = rest * rest
    sine = (-1.9515295891e-4 * square + 8.3321608736e-3) * square - 1.6666654611e-1
    sine = sine * square * rest + rest
    cosine = (2.443315711809948e-5 * square - 1.388731625493765e-3) * square + 4.166664568298827e-2
    cosine = cosine * square * square - 0.5 * square + 1.0
    quarter = turns.astype(jnp.int32)
    odd = (quarter & 1) == 1
    first, second = jnp.where(odd, sine, cosine), jnp.where(odd, cosine, sine)
    return (
        jnp.where(((quarter + 1) & 2) == 2, -first, first),
        jnp.where((quarter & 2) == 2, -second, second),
    )


def patch_body(row_ref, count_ref, own_in, next_in, probe, patterns, wr_ref, wi_ref, own_out, next_out):
    angles, slots, rows, width = own_in.shape
    f32, bf16 = jnp.float32, jnp.bfloat16
    blocks = angles // 2
    tall = 2 * blocks * rows
    for slot in range(slots):
        row = row_ref[slot]

        @pl.when(slot < count_ref[0])
        def _():
            pick = one_hot(width, tall, -row)
            window = []
            for part in range(2):
                held = [ref[2 * k + part, slot] for ref in (own_in, next_in) for k in range(blocks)]
                window.append(dot(pick, jnp.concatenate(held, axis=0)))
            phase, absorption = window
            magnitude = jnp.exp(-absorption)
            cosine, sine = cos_sin(phase)
            trans_real = magnitude * cosine
            trans_imag = magnitude * sine
            probe_real, probe_imag = probe[0], probe[1]
            wr, wi = wr_ref[...], wi_ref[...]
            wave_real = (probe_real * trans_real - probe_imag * trans_imag).astype(bf16)
            wave_imag = (probe_real * trans_imag + probe_imag * trans_real).astype(bf16)
            left_real = (dot(wr, wave_real) - dot(wi, wave_imag)).astype(bf16)
            left_imag = (dot(wr, wave_imag) + dot(wi, wave_real)).astype(bf16)
            far_real = dot(left_real, wr) - dot(left_imag, wi)
            far_imag = dot(left_real, wi) + dot(left_imag, wr)
            power = far_real * far_real + far_imag * far_imag + floor_square
            keeping = 1.0 - patterns[slot].astype(f32) * lax.rsqrt(power)
            resid_real = (far_real * keeping).astype(bf16)
            resid_imag = (far_imag * keeping).astype(bf16)
            back_real = (dot(wr, resid_real) + dot(wi, resid_imag)).astype(bf16)
            back_imag = (dot(wr, resid_imag) - dot(wi, resid_real)).astype(bf16)
            exit_real = dot(back_real, wr) + dot(back_imag, wi)
            exit_imag = dot(back_imag, wr) - dot(back_real, wi)
            mixed_real = probe_real * exit_real + probe_imag * exit_imag
            mixed_imag = probe_real * exit_imag - probe_imag * exit_real
            final_real = trans_real * mixed_real + trans_imag * mixed_imag
            final_imag = trans_real * mixed_imag - trans_imag * mixed_real
            put = one_hot(tall, width, row)
            for part, value in enumerate((final_imag, -final_real)):
                placed = dot(put, value.astype(bf16)).astype(bf16)
                for k in range(blocks):
                    own_out[2 * k + part, slot] = placed[k * rows : (k + 1) * rows]
                    below = placed[(blocks + k) * rows : (blocks + k + 1) * rows]
                    next_out[2 * (blocks - 1 - k) + part, slot] = below


def patch_gradients(slot_rows, count, own, after, probe_wave, patterns, tables):
    out = jax.ShapeDtypeStruct(own.shape, jnp.bfloat16)
    return call(patch_body, [out, out], [], slot_rows, count, own, after, probe_wave, patterns, *tables)


def place_body(facts_ref, slab_ref, windows, *refs):
    outs, total = refs[:-1], refs[-1]
    angles, slots, rows, width = windows.shape
    slabs = total.shape[0]
    facts = Facts(facts_ref, slab_ref, slots, slabs, total.shape[2])
    lane = lax.broadcasted_iota(jnp.int32, (rows, LANE), 1)
    total[...] = jnp.zeros_like(total)
    for slot in range(slots):
        for angle in range(angles):

            @pl.when(facts.slot(angle, slot)[2] > 0)
            def _():
                window = windows[angle, slot].astype(jnp.float32)
                for k in range(slabs):
                    layer = facts.layer(k) if len(outs) > 1 else k
                    starts, inside = facts.columns_of(angle, slot, layer)
                    first, second = (pltpu.roll(window[:, i * LANE : (i + 1) * LANE], inside, 1) for i in range(2))
                    there = lane < inside
                    total[k, :, pl.ds(starts[0], LANE)] += jnp.where(there, 0.0, first)
                    total[k, :, pl.ds(starts[1], LANE)] += jnp.where(there, first, second)
                    total[k, :, pl.ds(starts[2], LANE)] += jnp.where(there, second, 0.0)
    for k, out in enumerate(outs):
        out[...] = (total[k] if len(outs) > 1 else total[...]).astype(out.dtype)


def place_windows(facts, windows, slabs, columns, together=False):
    shape = (windows.shape[2], columns)
    outs = [jax.ShapeDtypeStruct(shape, jnp.bfloat16 if k else jnp.float32) for k in range(slabs)]
    if together:
        outs = [jax.ShapeDtypeStruct((slabs, *shape), jnp.bfloat16)]
    return call(place_body, outs, [pltpu.VMEM((slabs, *shape), jnp.float32)], *facts, windows)


def sum_body(*refs):
    *terms, out = refs
    total = sum(term[...].astype(jnp.float32) for term in terms).astype(out.dtype)
    for k in range(out.shape[0]):
        out[k] = total


def sum_copies(terms, copies):
    out = jax.ShapeDtypeStruct((copies, *terms[0].shape), jnp.bfloat16)
    return call(sum_body, [out], [], *terms)[0]


def step_body(part_ref, layer, gradient, *refs):
    out, made, sems = refs[-3:]
    part = part_ref[0]
    size = gradient.shape[0] // 4
    copies = []
    for n in range(4):
        rows = slice(n * size, (n + 1) * size)
        made[rows] = layer[part, rows].astype(jnp.float32) - step_size * gradient[rows].astype(jnp.float32)
        copies.append(
            pltpu.make_async_copy(made.at[pl.ds(n * size, size)], out.at[part, pl.ds(n * size, size)], sems.at[n])
        )
        copies[-1].start()
    for copy in copies:
        copy.wait()


def step(part, layer, gradient, *stepped):
    return pl.pallas_call(
        step_body,
        out_shape=jax.ShapeDtypeStruct(layer.shape, jnp.float32),
        in_specs=[pl.BlockSpec(memory_space=pltpu.SMEM), VMEM, VMEM]
        + [pl.BlockSpec(memory_space=pltpu.HBM)] * len(stepped),
        out_specs=pl.BlockSpec(memory_space=pltpu.HBM),
        scratch_shapes=[pltpu.VMEM(gradient.shape, jnp.float32), pltpu.SemaphoreType.DMA((4,))],
        input_output_aliases={3: 0} if stepped else {},
        compiler_params=pltpu.CompilerParams(vmem_limit_bytes=24 * 1024 * 1024),
    )(part.reshape(1).astype(jnp.int32), layer, gradient, *stepped)


def per_device(volume, probe_wave, amplitudes, offsets, column_starts, counts, angle_ids):
    layer = volume.reshape(volume.shape[0], *volume.shape[2:])
    tile_rows, columns = layer.shape[1:]
    width = amplitudes.shape[-1]
    slots = offsets.shape[3]
    angles, slabs, tiles = (lax.axis_size(axis) for axis in ("angle", "slab", "tile"))
    slab, angle = lax.axis_index("slab"), lax.axis_index("angle")
    f32, bf16 = jnp.float32, jnp.bfloat16
    tables = dft_tables(width)
    patterns = amplitudes.reshape(slots, width, width)

    core, place_z = angle % 2, angle // 2 % 4
    eight_groups = [[8 * f + i for i in range(8)] for f in range(angles // 8)]
    four_groups = [[8 * f + 2 * q + c for q in range(4)] for f in range(angles // 8) for c in range(2)]
    block_rows = tile_rows // 4

    def swap(value, by):
        return lax.ppermute(value, "angle", [(i, i ^ by) for i in range(angles)])

    def mirrored(value, by):
        pairs = [
            (a * tiles + t, (angles - 2 - (a - a % 2) + a % 2) * tiles + t + by)
            for a in range(angles)
            for t in range(tiles)
            if 0 <= t + by < tiles
        ]
        return lax.ppermute(value, ("angle", "tile"), pairs)

    def to_slab(value, by):
        return lax.ppermute(value, "slab", [(i, (i + by) % slabs) for i in range(slabs)])

    def to_eight(value):
        return lax.all_to_all(value, "angle", 0, 0, axis_index_groups=eight_groups, tiled=True)

    def to_four(value):
        return lax.all_to_all(value, "angle", 0, 0, axis_index_groups=four_groups, tiled=True)

    def to_slabs(value):
        return lax.all_to_all(value, "slab", 0, 0, tiled=True)

    def of_slabs(block):
        return [block] + [to_slab(block, k) for k in range(1, slabs)]

    def over_slabs(kept, *sent):
        return sum((to_slab(block, k + 1).astype(f32) for k, block in enumerate(sent)), kept)

    own_part = lax.dynamic_index_in_dim(layer, core, 0, keepdims=False)

    def rows_of(block):
        return lax.dynamic_slice(own_part, (block * block_rows, 0), (block_rows, columns))

    after = mirrored(rows_of(3 - place_z), -1)
    own = rows_of(place_z)

    slot_rows, count = offsets.reshape(slots), counts.reshape(1)
    line = jax.ShapeDtypeStruct((8, LANE), jnp.int32)
    meta = call(facts_body, [line], [], slot_rows, column_starts.reshape(slots), count, angle_ids)[0]
    eight = to_eight(meta)
    facts = (eight, slab.reshape(1).astype(jnp.int32))
    own = of_slabs(own)
    after, own = lax.optimization_barrier((after, own))
    own = cut_windows(facts, own, 8, slots, width)
    own, after = to_eight(own), of_slabs(after)
    after, own = lax.optimization_barrier((after, own))
    after = to_eight(cut_windows(facts, after, 8, slots, width))

    own, after = patch_gradients(slot_rows, count, own, after, probe_wave, patterns, tables)
    after, own = lax.optimization_barrier((to_eight(after), own))
    own = to_eight(own)
    spill = mirrored(over_slabs(*place_windows(facts, after, slabs, columns)).astype(bf16), 1)
    own = to_slabs(place_windows(facts, own, slabs, columns, together=True)[0])
    own = jnp.sum(own.astype(f32), axis=0)

    total = lax.optimization_barrier((own + spill.astype(f32)).astype(bf16))
    total = to_four(sum_copies([total, swap(total, 8)], 4)).reshape(tile_rows, columns)
    new = step(core, layer, total)
    return step(1 - core, layer, swap(total, 1), new).reshape(volume.shape)


def solution(mesh):
    in_specs = (
        P(None, "slab", "tile", None),
        P(),
        P("angle", "tile", "slab", None, None, None),
        P("angle", "tile", "slab", None),
        P("angle", "tile", "slab", None),
        P("angle", "tile", "slab"),
        P("angle"),
    )
    out_specs = P(None, "slab", "tile", None)
    return jax.shard_map(
        per_device, mesh=mesh, in_specs=in_specs, out_specs=out_specs, check_vma=False
    )
```

```python
import functools

import jax
import jax.numpy as jnp
import ml_dtypes
import numpy as np
from jax import lax
from jax.experimental import pallas as pl
from jax.experimental.pallas import tpu as pltpu
from jax.sharding import PartitionSpec as P

angle_center = 600
shear_divisor = 64
step_size = 0.03
floor_square = 0.25

LANE = 128


def dft_tables(plane_width):
    index_line = np.arange(plane_width, dtype=np.int32)
    product_mod = np.mod(index_line[:, None] * index_line[None, :], plane_width)
    phase_table = product_mod.astype(np.float32) * np.float32(2.0 * 3.141592653589793 / plane_width)
    scale_factor = np.float32(plane_width ** (-0.5))
    table_real = (np.cos(phase_table) * scale_factor).astype(ml_dtypes.bfloat16)
    table_imag = (-np.sin(phase_table) * scale_factor).astype(ml_dtypes.bfloat16)
    return table_real, table_imag


def dot(left, right):
    return jnp.dot(left, right, preferred_element_type=jnp.float32)


def one_hot(rows, columns, down):
    row = lax.broadcasted_iota(jnp.int32, (rows, columns), 0)
    column = lax.broadcasted_iota(jnp.int32, (rows, columns), 1)
    return (row - column == down).astype(jnp.float32).astype(jnp.bfloat16)


VMEM = pl.BlockSpec(memory_space=pltpu.VMEM)


def call(body, out_shape, scratch, *args):
    smem = pl.BlockSpec(memory_space=pltpu.SMEM)
    return pl.pallas_call(
        body,
        out_shape=out_shape,
        in_specs=[smem if x.dtype == jnp.int32 else VMEM for x in args],
        out_specs=[VMEM] * len(out_shape),
        scratch_shapes=scratch,
        compiler_params=pltpu.CompilerParams(vmem_limit_bytes=24 * 1024 * 1024),
    )(*args)


def facts_body(rows_ref, columns_ref, count_ref, index_ref, out):
    values = []
    for slot in range(rows_ref.shape[0]):
        values += [rows_ref[slot], columns_ref[slot], (slot < count_ref[0]).astype(jnp.int32)]
    lane = lax.broadcasted_iota(jnp.int32, out.shape, 1)
    line = jnp.zeros(out.shape, jnp.int32)
    for n, value in enumerate(values + [index_ref[0]]):
        line = jnp.where(lane == n, value, line)
    out[...] = line


class Facts:
    def __init__(self, ref, slab_ref, slots, slabs, columns):
        self.ref, self.slab, self.slots, self.slabs, self.columns = ref, slab_ref[0], slots, slabs, columns

    def slot(self, angle, slot):
        return tuple(self.ref[angle, 3 * slot + i] for i in range(3))

    def layer(self, step):
        layer = self.slab + step
        layer = jnp.where(layer < 0, layer + self.slabs, layer)
        return jnp.where(layer >= self.slabs, layer - self.slabs, layer)

    def columns_of(self, angle, slot, layer):
        index = self.ref[angle, 3 * self.slots]
        shift = ((index - angle_center) * (layer - self.slabs // 2)) >> (shear_divisor.bit_length() - 1)
        left = self.slot(angle, slot)[1] + shift
        left = jnp.where(left < 0, left + self.columns, left)
        left = jnp.where(left >= self.columns, left - self.columns, left)
        starts = []
        for i in range(3):
            start = (left & -LANE) + i * LANE
            start = jnp.where(start >= self.columns, start - self.columns, start)
            starts.append(pl.multiple_of(start, LANE))
        return starts, left & (LANE - 1)


def cut_body(facts_ref, slab_ref, *refs):
    blocks, out = refs[:-1], refs[-1]
    angles, slots, rows, width = out.shape
    facts = Facts(facts_ref, slab_ref, slots, len(blocks), blocks[0].shape[1])
    lane = lax.broadcasted_iota(jnp.int32, (rows, LANE), 1)
    for slot in range(slots):
        for angle in range(angles):

            @pl.when(facts.slot(angle, slot)[2] > 0)
            def _():
                total = [jnp.zeros((rows, LANE), jnp.float32)] * 2
                for k, block in enumerate(blocks):
                    starts, inside = facts.columns_of(angle, slot, facts.layer(-k))
                    turned = [
                        pltpu.roll(block[:, pl.ds(start, LANE)].astype(jnp.float32), (LANE - inside) & (LANE - 1), 1)
                        for start in starts
                    ]
                    here = lane < LANE - inside
                    total = [t + jnp.where(here, turned[i], turned[i + 1]) for i, t in enumerate(total)]
                out[angle, slot] = jnp.concatenate(total, axis=1).astype(jnp.bfloat16)


def cut_windows(facts, blocks, angles, slots, width):
    out = jax.ShapeDtypeStruct((angles, slots, blocks[0].shape[0], width), jnp.bfloat16)
    return call(cut_body, [out], [], *facts, *blocks)[0]


def cut_rest(facts, blocks, done, which):
    angles, slots, rows, width = done.shape
    out = jax.ShapeDtypeStruct((angles, 2, slots, rows, width), jnp.bfloat16)

    def body(facts_ref, slab_ref, *refs):
        *blocks, done, out = refs
        out[:, 1 - which] = done[...]
        cut_body(facts_ref, slab_ref, *blocks, out.at[:, which])

    return call(body, [out], [], *facts, *blocks, done)[0]


def cos_sin(angle):
    turns = jnp.round(angle * 0.6366197723675814)
    rest = angle - turns * 1.5703125
    rest = rest - turns * 4.837512969970703e-4
    rest = rest - turns * 7.549789948768648e-8
    square = rest * rest
    sine = (-1.9515295891e-4 * square + 8.3321608736e-3) * square - 1.6666654611e-1
    sine = sine * square * rest + rest
    cosine = (2.443315711809948e-5 * square - 1.388731625493765e-3) * square + 4.166664568298827e-2
    cosine = cosine * square * square - 0.5 * square + 1.0
    quarter = turns.astype(jnp.int32)
    odd = (quarter & 1) == 1
    first, second = jnp.where(odd, sine, cosine), jnp.where(odd, cosine, sine)
    return (
        jnp.where(((quarter + 1) & 2) == 2, -first, first),
        jnp.where((quarter & 2) == 2, -second, second),
    )


def patch_body(row_ref, count_ref, windows, probe, patterns, wr_ref, wi_ref, own_out, next_out):
    angles, _, slots, rows, width = windows.shape
    f32, bf16 = jnp.float32, jnp.bfloat16
    blocks = angles // 2
    tall = 2 * blocks * rows
    for slot in range(slots):
        row = row_ref[slot]

        @pl.when(slot < count_ref[0])
        def _():
            pick = one_hot(width, tall, -row)
            window = []
            for part in range(2):
                held = [windows[2 * k + part, tile, slot] for tile in range(2) for k in range(blocks)]
                window.append(dot(pick, jnp.concatenate(held, axis=0)))
            phase, absorption = window
            magnitude = jnp.exp(-absorption)
            cosine, sine = cos_sin(phase)
            trans_real = magnitude * cosine
            trans_imag = magnitude * sine
            probe_real, probe_imag = probe[0], probe[1]
            wr, wi = wr_ref[...], wi_ref[...]
            wave_real = (probe_real * trans_real - probe_imag * trans_imag).astype(bf16)
            wave_imag = (probe_real * trans_imag + probe_imag * trans_real).astype(bf16)
            left_real = (dot(wr, wave_real) - dot(wi, wave_imag)).astype(bf16)
            left_imag = (dot(wr, wave_imag) + dot(wi, wave_real)).astype(bf16)
            far_real = dot(left_real, wr) - dot(left_imag, wi)
            far_imag = dot(left_real, wi) + dot(left_imag, wr)
            power = far_real * far_real + far_imag * far_imag + floor_square
            keeping = 1.0 - patterns[slot].astype(f32) * lax.rsqrt(power)
            resid_real = (far_real * keeping).astype(bf16)
            resid_imag = (far_imag * keeping).astype(bf16)
            back_real = (dot(wr, resid_real) + dot(wi, resid_imag)).astype(bf16)
            back_imag = (dot(wr, resid_imag) - dot(wi, resid_real)).astype(bf16)
            exit_real = dot(back_real, wr) + dot(back_imag, wi)
            exit_imag = dot(back_imag, wr) - dot(back_real, wi)
            mixed_real = probe_real * exit_real + probe_imag * exit_imag
            mixed_imag = probe_real * exit_imag - probe_imag * exit_real
            final_real = trans_real * mixed_real + trans_imag * mixed_imag
            final_imag = trans_real * mixed_imag - trans_imag * mixed_real
            put = one_hot(tall, width, row)
            for part, value in enumerate((final_imag, -final_real)):
                placed = dot(put, value.astype(bf16)).astype(bf16)
                for k in range(blocks):
                    own_out[2 * k + part, slot] = placed[k * rows : (k + 1) * rows]
                    below = placed[(blocks + k) * rows : (blocks + k + 1) * rows]
                    next_out[2 * (blocks - 1 - k) + part, slot] = below


def patch_gradients(slot_rows, count, windows, probe_wave, patterns, tables):
    angles, _, slots, rows, width = windows.shape
    out = jax.ShapeDtypeStruct((angles, slots, rows, width), jnp.bfloat16)
    return call(patch_body, [out, out], [], slot_rows, count, windows, probe_wave, patterns, *tables)


def place_body(facts_ref, slab_ref, windows, *refs):
    outs, total = refs[:-1], refs[-1]
    angles, slots, rows, width = windows.shape
    slabs = total.shape[0]
    facts = Facts(facts_ref, slab_ref, slots, slabs, total.shape[2])
    lane = lax.broadcasted_iota(jnp.int32, (rows, LANE), 1)
    total[...] = jnp.zeros_like(total)
    for slot in range(slots):
        for angle in range(angles):

            @pl.when(facts.slot(angle, slot)[2] > 0)
            def _():
                window = windows[angle, slot].astype(jnp.float32)
                for k in range(slabs):
                    layer = facts.layer(k) if len(outs) > 1 else k
                    starts, inside = facts.columns_of(angle, slot, layer)
                    first, second = (pltpu.roll(window[:, i * LANE : (i + 1) * LANE], inside, 1) for i in range(2))
                    there = lane < inside
                    total[k, :, pl.ds(starts[0], LANE)] += jnp.where(there, 0.0, first)
                    total[k, :, pl.ds(starts[1], LANE)] += jnp.where(there, first, second)
                    total[k, :, pl.ds(starts[2], LANE)] += jnp.where(there, second, 0.0)
    for k, out in enumerate(outs):
        out[...] = (total[k] if len(outs) > 1 else total[...]).astype(out.dtype)


def place_windows(facts, windows, slabs, columns, together=False):
    shape = (windows.shape[2], columns)
    outs = [jax.ShapeDtypeStruct(shape, jnp.bfloat16 if k else jnp.float32) for k in range(slabs)]
    if together:
        outs = [jax.ShapeDtypeStruct((slabs, *shape), jnp.bfloat16)]
    return call(place_body, outs, [pltpu.VMEM((slabs, *shape), jnp.float32)], *facts, windows)


def sum_body(*refs):
    *terms, out = refs
    total = sum(term[...].astype(jnp.float32) for term in terms).astype(out.dtype)
    for k in range(out.shape[0]):
        out[k] = total


def sum_copies(terms, copies):
    out = jax.ShapeDtypeStruct((copies, *terms[0].shape), jnp.bfloat16)
    return call(sum_body, [out], [], *terms)[0]


def step_body(part_ref, layer, gradient, *refs):
    out, made, sems = refs[-3:]
    part = part_ref[0]
    size = gradient.shape[0] // 4
    copies = []
    for n in range(4):
        rows = slice(n * size, (n + 1) * size)
        made[rows] = layer[part, rows].astype(jnp.float32) - step_size * gradient[rows].astype(jnp.float32)
        copies.append(
            pltpu.make_async_copy(made.at[pl.ds(n * size, size)], out.at[part, pl.ds(n * size, size)], sems.at[n])
        )
        copies[-1].start()
    for copy in copies:
        copy.wait()


def step(part, layer, gradient, *stepped):
    return pl.pallas_call(
        step_body,
        out_shape=jax.ShapeDtypeStruct(layer.shape, jnp.float32),
        in_specs=[pl.BlockSpec(memory_space=pltpu.SMEM), VMEM, VMEM]
        + [pl.BlockSpec(memory_space=pltpu.HBM)] * len(stepped),
        out_specs=pl.BlockSpec(memory_space=pltpu.HBM),
        scratch_shapes=[pltpu.VMEM(gradient.shape, jnp.float32), pltpu.SemaphoreType.DMA((4,))],
        input_output_aliases={3: 0} if stepped else {},
        compiler_params=pltpu.CompilerParams(vmem_limit_bytes=24 * 1024 * 1024),
    )(part.reshape(1).astype(jnp.int32), layer, gradient, *stepped)


def per_device(volume, probe_wave, amplitudes, offsets, column_starts, counts, angle_ids):
    layer = volume.reshape(volume.shape[0], *volume.shape[2:])
    tile_rows, columns = layer.shape[1:]
    width = amplitudes.shape[-1]
    slots = offsets.shape[3]
    angles, slabs, tiles = (lax.axis_size(axis) for axis in ("angle", "slab", "tile"))
    slab, angle = lax.axis_index("slab"), lax.axis_index("angle")
    f32, bf16 = jnp.float32, jnp.bfloat16
    tables = dft_tables(width)
    patterns = amplitudes.reshape(slots, width, width)

    core, place_z = angle % 2, angle // 2 % 4
    eight_groups = [[8 * f + i for i in range(8)] for f in range(angles // 8)]
    four_groups = [[8 * f + 2 * q + c for q in range(4)] for f in range(angles // 8) for c in range(2)]
    block_rows = tile_rows // 4

    def swap(value, by):
        return lax.ppermute(value, "angle", [(i, i ^ by) for i in range(angles)])

    def mirrored(value, by):
        pairs = [
            (a * tiles + t, (angles - 2 - (a - a % 2) + a % 2) * tiles + t + by)
            for a in range(angles)
            for t in range(tiles)
            if 0 <= t + by < tiles
        ]
        return lax.ppermute(value, ("angle", "tile"), pairs)

    def to_slab(value, by):
        return lax.ppermute(value, "slab", [(i, (i + by) % slabs) for i in range(slabs)])

    def to_eight(value):
        return lax.all_to_all(value, "angle", 0, 0, axis_index_groups=eight_groups, tiled=True)

    def to_four(value):
        return lax.all_to_all(value, "angle", 0, 0, axis_index_groups=four_groups, tiled=True)

    def to_slabs(value):
        return lax.all_to_all(value, "slab", 0, 0, tiled=True)

    def of_slabs(block):
        return [block] + [to_slab(block, k) for k in range(1, slabs)]

    def over_slabs(kept, *sent):
        return sum((to_slab(block, k + 1).astype(f32) for k, block in enumerate(sent)), kept)

    own_part = lax.dynamic_index_in_dim(layer, core, 0, keepdims=False)

    def rows_of(block):
        return lax.dynamic_slice(own_part, (block * block_rows, 0), (block_rows, columns))

    after = mirrored(rows_of(3 - place_z), -1)
    own = rows_of(place_z)

    slot_rows, count = offsets.reshape(slots), counts.reshape(1)
    line = jax.ShapeDtypeStruct((8, LANE), jnp.int32)
    meta = call(facts_body, [line], [], slot_rows, column_starts.reshape(slots), count, angle_ids)[0]
    eight = to_eight(meta)
    facts = (eight, slab.reshape(1).astype(jnp.int32))
    own = of_slabs(own)
    after, own, facts = lax.optimization_barrier((after, own, facts))
    own, after = cut_windows(facts, own, 8, slots, width), of_slabs(after)
    after, own = lax.optimization_barrier((after, own))
    windows = to_eight(cut_rest(facts, after, own, 1))

    own, after = patch_gradients(slot_rows, count, windows, probe_wave, patterns, tables)
    after, own = lax.optimization_barrier((to_eight(after), own))
    own = to_eight(own)
    spill = mirrored(over_slabs(*place_windows(facts, after, slabs, columns)).astype(bf16), 1)
    own = to_slabs(place_windows(facts, own, slabs, columns, together=True)[0])
    own = jnp.sum(own.astype(f32), axis=0)

    total = lax.optimization_barrier((own + spill.astype(f32)).astype(bf16))
    total = to_four(sum_copies([total, swap(total, 8)], 4)).reshape(tile_rows, columns)
    new = step(core, layer, total)
    return step(1 - core, layer, swap(total, 1), new).reshape(volume.shape)


def solution(mesh):
    in_specs = (
        P(None, "slab", "tile", None),
        P(),
        P("angle", "tile", "slab", None, None, None),
        P("angle", "tile", "slab", None),
        P("angle", "tile", "slab", None),
        P("angle", "tile", "slab"),
        P("angle"),
    )
    out_specs = P(None, "slab", "tile", None)
    return jax.shard_map(
        per_device, mesh=mesh, in_specs=in_specs, out_specs=out_specs, check_vma=False
    )
```

```python
import functools

import jax
import jax.numpy as jnp
import ml_dtypes
import numpy as np
from jax import lax
from jax.experimental import pallas as pl
from jax.experimental.pallas import tpu as pltpu
from jax.sharding import PartitionSpec as P

angle_center = 600
shear_divisor = 64
step_size = 0.03
floor_square = 0.25

LANE = 128


def dft_tables(plane_width):
    index_line = np.arange(plane_width, dtype=np.int32)
    product_mod = np.mod(index_line[:, None] * index_line[None, :], plane_width)
    phase_table = product_mod.astype(np.float32) * np.float32(2.0 * 3.141592653589793 / plane_width)
    scale_factor = np.float32(plane_width ** (-0.5))
    table_real = (np.cos(phase_table) * scale_factor).astype(ml_dtypes.bfloat16)
    table_imag = (-np.sin(phase_table) * scale_factor).astype(ml_dtypes.bfloat16)
    return table_real, table_imag


def dot(left, right):
    return jnp.dot(left, right, preferred_element_type=jnp.float32)


def one_hot(rows, columns, down):
    row = lax.broadcasted_iota(jnp.int32, (rows, columns), 0)
    column = lax.broadcasted_iota(jnp.int32, (rows, columns), 1)
    return (row - column == down).astype(jnp.float32).astype(jnp.bfloat16)


VMEM = pl.BlockSpec(memory_space=pltpu.VMEM)


def call(body, out_shape, scratch, *args):
    smem = pl.BlockSpec(memory_space=pltpu.SMEM)
    return pl.pallas_call(
        body,
        out_shape=out_shape,
        in_specs=[smem if x.dtype == jnp.int32 else VMEM for x in args],
        out_specs=[VMEM] * len(out_shape),
        scratch_shapes=scratch,
        compiler_params=pltpu.CompilerParams(vmem_limit_bytes=24 * 1024 * 1024),
    )(*args)


def facts_body(rows_ref, columns_ref, count_ref, index_ref, out):
    values = []
    for slot in range(rows_ref.shape[0]):
        values += [rows_ref[slot], columns_ref[slot], (slot < count_ref[0]).astype(jnp.int32)]
    lane = lax.broadcasted_iota(jnp.int32, out.shape, 1)
    line = jnp.zeros(out.shape, jnp.int32)
    for n, value in enumerate(values + [index_ref[0]]):
        line = jnp.where(lane == n, value, line)
    out[...] = line


class Facts:
    def __init__(self, ref, slab_ref, slots, slabs, columns):
        self.ref, self.slab, self.slots, self.slabs, self.columns = ref, slab_ref[0], slots, slabs, columns

    def slot(self, angle, slot):
        return tuple(self.ref[angle, 3 * slot + i] for i in range(3))

    def layer(self, step):
        layer = self.slab + step
        layer = jnp.where(layer < 0, layer + self.slabs, layer)
        return jnp.where(layer >= self.slabs, layer - self.slabs, layer)

    def columns_of(self, angle, slot, layer):
        index = self.ref[angle, 3 * self.slots]
        shift = ((index - angle_center) * (layer - self.slabs // 2)) >> (shear_divisor.bit_length() - 1)
        left = self.slot(angle, slot)[1] + shift
        left = jnp.where(left < 0, left + self.columns, left)
        left = jnp.where(left >= self.columns, left - self.columns, left)
        starts = []
        for i in range(3):
            start = (left & -LANE) + i * LANE
            start = jnp.where(start >= self.columns, start - self.columns, start)
            starts.append(pl.multiple_of(start, LANE))
        return starts, left & (LANE - 1)


def cut_body(absolute, facts_ref, slab_ref, *refs):
    blocks, out = refs[:-1], refs[-1]
    angles, slots, rows, width = out.shape
    facts = Facts(facts_ref, slab_ref, slots, len(blocks), blocks[0].shape[1])
    lane = lax.broadcasted_iota(jnp.int32, (rows, LANE), 1)
    for slot in range(slots):
        for angle in range(angles):

            @pl.when(facts.slot(angle, slot)[2] > 0)
            def _():
                total = [jnp.zeros((rows, LANE), jnp.float32)] * 2
                for k, block in enumerate(blocks):
                    layer = k if absolute else facts.layer(-k)
                    starts, inside = facts.columns_of(angle, slot, layer)
                    turned = [
                        pltpu.roll(block[:, pl.ds(start, LANE)].astype(jnp.float32), (LANE - inside) & (LANE - 1), 1)
                        for start in starts
                    ]
                    here = lane < LANE - inside
                    total = [t + jnp.where(here, turned[i], turned[i + 1]) for i, t in enumerate(total)]
                out[angle, slot] = jnp.concatenate(total, axis=1).astype(jnp.bfloat16)


def cut_windows(facts, blocks, angles, slots, width):
    out = jax.ShapeDtypeStruct((angles, slots, blocks[0].shape[0], width), jnp.bfloat16)
    return call(functools.partial(cut_body, False), [out], [], *facts, *blocks)[0]


def cut_rest(facts, blocks, done, which):
    angles, slots, rows, width = done.shape
    out = jax.ShapeDtypeStruct((angles, 2, slots, rows, width), jnp.bfloat16)

    def body(facts_ref, slab_ref, blocks, done, out):
        out[:, 1 - which] = done[...]
        cut_body(True, facts_ref, slab_ref, *(blocks.at[k] for k in range(blocks.shape[0])), out.at[:, which])

    return call(body, [out], [], *facts, blocks, done)[0]


def cos_sin(angle):
    turns = jnp.round(angle * 0.6366197723675814)
    rest = angle - turns * 1.5703125
    rest = rest - turns * 4.837512969970703e-4
    rest = rest - turns * 7.549789948768648e-8
    square = rest * rest
    sine = (-1.9515295891e-4 * square + 8.3321608736e-3) * square - 1.6666654611e-1
    sine = sine * square * rest + rest
    cosine = (2.443315711809948e-5 * square - 1.388731625493765e-3) * square + 4.166664568298827e-2
    cosine = cosine * square * square - 0.5 * square + 1.0
    quarter = turns.astype(jnp.int32)
    odd = (quarter & 1) == 1
    first, second = jnp.where(odd, sine, cosine), jnp.where(odd, cosine, sine)
    return (
        jnp.where(((quarter + 1) & 2) == 2, -first, first),
        jnp.where((quarter & 2) == 2, -second, second),
    )


def patch_body(row_ref, count_ref, windows, probe, patterns, wr_ref, wi_ref, own_out, next_out):
    angles, _, slots, rows, width = windows.shape
    f32, bf16 = jnp.float32, jnp.bfloat16
    blocks = angles // 2
    tall = 2 * blocks * rows
    for slot in range(slots):
        row = row_ref[slot]

        @pl.when(slot < count_ref[0])
        def _():
            pick = one_hot(width, tall, -row)
            window = []
            for part in range(2):
                held = [windows[2 * k + part, tile, slot] for tile in range(2) for k in range(blocks)]
                window.append(dot(pick, jnp.concatenate(held, axis=0)))
            phase, absorption = window
            magnitude = jnp.exp(-absorption)
            cosine, sine = cos_sin(phase)
            trans_real = magnitude * cosine
            trans_imag = magnitude * sine
            probe_real, probe_imag = probe[0], probe[1]
            wr, wi = wr_ref[...], wi_ref[...]
            wave_real = (probe_real * trans_real - probe_imag * trans_imag).astype(bf16)
            wave_imag = (probe_real * trans_imag + probe_imag * trans_real).astype(bf16)
            left_real = (dot(wr, wave_real) - dot(wi, wave_imag)).astype(bf16)
            left_imag = (dot(wr, wave_imag) + dot(wi, wave_real)).astype(bf16)
            far_real = dot(left_real, wr) - dot(left_imag, wi)
            far_imag = dot(left_real, wi) + dot(left_imag, wr)
            power = far_real * far_real + far_imag * far_imag + floor_square
            keeping = 1.0 - patterns[slot].astype(f32) * lax.rsqrt(power)
            resid_real = (far_real * keeping).astype(bf16)
            resid_imag = (far_imag * keeping).astype(bf16)
            back_real = (dot(wr, resid_real) + dot(wi, resid_imag)).astype(bf16)
            back_imag = (dot(wr, resid_imag) - dot(wi, resid_real)).astype(bf16)
            exit_real = dot(back_real, wr) + dot(back_imag, wi)
            exit_imag = dot(back_imag, wr) - dot(back_real, wi)
            mixed_real = probe_real * exit_real + probe_imag * exit_imag
            mixed_imag = probe_real * exit_imag - probe_imag * exit_real
            final_real = trans_real * mixed_real + trans_imag * mixed_imag
            final_imag = trans_real * mixed_imag - trans_imag * mixed_real
            put = one_hot(tall, width, row)
            for part, value in enumerate((final_imag, -final_real)):
                placed = dot(put, value.astype(bf16)).astype(bf16)
                for k in range(blocks):
                    own_out[2 * k + part, slot] = placed[k * rows : (k + 1) * rows]
                    below = placed[(blocks + k) * rows : (blocks + k + 1) * rows]
                    next_out[2 * (blocks - 1 - k) + part, slot] = below


def patch_gradients(slot_rows, count, windows, probe_wave, patterns, tables):
    angles, _, slots, rows, width = windows.shape
    out = jax.ShapeDtypeStruct((angles, slots, rows, width), jnp.bfloat16)
    return call(patch_body, [out, out], [], slot_rows, count, windows, probe_wave, patterns, *tables)


def place_body(facts_ref, slab_ref, windows, *refs):
    outs, total = refs[:-1], refs[-1]
    angles, slots, rows, width = windows.shape
    slabs = total.shape[0]
    facts = Facts(facts_ref, slab_ref, slots, slabs, total.shape[2])
    lane = lax.broadcasted_iota(jnp.int32, (rows, LANE), 1)
    total[...] = jnp.zeros_like(total)
    for slot in range(slots):
        for angle in range(angles):

            @pl.when(facts.slot(angle, slot)[2] > 0)
            def _():
                window = windows[angle, slot].astype(jnp.float32)
                for k in range(slabs):
                    layer = facts.layer(k) if len(outs) > 1 else k
                    starts, inside = facts.columns_of(angle, slot, layer)
                    first, second = (pltpu.roll(window[:, i * LANE : (i + 1) * LANE], inside, 1) for i in range(2))
                    there = lane < inside
                    total[k, :, pl.ds(starts[0], LANE)] += jnp.where(there, 0.0, first)
                    total[k, :, pl.ds(starts[1], LANE)] += jnp.where(there, first, second)
                    total[k, :, pl.ds(starts[2], LANE)] += jnp.where(there, second, 0.0)
    for k, out in enumerate(outs):
        out[...] = (total[k] if len(outs) > 1 else total[...]).astype(out.dtype)


def place_windows(facts, windows, slabs, columns, together=False):
    shape = (windows.shape[2], columns)
    outs = [jax.ShapeDtypeStruct(shape, jnp.bfloat16 if k else jnp.float32) for k in range(slabs)]
    if together:
        outs = [jax.ShapeDtypeStruct((slabs, *shape), jnp.bfloat16)]
    return call(place_body, outs, [pltpu.VMEM((slabs, *shape), jnp.float32)], *facts, windows)


def sum_body(*refs):
    *terms, out = refs
    total = sum(term[...].astype(jnp.float32) for term in terms).astype(out.dtype)
    for k in range(out.shape[0]):
        out[k] = total


def sum_copies(terms, copies):
    out = jax.ShapeDtypeStruct((copies, *terms[0].shape), jnp.bfloat16)
    return call(sum_body, [out], [], *terms)[0]


def step_body(part_ref, layer, gradient, *refs):
    out, made, sems = refs[-3:]
    part = part_ref[0]
    size = gradient.shape[0] // 4
    copies = []
    for n in range(4):
        rows = slice(n * size, (n + 1) * size)
        made[rows] = layer[part, rows].astype(jnp.float32) - step_size * gradient[rows].astype(jnp.float32)
        copies.append(
            pltpu.make_async_copy(made.at[pl.ds(n * size, size)], out.at[part, pl.ds(n * size, size)], sems.at[n])
        )
        copies[-1].start()
    for copy in copies:
        copy.wait()


def step(part, layer, gradient, *stepped):
    return pl.pallas_call(
        step_body,
        out_shape=jax.ShapeDtypeStruct(layer.shape, jnp.float32),
        in_specs=[pl.BlockSpec(memory_space=pltpu.SMEM), VMEM, VMEM]
        + [pl.BlockSpec(memory_space=pltpu.HBM)] * len(stepped),
        out_specs=pl.BlockSpec(memory_space=pltpu.HBM),
        scratch_shapes=[pltpu.VMEM(gradient.shape, jnp.float32), pltpu.SemaphoreType.DMA((4,))],
        input_output_aliases={3: 0} if stepped else {},
        compiler_params=pltpu.CompilerParams(vmem_limit_bytes=24 * 1024 * 1024),
    )(part.reshape(1).astype(jnp.int32), layer, gradient, *stepped)


def per_device(volume, probe_wave, amplitudes, offsets, column_starts, counts, angle_ids):
    layer = volume.reshape(volume.shape[0], *volume.shape[2:])
    tile_rows, columns = layer.shape[1:]
    width = amplitudes.shape[-1]
    slots = offsets.shape[3]
    angles, slabs, tiles = (lax.axis_size(axis) for axis in ("angle", "slab", "tile"))
    slab, angle = lax.axis_index("slab"), lax.axis_index("angle")
    f32, bf16 = jnp.float32, jnp.bfloat16
    tables = dft_tables(width)
    patterns = amplitudes.reshape(slots, width, width)

    core, place_z = angle % 2, angle // 2 % 4
    eight_groups = [[8 * f + i for i in range(8)] for f in range(angles // 8)]
    four_groups = [[8 * f + 2 * q + c for q in range(4)] for f in range(angles // 8) for c in range(2)]
    block_rows = tile_rows // 4

    def swap(value, by):
        return lax.ppermute(value, "angle", [(i, i ^ by) for i in range(angles)])

    def mirrored(value, by):
        pairs = [
            (a * tiles + t, (angles - 2 - (a - a % 2) + a % 2) * tiles + t + by)
            for a in range(angles)
            for t in range(tiles)
            if 0 <= t + by < tiles
        ]
        return lax.ppermute(value, ("angle", "tile"), pairs)

    def to_slab(value, by):
        return lax.ppermute(value, "slab", [(i, (i + by) % slabs) for i in range(slabs)])

    def to_eight(value):
        return lax.all_to_all(value, "angle", 0, 0, axis_index_groups=eight_groups, tiled=True)

    def to_four(value):
        return lax.all_to_all(value, "angle", 0, 0, axis_index_groups=four_groups, tiled=True)

    def to_slabs(value):
        return lax.all_to_all(value, "slab", 0, 0, tiled=True)

    def of_slabs(block):
        return [block] + [to_slab(block, k) for k in range(1, slabs)]

    def over_slabs(kept, *sent):
        return sum((to_slab(block, k + 1).astype(f32) for k, block in enumerate(sent)), kept)

    def live_to_eight(value, axis):
        def first(value):
            sent = to_eight(lax.slice_in_dim(value, 0, 1, axis=axis))
            return jnp.concatenate([sent, lax.slice_in_dim(value, 1, slots, axis=axis)], axis=axis)

        return lax.cond(more, to_eight, first, value)

    own_part = lax.dynamic_index_in_dim(layer, core, 0, keepdims=False)

    def rows_of(block):
        return lax.dynamic_slice(own_part, (block * block_rows, 0), (block_rows, columns))

    after = mirrored(rows_of(3 - place_z), -1)
    own = rows_of(place_z)

    slot_rows, count = offsets.reshape(slots), counts.reshape(1)
    line = jax.ShapeDtypeStruct((8, LANE), jnp.int32)
    meta = call(facts_body, [line], [], slot_rows, column_starts.reshape(slots), count, angle_ids)[0]
    eight = to_eight(meta)
    facts = (eight, slab.reshape(1).astype(jnp.int32))
    more = jnp.max(eight[:, 5 : 3 * slots : 3]) > 0
    own = of_slabs(own)
    after, own = lax.optimization_barrier((after, own))
    own = cut_windows(facts, own, 8, slots, width)
    after = to_slabs(jnp.broadcast_to(after, (slabs, *after.shape)))
    after, own = lax.optimization_barrier((after, own))
    windows = live_to_eight(cut_rest(facts, after, own, 1), 2)

    own, after = patch_gradients(slot_rows, count, windows, probe_wave, patterns, tables)
    after, own = lax.optimization_barrier((live_to_eight(after, 1), own))
    own = to_eight(own)
    spill = mirrored(over_slabs(*place_windows(facts, after, slabs, columns)).astype(bf16), 1)
    own = to_slabs(place_windows(facts, own, slabs, columns, together=True)[0])
    own = jnp.sum(own.astype(f32), axis=0)

    total = lax.optimization_barrier((own + spill.astype(f32)).astype(bf16))
    total = to_four(sum_copies([total, swap(total, 8)], 4)).reshape(tile_rows, columns)
    new = step(core, layer, total)
    return step(1 - core, layer, swap(total, 1), new).reshape(volume.shape)


def solution(mesh):
    in_specs = (
        P(None, "slab", "tile", None),
        P(),
        P("angle", "tile", "slab", None, None, None),
        P("angle", "tile", "slab", None),
        P("angle", "tile", "slab", None),
        P("angle", "tile", "slab"),
        P("angle"),
    )
    out_specs = P(None, "slab", "tile", None)
    return jax.shard_map(
        per_device, mesh=mesh, in_specs=in_specs, out_specs=out_specs, check_vma=False
    )
```

```python
import functools

import jax
import jax.numpy as jnp
import ml_dtypes
import numpy as np
from jax import lax
from jax.experimental import pallas as pl
from jax.experimental.pallas import tpu as pltpu
from jax.sharding import PartitionSpec as P

angle_center = 600
shear_divisor = 64
step_size = 0.03
floor_square = 0.25

LANE = 128


def dft_tables(plane_width):
    index_line = np.arange(plane_width, dtype=np.int32)
    product_mod = np.mod(index_line[:, None] * index_line[None, :], plane_width)
    phase_table = product_mod.astype(np.float32) * np.float32(2.0 * 3.141592653589793 / plane_width)
    scale_factor = np.float32(plane_width ** (-0.5))
    table_real = (np.cos(phase_table) * scale_factor).astype(ml_dtypes.bfloat16)
    table_imag = (-np.sin(phase_table) * scale_factor).astype(ml_dtypes.bfloat16)
    return table_real, table_imag


def dot(left, right):
    return jnp.dot(left, right, preferred_element_type=jnp.float32)


def one_hot(rows, columns, down):
    row = lax.broadcasted_iota(jnp.int32, (rows, columns), 0)
    column = lax.broadcasted_iota(jnp.int32, (rows, columns), 1)
    return (row - column == down).astype(jnp.float32).astype(jnp.bfloat16)


VMEM = pl.BlockSpec(memory_space=pltpu.VMEM)


def call(body, out_shape, scratch, *args):
    smem = pl.BlockSpec(memory_space=pltpu.SMEM)
    return pl.pallas_call(
        body,
        out_shape=out_shape,
        in_specs=[smem if x.dtype == jnp.int32 else VMEM for x in args],
        out_specs=[VMEM] * len(out_shape),
        scratch_shapes=scratch,
        compiler_params=pltpu.CompilerParams(vmem_limit_bytes=24 * 1024 * 1024),
    )(*args)


def facts_body(rows_ref, columns_ref, count_ref, index_ref, out):
    values = []
    for slot in range(rows_ref.shape[0]):
        values += [rows_ref[slot], columns_ref[slot], (slot < count_ref[0]).astype(jnp.int32)]
    lane = lax.broadcasted_iota(jnp.int32, out.shape, 1)
    line = jnp.zeros(out.shape, jnp.int32)
    for n, value in enumerate(values + [index_ref[0]]):
        line = jnp.where(lane == n, value, line)
    out[...] = line


class Facts:
    def __init__(self, ref, slab_ref, slots, slabs, columns):
        self.ref, self.slab, self.slots, self.slabs, self.columns = ref, slab_ref[0], slots, slabs, columns

    def slot(self, angle, slot):
        return tuple(self.ref[angle, 3 * slot + i] for i in range(3))

    def layer(self, step):
        layer = self.slab + step
        layer = jnp.where(layer < 0, layer + self.slabs, layer)
        return jnp.where(layer >= self.slabs, layer - self.slabs, layer)

    def columns_of(self, angle, slot, layer):
        index = self.ref[angle, 3 * self.slots]
        shift = ((index - angle_center) * (layer - self.slabs // 2)) >> (shear_divisor.bit_length() - 1)
        left = self.slot(angle, slot)[1] + shift
        left = jnp.where(left < 0, left + self.columns, left)
        left = jnp.where(left >= self.columns, left - self.columns, left)
        starts = []
        for i in range(3):
            start = (left & -LANE) + i * LANE
            start = jnp.where(start >= self.columns, start - self.columns, start)
            starts.append(pl.multiple_of(start, LANE))
        return starts, left & (LANE - 1)


def cut_body(absolute, facts_ref, slab_ref, *refs):
    blocks, out = refs[:-1], refs[-1]
    angles, slots, rows, width = out.shape
    facts = Facts(facts_ref, slab_ref, slots, len(blocks), blocks[0].shape[1])
    lane = lax.broadcasted_iota(jnp.int32, (rows, LANE), 1)
    for slot in range(slots):
        for angle in range(angles):

            @pl.when(facts.slot(angle, slot)[2] > 0)
            def _():
                total = [jnp.zeros((rows, LANE), jnp.float32)] * 2
                for k, block in enumerate(blocks):
                    layer = k if absolute else facts.layer(-k)
                    starts, inside = facts.columns_of(angle, slot, layer)
                    turned = [
                        pltpu.roll(block[:, pl.ds(start, LANE)].astype(jnp.float32), (LANE - inside) & (LANE - 1), 1)
                        for start in starts
                    ]
                    here = lane < LANE - inside
                    total = [t + jnp.where(here, turned[i], turned[i + 1]) for i, t in enumerate(total)]
                out[angle, slot] = jnp.concatenate(total, axis=1).astype(jnp.bfloat16)


def cut_windows(facts, blocks, angles, slots, width):
    out = jax.ShapeDtypeStruct((angles, slots, blocks[0].shape[0], width), jnp.bfloat16)
    return call(functools.partial(cut_body, False), [out], [], *facts, *blocks)[0]


def cut_rest(facts, blocks, done, which):
    angles, slots, rows, width = done.shape
    out = jax.ShapeDtypeStruct((angles, 2, slots, rows, width), jnp.bfloat16)

    def body(facts_ref, slab_ref, blocks, done, out):
        out[:, 1 - which] = done[...]
        cut_body(True, facts_ref, slab_ref, *(blocks.at[k] for k in range(blocks.shape[0])), out.at[:, which])

    return call(body, [out], [], *facts, blocks, done)[0]


def cos_sin(angle):
    turns = jnp.round(angle * 0.6366197723675814)
    rest = angle - turns * 1.5703125
    rest = rest - turns * 4.837512969970703e-4
    rest = rest - turns * 7.549789948768648e-8
    square = rest * rest
    sine = (-1.9515295891e-4 * square + 8.3321608736e-3) * square - 1.6666654611e-1
    sine = sine * square * rest + rest
    cosine = (2.443315711809948e-5 * square - 1.388731625493765e-3) * square + 4.166664568298827e-2
    cosine = cosine * square * square - 0.5 * square + 1.0
    quarter = turns.astype(jnp.int32)
    odd = (quarter & 1) == 1
    first, second = jnp.where(odd, sine, cosine), jnp.where(odd, cosine, sine)
    return (
        jnp.where(((quarter + 1) & 2) == 2, -first, first),
        jnp.where((quarter & 2) == 2, -second, second),
    )


def patch_body(row_ref, count_ref, windows, probe, patterns, wr_ref, wi_ref, own_out, next_out):
    angles, _, slots, rows, width = windows.shape
    f32, bf16 = jnp.float32, jnp.bfloat16
    blocks = angles // 2
    tall = 2 * blocks * rows
    for slot in range(slots):
        row = row_ref[slot]

        @pl.when(slot < count_ref[0])
        def _():
            pick = one_hot(width, tall, -row)
            window = []
            for part in range(2):
                held = [windows[2 * k + part, tile, slot] for tile in range(2) for k in range(blocks)]
                window.append(dot(pick, jnp.concatenate(held, axis=0)))
            phase, absorption = window
            magnitude = jnp.exp(-absorption)
            cosine, sine = cos_sin(phase)
            trans_real = magnitude * cosine
            trans_imag = magnitude * sine
            probe_real, probe_imag = probe[0], probe[1]
            wr, wi = wr_ref[...], wi_ref[...]
            wave_real = (probe_real * trans_real - probe_imag * trans_imag).astype(bf16)
            wave_imag = (probe_real * trans_imag + probe_imag * trans_real).astype(bf16)
            left_real = (dot(wr, wave_real) - dot(wi, wave_imag)).astype(bf16)
            left_imag = (dot(wr, wave_imag) + dot(wi, wave_real)).astype(bf16)
            far_real = dot(left_real, wr) - dot(left_imag, wi)
            far_imag = dot(left_real, wi) + dot(left_imag, wr)
            power = far_real * far_real + far_imag * far_imag + floor_square
            keeping = 1.0 - patterns[slot].astype(f32) * lax.rsqrt(power)
            resid_real = (far_real * keeping).astype(bf16)
            resid_imag = (far_imag * keeping).astype(bf16)
            back_real = (dot(wr, resid_real) + dot(wi, resid_imag)).astype(bf16)
            back_imag = (dot(wr, resid_imag) - dot(wi, resid_real)).astype(bf16)
            exit_real = dot(back_real, wr) + dot(back_imag, wi)
            exit_imag = dot(back_imag, wr) - dot(back_real, wi)
            mixed_real = probe_real * exit_real + probe_imag * exit_imag
            mixed_imag = probe_real * exit_imag - probe_imag * exit_real
            final_real = trans_real * mixed_real + trans_imag * mixed_imag
            final_imag = trans_real * mixed_imag - trans_imag * mixed_real
            put = one_hot(tall, width, row)
            for part, value in enumerate((final_imag, -final_real)):
                placed = dot(put, value.astype(bf16)).astype(bf16)
                for k in range(blocks):
                    own_out[2 * k + part, slot] = placed[k * rows : (k + 1) * rows]
                    below = placed[(blocks + k) * rows : (blocks + k + 1) * rows]
                    next_out[2 * (blocks - 1 - k) + part, slot] = below


def patch_gradients(slot_rows, count, windows, probe_wave, patterns, tables):
    angles, _, slots, rows, width = windows.shape
    out = jax.ShapeDtypeStruct((angles, slots, rows, width), jnp.bfloat16)
    return call(patch_body, [out, out], [], slot_rows, count, windows, probe_wave, patterns, *tables)


def place_body(facts_ref, slab_ref, windows, *refs):
    outs, total = refs[:-1], refs[-1]
    angles, slots, rows, width = windows.shape
    slabs = total.shape[0]
    facts = Facts(facts_ref, slab_ref, slots, slabs, total.shape[2])
    lane = lax.broadcasted_iota(jnp.int32, (rows, LANE), 1)
    total[...] = jnp.zeros_like(total)
    for slot in range(slots):
        for angle in range(angles):

            @pl.when(facts.slot(angle, slot)[2] > 0)
            def _():
                window = windows[angle, slot].astype(jnp.float32)
                for k in range(slabs):
                    starts, inside = facts.columns_of(angle, slot, facts.layer(k))
                    first, second = (pltpu.roll(window[:, i * LANE : (i + 1) * LANE], inside, 1) for i in range(2))
                    there = lane < inside
                    total[k, :, pl.ds(starts[0], LANE)] += jnp.where(there, 0.0, first)
                    total[k, :, pl.ds(starts[1], LANE)] += jnp.where(there, first, second)
                    total[k, :, pl.ds(starts[2], LANE)] += jnp.where(there, second, 0.0)
    for k, out in enumerate(outs):
        out[...] = total[k].astype(out.dtype)


def place_windows(facts, windows, slabs, columns):
    shape = (windows.shape[2], columns)
    outs = [jax.ShapeDtypeStruct(shape, jnp.bfloat16 if k else jnp.float32) for k in range(slabs)]
    return call(place_body, outs, [pltpu.VMEM((slabs, *shape), jnp.float32)], *facts, windows)


def sum_body(*refs):
    *terms, out = refs
    total = sum(term[...].astype(jnp.float32) for term in terms).astype(out.dtype)
    for k in range(out.shape[0]):
        out[k] = total


def sum_copies(terms, copies):
    out = jax.ShapeDtypeStruct((copies, *terms[0].shape), jnp.bfloat16)
    return call(sum_body, [out], [], *terms)[0]


def step_body(part_ref, layer, gradient, *refs):
    out, made, sems = refs[-3:]
    part = part_ref[0]
    size = gradient.shape[0] // 4
    copies = []
    for n in range(4):
        rows = slice(n * size, (n + 1) * size)
        made[rows] = layer[part, rows].astype(jnp.float32) - step_size * gradient[rows].astype(jnp.float32)
        copies.append(
            pltpu.make_async_copy(made.at[pl.ds(n * size, size)], out.at[part, pl.ds(n * size, size)], sems.at[n])
        )
        copies[-1].start()
    for copy in copies:
        copy.wait()


def step(part, layer, gradient, *stepped):
    return pl.pallas_call(
        step_body,
        out_shape=jax.ShapeDtypeStruct(layer.shape, jnp.float32),
        in_specs=[pl.BlockSpec(memory_space=pltpu.SMEM), VMEM, VMEM]
        + [pl.BlockSpec(memory_space=pltpu.HBM)] * len(stepped),
        out_specs=pl.BlockSpec(memory_space=pltpu.HBM),
        scratch_shapes=[pltpu.VMEM(gradient.shape, jnp.float32), pltpu.SemaphoreType.DMA((4,))],
        input_output_aliases={3: 0} if stepped else {},
        compiler_params=pltpu.CompilerParams(vmem_limit_bytes=24 * 1024 * 1024),
    )(part.reshape(1).astype(jnp.int32), layer, gradient, *stepped)


def per_device(volume, probe_wave, amplitudes, offsets, column_starts, counts, angle_ids):
    layer = volume.reshape(volume.shape[0], *volume.shape[2:])
    tile_rows, columns = layer.shape[1:]
    width = amplitudes.shape[-1]
    slots = offsets.shape[3]
    angles, slabs, tiles = (lax.axis_size(axis) for axis in ("angle", "slab", "tile"))
    slab, angle = lax.axis_index("slab"), lax.axis_index("angle")
    f32, bf16 = jnp.float32, jnp.bfloat16
    tables = dft_tables(width)
    patterns = amplitudes.reshape(slots, width, width)

    core, place_z = angle % 2, angle // 2 % 4
    eight_groups = [[8 * f + i for i in range(8)] for f in range(angles // 8)]
    four_groups = [[8 * f + 2 * q + c for q in range(4)] for f in range(angles // 8) for c in range(2)]
    block_rows = tile_rows // 4

    def swap(value, by):
        return lax.ppermute(value, "angle", [(i, i ^ by) for i in range(angles)])

    def mirrored(value, by):
        pairs = [
            (a * tiles + t, (angles - 2 - (a - a % 2) + a % 2) * tiles + t + by)
            for a in range(angles)
            for t in range(tiles)
            if 0 <= t + by < tiles
        ]
        return lax.ppermute(value, ("angle", "tile"), pairs)

    def to_slab(value, by):
        return lax.ppermute(value, "slab", [(i, (i + by) % slabs) for i in range(slabs)])

    def to_eight(value):
        return lax.all_to_all(value, "angle", 0, 0, axis_index_groups=eight_groups, tiled=True)

    def to_four(value):
        return lax.all_to_all(value, "angle", 0, 0, axis_index_groups=four_groups, tiled=True)

    def to_slabs(value):
        return lax.all_to_all(value, "slab", 0, 0, tiled=True)

    def of_slabs(block):
        return [block] + [to_slab(block, k) for k in range(1, slabs)]

    def over_slabs(kept, *sent):
        return sum((to_slab(block, k + 1).astype(f32) for k, block in enumerate(sent)), kept)

    def live_to_eight(value, axis):
        def first(value):
            sent = to_eight(lax.slice_in_dim(value, 0, 1, axis=axis))
            return jnp.concatenate([sent, lax.slice_in_dim(value, 1, slots, axis=axis)], axis=axis)

        return lax.cond(more, to_eight, first, value)

    own_part = lax.dynamic_index_in_dim(layer, core, 0, keepdims=False)

    def rows_of(block):
        return lax.dynamic_slice(own_part, (block * block_rows, 0), (block_rows, columns))

    after = mirrored(rows_of(3 - place_z), -1)
    own = rows_of(place_z)

    slot_rows, count = offsets.reshape(slots), counts.reshape(1)
    line = jax.ShapeDtypeStruct((8, LANE), jnp.int32)
    meta = call(facts_body, [line], [], slot_rows, column_starts.reshape(slots), count, angle_ids)[0]
    eight = to_eight(meta)
    facts = (eight, slab.reshape(1).astype(jnp.int32))
    more = jnp.max(eight[:, 5 : 3 * slots : 3]) > 0
    own = of_slabs(own)
    after, own = lax.optimization_barrier((after, own))
    own = cut_windows(facts, own, 8, slots, width)
    after = to_slabs(jnp.broadcast_to(after, (slabs, *after.shape)))
    after, own = lax.optimization_barrier((after, own))
    windows = live_to_eight(cut_rest(facts, after, own, 1), 2)

    own, after = patch_gradients(slot_rows, count, windows, probe_wave, patterns, tables)
    after, own = lax.optimization_barrier((live_to_eight(after, 1), own))
    own = to_eight(own)
    spill = mirrored(over_slabs(*place_windows(facts, after, slabs, columns)).astype(bf16), 1)
    own = over_slabs(*place_windows(facts, own, slabs, columns))

    total = lax.optimization_barrier((own + spill.astype(f32)).astype(bf16))
    total = to_four(sum_copies([total, swap(total, 8)], 4)).reshape(tile_rows, columns)
    new = step(core, layer, total)
    return step(1 - core, layer, swap(total, 1), new).reshape(volume.shape)


def solution(mesh):
    in_specs = (
        P(None, "slab", "tile", None),
        P(),
        P("angle", "tile", "slab", None, None, None),
        P("angle", "tile", "slab", None),
        P("angle", "tile", "slab", None),
        P("angle", "tile", "slab"),
        P("angle"),
    )
    out_specs = P(None, "slab", "tile", None)
    return jax.shard_map(
        per_device, mesh=mesh, in_specs=in_specs, out_specs=out_specs, check_vma=False
    )
```

```python
import functools

import jax
import jax.numpy as jnp
import ml_dtypes
import numpy as np
from jax import lax
from jax.experimental import pallas as pl
from jax.experimental.pallas import tpu as pltpu
from jax.sharding import PartitionSpec as P

angle_center = 600
shear_divisor = 64
step_size = 0.03
floor_square = 0.25

LANE = 128


def dft_tables(plane_width):
    index_line = np.arange(plane_width, dtype=np.int32)
    product_mod = np.mod(index_line[:, None] * index_line[None, :], plane_width)
    phase_table = product_mod.astype(np.float32) * np.float32(2.0 * 3.141592653589793 / plane_width)
    scale_factor = np.float32(plane_width ** (-0.5))
    table_real = (np.cos(phase_table) * scale_factor).astype(ml_dtypes.bfloat16)
    table_imag = (-np.sin(phase_table) * scale_factor).astype(ml_dtypes.bfloat16)
    return table_real, table_imag


def dot(left, right):
    return jnp.dot(left, right, preferred_element_type=jnp.float32)


def one_hot(rows, columns, down):
    row = lax.broadcasted_iota(jnp.int32, (rows, columns), 0)
    column = lax.broadcasted_iota(jnp.int32, (rows, columns), 1)
    return (row - column == down).astype(jnp.float32).astype(jnp.bfloat16)


VMEM = pl.BlockSpec(memory_space=pltpu.VMEM)


def call(body, out_shape, scratch, *args):
    smem = pl.BlockSpec(memory_space=pltpu.SMEM)
    return pl.pallas_call(
        body,
        out_shape=out_shape,
        in_specs=[smem if x.dtype == jnp.int32 else VMEM for x in args],
        out_specs=[VMEM] * len(out_shape),
        scratch_shapes=scratch,
        compiler_params=pltpu.CompilerParams(vmem_limit_bytes=24 * 1024 * 1024),
    )(*args)


def facts_body(rows_in, columns_in, count_in, index_in, out, rows_ref, columns_ref, count_ref, index_ref, sems):
    pairs = zip((rows_in, columns_in, count_in, index_in), (rows_ref, columns_ref, count_ref, index_ref))
    copies = [pltpu.make_async_copy(ref, to, sems.at[n]) for n, (ref, to) in enumerate(pairs)]
    for copy in copies:
        copy.start()
    for copy in copies:
        copy.wait()
    values = []
    for slot in range(rows_ref.shape[0]):
        values += [rows_ref[slot], columns_ref[slot], (slot < count_ref[0]).astype(jnp.int32)]
    lane = lax.broadcasted_iota(jnp.int32, out.shape, 1)
    line = jnp.zeros(out.shape, jnp.int32)
    for n, value in enumerate(values + [index_ref[0]]):
        line = jnp.where(lane == n, value, line)
    out[...] = line


def facts_line(*args):
    return pl.pallas_call(
        facts_body,
        out_shape=jax.ShapeDtypeStruct((8, LANE), jnp.int32),
        in_specs=[pl.BlockSpec(memory_space=pltpu.HBM)] * len(args),
        out_specs=VMEM,
        scratch_shapes=[pltpu.SMEM(x.shape, jnp.int32) for x in args] + [pltpu.SemaphoreType.DMA((len(args),))],
    )(*args)


class Facts:
    def __init__(self, ref, slab_ref, slots, slabs, columns):
        self.ref, self.slab, self.slots, self.slabs, self.columns = ref, slab_ref[0], slots, slabs, columns

    def slot(self, angle, slot):
        return tuple(self.ref[angle, 3 * slot + i] for i in range(3))

    def layer(self, step):
        layer = self.slab + step
        layer = jnp.where(layer < 0, layer + self.slabs, layer)
        return jnp.where(layer >= self.slabs, layer - self.slabs, layer)

    def columns_of(self, angle, slot, layer):
        index = self.ref[angle, 3 * self.slots]
        shift = ((index - angle_center) * (layer - self.slabs // 2)) >> (shear_divisor.bit_length() - 1)
        left = self.slot(angle, slot)[1] + shift
        left = jnp.where(left < 0, left + self.columns, left)
        left = jnp.where(left >= self.columns, left - self.columns, left)
        starts = []
        for i in range(3):
            start = (left & -LANE) + i * LANE
            start = jnp.where(start >= self.columns, start - self.columns, start)
            starts.append(pl.multiple_of(start, LANE))
        return starts, left & (LANE - 1)


def cut_body(absolute, facts_ref, slab_ref, *refs):
    blocks, out = refs[:-1], refs[-1]
    angles, slots, rows, width = out.shape
    facts = Facts(facts_ref, slab_ref, slots, len(blocks), blocks[0].shape[1])
    lane = lax.broadcasted_iota(jnp.int32, (rows, LANE), 1)
    for slot in range(slots):
        for angle in range(angles):

            @pl.when(facts.slot(angle, slot)[2] > 0)
            def _():
                total = [jnp.zeros((rows, LANE), jnp.float32)] * 2
                for k, block in enumerate(blocks):
                    layer = k if absolute else facts.layer(-k)
                    starts, inside = facts.columns_of(angle, slot, layer)
                    turned = [
                        pltpu.roll(block[:, pl.ds(start, LANE)].astype(jnp.float32), (LANE - inside) & (LANE - 1), 1)
                        for start in starts
                    ]
                    here = lane < LANE - inside
                    total = [t + jnp.where(here, turned[i], turned[i + 1]) for i, t in enumerate(total)]
                out[angle, slot] = jnp.concatenate(total, axis=1).astype(jnp.bfloat16)


def cut_windows(facts, blocks, angles, slots, width):
    out = jax.ShapeDtypeStruct((angles, slots, blocks[0].shape[0], width), jnp.bfloat16)
    return call(functools.partial(cut_body, False), [out], [], *facts, *blocks)[0]


def cut_rest(facts, blocks, done, which):
    angles, slots, rows, width = done.shape
    out = jax.ShapeDtypeStruct((angles, 2, slots, rows, width), jnp.bfloat16)

    def body(facts_ref, slab_ref, blocks, done, out):
        out[:, 1 - which] = done[...]
        cut_body(True, facts_ref, slab_ref, *(blocks.at[k] for k in range(blocks.shape[0])), out.at[:, which])

    return call(body, [out], [], *facts, blocks, done)[0]


def cos_sin(angle):
    turns = jnp.round(angle * 0.6366197723675814)
    rest = angle - turns * 1.5703125
    rest = rest - turns * 4.837512969970703e-4
    rest = rest - turns * 7.549789948768648e-8
    square = rest * rest
    sine = (-1.9515295891e-4 * square + 8.3321608736e-3) * square - 1.6666654611e-1
    sine = sine * square * rest + rest
    cosine = (2.443315711809948e-5 * square - 1.388731625493765e-3) * square + 4.166664568298827e-2
    cosine = cosine * square * square - 0.5 * square + 1.0
    quarter = turns.astype(jnp.int32)
    odd = (quarter & 1) == 1
    first, second = jnp.where(odd, sine, cosine), jnp.where(odd, cosine, sine)
    return (
        jnp.where(((quarter + 1) & 2) == 2, -first, first),
        jnp.where((quarter & 2) == 2, -second, second),
    )


def patch_body(row_ref, count_ref, windows, probe, patterns, wr_ref, wi_ref, own_out, next_out):
    angles, _, slots, rows, width = windows.shape
    f32, bf16 = jnp.float32, jnp.bfloat16
    blocks = angles // 2
    tall = 2 * blocks * rows
    for slot in range(slots):
        row = row_ref[slot]

        @pl.when(slot < count_ref[0])
        def _():
            pick = one_hot(width, tall, -row)
            window = []
            for part in range(2):
                held = [windows[2 * k + part, tile, slot] for tile in range(2) for k in range(blocks)]
                window.append(dot(pick, jnp.concatenate(held, axis=0)))
            phase, absorption = window
            magnitude = jnp.exp(-absorption)
            cosine, sine = cos_sin(phase)
            trans_real = magnitude * cosine
            trans_imag = magnitude * sine
            probe_real, probe_imag = probe[0], probe[1]
            wr, wi = wr_ref[...], wi_ref[...]
            wave_real = (probe_real * trans_real - probe_imag * trans_imag).astype(bf16)
            wave_imag = (probe_real * trans_imag + probe_imag * trans_real).astype(bf16)
            left_real = (dot(wr, wave_real) - dot(wi, wave_imag)).astype(bf16)
            left_imag = (dot(wr, wave_imag) + dot(wi, wave_real)).astype(bf16)
            far_real = dot(left_real, wr) - dot(left_imag, wi)
            far_imag = dot(left_real, wi) + dot(left_imag, wr)
            power = far_real * far_real + far_imag * far_imag + floor_square
            keeping = 1.0 - patterns[slot].astype(f32) * lax.rsqrt(power)
            resid_real = (far_real * keeping).astype(bf16)
            resid_imag = (far_imag * keeping).astype(bf16)
            back_real = (dot(wr, resid_real) + dot(wi, resid_imag)).astype(bf16)
            back_imag = (dot(wr, resid_imag) - dot(wi, resid_real)).astype(bf16)
            exit_real = dot(back_real, wr) + dot(back_imag, wi)
            exit_imag = dot(back_imag, wr) - dot(back_real, wi)
            mixed_real = probe_real * exit_real + probe_imag * exit_imag
            mixed_imag = probe_real * exit_imag - probe_imag * exit_real
            final_real = trans_real * mixed_real + trans_imag * mixed_imag
            final_imag = trans_real * mixed_imag - trans_imag * mixed_real
            put = one_hot(tall, width, row)
            for part, value in enumerate((final_imag, -final_real)):
                placed = dot(put, value.astype(bf16)).astype(bf16)
                for k in range(blocks):
                    own_out[2 * k + part, slot] = placed[k * rows : (k + 1) * rows]
                    below = placed[(blocks + k) * rows : (blocks + k + 1) * rows]
                    next_out[2 * (blocks - 1 - k) + part, slot] = below


def patch_gradients(slot_rows, count, windows, probe_wave, patterns, tables):
    angles, _, slots, rows, width = windows.shape
    out = jax.ShapeDtypeStruct((angles, slots, rows, width), jnp.bfloat16)
    return call(patch_body, [out, out], [], slot_rows, count, windows, probe_wave, patterns, *tables)


def place_body(facts_ref, slab_ref, windows, *refs):
    outs, total = refs[:-1], refs[-1]
    angles, slots, rows, width = windows.shape
    slabs = total.shape[0]
    facts = Facts(facts_ref, slab_ref, slots, slabs, total.shape[2])
    lane = lax.broadcasted_iota(jnp.int32, (rows, LANE), 1)
    total[...] = jnp.zeros_like(total)
    for slot in range(slots):
        for angle in range(angles):

            @pl.when(facts.slot(angle, slot)[2] > 0)
            def _():
                window = windows[angle, slot].astype(jnp.float32)
                for k in range(slabs):
                    layer = facts.layer(k) if len(outs) > 1 else k
                    starts, inside = facts.columns_of(angle, slot, layer)
                    first, second = (pltpu.roll(window[:, i * LANE : (i + 1) * LANE], inside, 1) for i in range(2))
                    there = lane < inside
                    total[k, :, pl.ds(starts[0], LANE)] += jnp.where(there, 0.0, first)
                    total[k, :, pl.ds(starts[1], LANE)] += jnp.where(there, first, second)
                    total[k, :, pl.ds(starts[2], LANE)] += jnp.where(there, second, 0.0)
    for k, out in enumerate(outs):
        out[...] = (total[k] if len(outs) > 1 else total[...]).astype(out.dtype)


def place_windows(facts, windows, slabs, columns, together=False):
    shape = (windows.shape[2], columns)
    outs = [jax.ShapeDtypeStruct(shape, jnp.bfloat16 if k else jnp.float32) for k in range(slabs)]
    if together:
        outs = [jax.ShapeDtypeStruct((slabs, *shape), jnp.bfloat16)]
    return call(place_body, outs, [pltpu.VMEM((slabs, *shape), jnp.float32)], *facts, windows)


def sum_body(*refs):
    *terms, out = refs
    total = sum(term[...].astype(jnp.float32) for term in terms).astype(out.dtype)
    for k in range(out.shape[0]):
        out[k] = total


def sum_copies(terms, copies):
    out = jax.ShapeDtypeStruct((copies, *terms[0].shape), jnp.bfloat16)
    return call(sum_body, [out], [], *terms)[0]


def step_body(part_ref, layer, gradient, *refs):
    out, made, sems = refs[-3:]
    part = part_ref[0]
    size = gradient.shape[0] // 4
    copies = []
    for n in range(4):
        rows = slice(n * size, (n + 1) * size)
        made[rows] = layer[part, rows].astype(jnp.float32) - step_size * gradient[rows].astype(jnp.float32)
        copies.append(
            pltpu.make_async_copy(made.at[pl.ds(n * size, size)], out.at[part, pl.ds(n * size, size)], sems.at[n])
        )
        copies[-1].start()
    for copy in copies:
        copy.wait()


def step(part, layer, gradient, *stepped):
    return pl.pallas_call(
        step_body,
        out_shape=jax.ShapeDtypeStruct(layer.shape, jnp.float32),
        in_specs=[pl.BlockSpec(memory_space=pltpu.SMEM), VMEM, VMEM]
        + [pl.BlockSpec(memory_space=pltpu.HBM)] * len(stepped),
        out_specs=pl.BlockSpec(memory_space=pltpu.HBM),
        scratch_shapes=[pltpu.VMEM(gradient.shape, jnp.float32), pltpu.SemaphoreType.DMA((4,))],
        input_output_aliases={3: 0} if stepped else {},
        compiler_params=pltpu.CompilerParams(vmem_limit_bytes=24 * 1024 * 1024),
    )(part.reshape(1).astype(jnp.int32), layer, gradient, *stepped)


def per_device(volume, probe_wave, amplitudes, offsets, column_starts, counts, angle_ids):
    layer = volume.reshape(volume.shape[0], *volume.shape[2:])
    tile_rows, columns = layer.shape[1:]
    width = amplitudes.shape[-1]
    slots = offsets.shape[3]
    angles, slabs, tiles = (lax.axis_size(axis) for axis in ("angle", "slab", "tile"))
    slab, angle = lax.axis_index("slab"), lax.axis_index("angle")
    f32, bf16 = jnp.float32, jnp.bfloat16
    tables = dft_tables(width)
    patterns = amplitudes.reshape(slots, width, width)

    core, place_z = angle % 2, angle // 2 % 4
    eight_groups = [[8 * f + i for i in range(8)] for f in range(angles // 8)]
    four_groups = [[8 * f + 2 * q + c for q in range(4)] for f in range(angles // 8) for c in range(2)]
    block_rows = tile_rows // 4

    def swap(value, by):
        return lax.ppermute(value, "angle", [(i, i ^ by) for i in range(angles)])

    def mirrored(value, by):
        pairs = [
            (a * tiles + t, (angles - 2 - (a - a % 2) + a % 2) * tiles + t + by)
            for a in range(angles)
            for t in range(tiles)
            if 0 <= t + by < tiles
        ]
        return lax.ppermute(value, ("angle", "tile"), pairs)

    def to_slab(value, by):
        return lax.ppermute(value, "slab", [(i, (i + by) % slabs) for i in range(slabs)])

    def to_eight(value):
        return lax.all_to_all(value, "angle", 0, 0, axis_index_groups=eight_groups, tiled=True)

    def to_four(value):
        return lax.all_to_all(value, "angle", 0, 0, axis_index_groups=four_groups, tiled=True)

    def to_slabs(value):
        return lax.all_to_all(value, "slab", 0, 0, tiled=True)

    def of_slabs(block):
        return [block] + [to_slab(block, k) for k in range(1, slabs)]

    def over_slabs(kept, *sent):
        return sum((to_slab(block, k + 1).astype(f32) for k, block in enumerate(sent)), kept)

    def live_to_eight(value, axis):
        def first(value):
            sent = to_eight(lax.slice_in_dim(value, 0, 1, axis=axis))
            return jnp.concatenate([sent, lax.slice_in_dim(value, 1, slots, axis=axis)], axis=axis)

        return lax.cond(more, to_eight, first, value)

    own_part = lax.dynamic_index_in_dim(layer, core, 0, keepdims=False)

    def rows_of(block):
        return lax.dynamic_slice(own_part, (block * block_rows, 0), (block_rows, columns))

    after = mirrored(rows_of(3 - place_z), -1)
    own = rows_of(place_z)

    slot_rows, count = offsets.reshape(slots), counts.reshape(1)
    meta = facts_line(slot_rows, column_starts.reshape(slots), count, angle_ids)
    eight = to_eight(meta)
    facts = (eight, slab.reshape(1).astype(jnp.int32))
    more = jnp.max(eight[:, 5 : 3 * slots : 3]) > 0
    own = of_slabs(own)
    after, own = lax.optimization_barrier((after, own))
    own = cut_windows(facts, own, 8, slots, width)
    after = to_slabs(jnp.broadcast_to(after, (slabs, *after.shape)))
    after, own = lax.optimization_barrier((after, own))
    windows = live_to_eight(cut_rest(facts, after, own, 1), 2)

    own, after = patch_gradients(slot_rows, count, windows, probe_wave, patterns, tables)
    after, own = lax.optimization_barrier((live_to_eight(after, 1), own))
    own = to_eight(own)
    spill = mirrored(over_slabs(*place_windows(facts, after, slabs, columns)).astype(bf16), 1)
    own = to_slabs(place_windows(facts, own, slabs, columns, together=True)[0])
    own = jnp.sum(own.astype(f32), axis=0)

    total = lax.optimization_barrier((own + spill.astype(f32)).astype(bf16))
    total = to_four(sum_copies([total, swap(total, 8)], 4)).reshape(tile_rows, columns)
    new = step(core, layer, total)
    return step(1 - core, layer, swap(total, 1), new).reshape(volume.shape)


def solution(mesh):
    in_specs = (
        P(None, "slab", "tile", None),
        P(),
        P("angle", "tile", "slab", None, None, None),
        P("angle", "tile", "slab", None),
        P("angle", "tile", "slab", None),
        P("angle", "tile", "slab"),
        P("angle"),
    )
    out_specs = P(None, "slab", "tile", None)
    return jax.shard_map(
        per_device, mesh=mesh, in_specs=in_specs, out_specs=out_specs, check_vma=False
    )
```

```python
import functools

import jax
import jax.numpy as jnp
import ml_dtypes
import numpy as np
from jax import lax
from jax.experimental import pallas as pl
from jax.experimental.pallas import tpu as pltpu
from jax.sharding import PartitionSpec as P

angle_center = 600
shear_divisor = 64
step_size = 0.03
floor_square = 0.25

LANE = 128
CHUNK = 16
FOUR = 4


def dft_tables(plane_width):
    index_line = np.arange(plane_width, dtype=np.int32)
    product_mod = np.mod(index_line[:, None] * index_line[None, :], plane_width)
    phase_table = product_mod.astype(np.float32) * np.float32(2.0 * 3.141592653589793 / plane_width)
    scale_factor = np.float32(plane_width ** (-0.5))
    table_real = (np.cos(phase_table) * scale_factor).astype(ml_dtypes.bfloat16)
    table_imag = (-np.sin(phase_table) * scale_factor).astype(ml_dtypes.bfloat16)
    return table_real, table_imag


def dot(left, right):
    return jnp.dot(left, right, preferred_element_type=jnp.float32)


def one_hot(rows, columns, down):
    row = lax.broadcasted_iota(jnp.int32, (rows, columns), 0)
    column = lax.broadcasted_iota(jnp.int32, (rows, columns), 1)
    return (row - column == down).astype(jnp.float32).astype(jnp.bfloat16)


VMEM = pl.BlockSpec(memory_space=pltpu.VMEM)


def call(body, out_shape, scratch, *args):
    smem = pl.BlockSpec(memory_space=pltpu.SMEM)
    return pl.pallas_call(
        body,
        out_shape=out_shape,
        in_specs=[smem if x.dtype == jnp.int32 else VMEM for x in args],
        out_specs=[VMEM] * len(out_shape),
        scratch_shapes=scratch,
        compiler_params=pltpu.CompilerParams(vmem_limit_bytes=24 * 1024 * 1024),
    )(*args)


def facts_body(rows_in, columns_in, count_in, index_in, out, rows_ref, columns_ref, count_ref, index_ref, sems):
    pairs = zip((rows_in, columns_in, count_in, index_in), (rows_ref, columns_ref, count_ref, index_ref))
    copies = [pltpu.make_async_copy(ref, to, sems.at[n]) for n, (ref, to) in enumerate(pairs)]
    for copy in copies:
        copy.start()
    for copy in copies:
        copy.wait()
    values = []
    for slot in range(rows_ref.shape[0]):
        values += [rows_ref[slot], columns_ref[slot], (slot < count_ref[0]).astype(jnp.int32)]
    lane = lax.broadcasted_iota(jnp.int32, out.shape, 1)
    line = jnp.zeros(out.shape, jnp.int32)
    for n, value in enumerate(values + [index_ref[0]]):
        line = jnp.where(lane == n, value, line)
    out[...] = line


def facts_line(*args):
    return pl.pallas_call(
        facts_body,
        out_shape=jax.ShapeDtypeStruct((8, LANE), jnp.int32),
        in_specs=[pl.BlockSpec(memory_space=pltpu.HBM)] * len(args),
        out_specs=VMEM,
        scratch_shapes=[pltpu.SMEM(x.shape, jnp.int32) for x in args] + [pltpu.SemaphoreType.DMA((len(args),))],
    )(*args)


class Facts:
    def __init__(self, ref, slab_ref, slots, slabs, columns):
        self.ref, self.slab, self.slots, self.slabs, self.columns = ref, slab_ref[0], slots, slabs, columns

    def slot(self, angle, slot):
        return tuple(self.ref[angle, 3 * slot + i] for i in range(3))

    def layer(self, step):
        layer = self.slab + step
        layer = jnp.where(layer < 0, layer + self.slabs, layer)
        return jnp.where(layer >= self.slabs, layer - self.slabs, layer)

    def columns_of(self, angle, slot, layer):
        index = self.ref[angle, 3 * self.slots]
        shift = ((index - angle_center) * (layer - self.slabs // 2)) >> (shear_divisor.bit_length() - 1)
        left = self.slot(angle, slot)[1] + shift
        left = jnp.where(left < 0, left + self.columns, left)
        left = jnp.where(left >= self.columns, left - self.columns, left)
        starts = []
        for i in range(3):
            start = (left & -LANE) + i * LANE
            start = jnp.where(start >= self.columns, start - self.columns, start)
            starts.append(pl.multiple_of(start, LANE))
        return starts, left & (LANE - 1)


def needed(row, chunk, width, tile_rows):
    first = chunk * CHUNK
    return first + CHUNK > row, first + tile_rows < row + width


def cut_body(absolute, put, angles, slots, facts_ref, slab_ref, *refs):
    blocks, out = refs[:-1], refs[-1]
    rows = blocks[0].shape[0]
    facts = Facts(facts_ref, slab_ref, slots, len(blocks), blocks[0].shape[1])
    lane = lax.broadcasted_iota(jnp.int32, (rows, LANE), 1)
    for slot in range(slots):
        for angle in range(angles):

            @pl.when(facts.slot(angle, slot)[2] > 0)
            def _():
                total = [jnp.zeros((rows, LANE), jnp.float32)] * 2
                for k, block in enumerate(blocks):
                    layer = k if absolute else facts.layer(-k)
                    starts, inside = facts.columns_of(angle, slot, layer)
                    turned = [
                        pltpu.roll(block[:, pl.ds(start, LANE)].astype(jnp.float32), (LANE - inside) & (LANE - 1), 1)
                        for start in starts
                    ]
                    here = lane < LANE - inside
                    total = [t + jnp.where(here, turned[i], turned[i + 1]) for i, t in enumerate(total)]
                put(out, angle, slot, jnp.concatenate(total, axis=1).astype(jnp.bfloat16))


def cut_windows(facts, blocks, angles, slots, width):
    out = jax.ShapeDtypeStruct((angles, slots, blocks[0].shape[0], width), jnp.bfloat16)

    def put(out, angle, slot, window):
        out[angle, slot] = window

    return call(functools.partial(cut_body, False, put, angles, slots), [out], [], *facts, *blocks)[0]


def cut_rest(facts, place_z, blocks, done, tile_rows):
    angles, slots, rows, width = done.shape
    chunks = rows // CHUNK
    out = jax.ShapeDtypeStruct((angles, slots, chunks + 2, CHUNK, width), jnp.bfloat16)

    def body(place_ref, facts_ref, slab_ref, blocks, done, out):
        facts = Facts(facts_ref, slab_ref, slots, blocks.shape[0], blocks.shape[2])

        def put(out, angle, slot, window):
            row = facts.slot(angle, slot)[0]
            extra = chunks
            for i in range(chunks):
                own, after = needed(row, place_ref[0] + FOUR * i, width, tile_rows)
                piece = window[i * CHUNK : (i + 1) * CHUNK]
                out[angle, slot, i] = done[angle, slot, i * CHUNK : (i + 1) * CHUNK]

                @pl.when(jnp.logical_not(own))
                def _():
                    out[angle, slot, i] = piece

                both = jnp.logical_and(own, after)

                @pl.when(both)
                def _():
                    out[angle, slot, extra] = piece

                extra = extra + both.astype(jnp.int32)

        cut_body(
            True, put, angles, slots, facts_ref, slab_ref, *(blocks.at[k] for k in range(blocks.shape[0])), out
        )

    return call(body, [out], [], place_z, *facts, blocks, done)[0]


def cos_sin(angle):
    turns = jnp.round(angle * 0.6366197723675814)
    rest = angle - turns * 1.5703125
    rest = rest - turns * 4.837512969970703e-4
    rest = rest - turns * 7.549789948768648e-8
    square = rest * rest
    sine = (-1.9515295891e-4 * square + 8.3321608736e-3) * square - 1.6666654611e-1
    sine = sine * square * rest + rest
    cosine = (2.443315711809948e-5 * square - 1.388731625493765e-3) * square + 4.166664568298827e-2
    cosine = cosine * square * square - 0.5 * square + 1.0
    quarter = turns.astype(jnp.int32)
    odd = (quarter & 1) == 1
    first, second = jnp.where(odd, sine, cosine), jnp.where(odd, cosine, sine)
    return (
        jnp.where(((quarter + 1) & 2) == 2, -first, first),
        jnp.where((quarter & 2) == 2, -second, second),
    )


def patch_body(row_ref, count_ref, windows, probe, patterns, wr_ref, wi_ref, own_out, next_out):
    angles, slots, chunks, _, width = windows.shape
    chunks = chunks - 2
    tile_rows = FOUR * chunks * CHUNK
    f32, bf16 = jnp.float32, jnp.bfloat16
    tall = 2 * tile_rows
    for slot in range(slots):
        row = row_ref[slot]

        @pl.when(slot < count_ref[0])
        def _():
            pick = one_hot(width, tall, -row)
            window = []
            after_at = [[None] * FOUR for _ in range(chunks)]
            for k in range(FOUR):
                extra = chunks
                for i in range(chunks):
                    own, after = needed(row, k + FOUR * i, width, tile_rows)
                    both = jnp.logical_and(own, after)
                    after_at[i][k] = jnp.where(both, extra, i)
                    extra = extra + both.astype(jnp.int32)
            for part in range(2):
                order = [(i, k) for i in range(chunks) for k in range(FOUR)]
                held = [windows[2 * k + part, slot, i] for i, k in order]
                held += [windows[2 * k + part, slot, after_at[i][k]] for i, k in order]
                window.append(dot(pick, jnp.concatenate(held, axis=0)))
            phase, absorption = window
            magnitude = jnp.exp(-absorption)
            cosine, sine = cos_sin(phase)
            trans_real = magnitude * cosine
            trans_imag = magnitude * sine
            probe_real, probe_imag = probe[0], probe[1]
            wr, wi = wr_ref[...], wi_ref[...]
            wave_real = (probe_real * trans_real - probe_imag * trans_imag).astype(bf16)
            wave_imag = (probe_real * trans_imag + probe_imag * trans_real).astype(bf16)
            left_real = (dot(wr, wave_real) - dot(wi, wave_imag)).astype(bf16)
            left_imag = (dot(wr, wave_imag) + dot(wi, wave_real)).astype(bf16)
            far_real = dot(left_real, wr) - dot(left_imag, wi)
            far_imag = dot(left_real, wi) + dot(left_imag, wr)
            power = far_real * far_real + far_imag * far_imag + floor_square
            keeping = 1.0 - patterns[slot].astype(f32) * lax.rsqrt(power)
            resid_real = (far_real * keeping).astype(bf16)
            resid_imag = (far_imag * keeping).astype(bf16)
            back_real = (dot(wr, resid_real) + dot(wi, resid_imag)).astype(bf16)
            back_imag = (dot(wr, resid_imag) - dot(wi, resid_real)).astype(bf16)
            exit_real = dot(back_real, wr) + dot(back_imag, wi)
            exit_imag = dot(back_imag, wr) - dot(back_real, wi)
            mixed_real = probe_real * exit_real + probe_imag * exit_imag
            mixed_imag = probe_real * exit_imag - probe_imag * exit_real
            final_real = trans_real * mixed_real + trans_imag * mixed_imag
            final_imag = trans_real * mixed_imag - trans_imag * mixed_real
            put = one_hot(tall, width, row)
            for part, value in enumerate((final_imag, -final_real)):
                placed = dot(put, value.astype(bf16)).astype(bf16)
                for i, k in order:
                    at, first = slice(i * CHUNK, (i + 1) * CHUNK), (FOUR * i + k) * CHUNK
                    own_out[2 * k + part, slot, at] = placed[first : first + CHUNK]
                    below = placed[tile_rows + first : tile_rows + first + CHUNK]
                    next_out[2 * (FOUR - 1 - k) + part, slot, at] = below


def patch_gradients(slot_rows, count, windows, probe_wave, patterns, tables):
    angles, slots, chunks, _, width = windows.shape
    out = jax.ShapeDtypeStruct((angles, slots, (chunks - 2) * CHUNK, width), jnp.bfloat16)
    return call(patch_body, [out, out], [], slot_rows, count, windows, probe_wave, patterns, *tables)


def place_body(facts_ref, slab_ref, windows, *refs):
    outs, total = refs[:-1], refs[-1]
    angles, slots, rows, width = windows.shape
    slabs = total.shape[0]
    facts = Facts(facts_ref, slab_ref, slots, slabs, total.shape[2])
    lane = lax.broadcasted_iota(jnp.int32, (rows, LANE), 1)
    total[...] = jnp.zeros_like(total)
    for slot in range(slots):
        for angle in range(angles):

            @pl.when(facts.slot(angle, slot)[2] > 0)
            def _():
                window = windows[angle, slot].astype(jnp.float32)
                for k in range(slabs):
                    layer = facts.layer(k) if len(outs) > 1 else k
                    starts, inside = facts.columns_of(angle, slot, layer)
                    first, second = (pltpu.roll(window[:, i * LANE : (i + 1) * LANE], inside, 1) for i in range(2))
                    there = lane < inside
                    total[k, :, pl.ds(starts[0], LANE)] += jnp.where(there, 0.0, first)
                    total[k, :, pl.ds(starts[1], LANE)] += jnp.where(there, first, second)
                    total[k, :, pl.ds(starts[2], LANE)] += jnp.where(there, second, 0.0)
    for k, out in enumerate(outs):
        out[...] = (total[k] if len(outs) > 1 else total[...]).astype(out.dtype)


def place_windows(facts, windows, slabs, columns, together=False):
    shape = (windows.shape[2], columns)
    outs = [jax.ShapeDtypeStruct(shape, jnp.bfloat16 if k else jnp.float32) for k in range(slabs)]
    if together:
        outs = [jax.ShapeDtypeStruct((slabs, *shape), jnp.bfloat16)]
    return call(place_body, outs, [pltpu.VMEM((slabs, *shape), jnp.float32)], *facts, windows)


def sum_body(*refs):
    *terms, out = refs
    total = sum(term[...].astype(jnp.float32) for term in terms).astype(out.dtype)
    for k in range(out.shape[0]):
        out[k] = total


def sum_copies(terms, copies):
    out = jax.ShapeDtypeStruct((copies, *terms[0].shape), jnp.bfloat16)
    return call(sum_body, [out], [], *terms)[0]


def step_body(part_ref, layer, gradient, *refs):
    out, made, sems = refs[-3:]
    part = part_ref[0]
    chunks = gradient.shape[1] // CHUNK
    size = FOUR * CHUNK
    copies = []
    for i in range(chunks):
        for k in range(FOUR):
            rows = slice(i * size + k * CHUNK, i * size + (k + 1) * CHUNK)
            change = gradient[k, i * CHUNK : (i + 1) * CHUNK].astype(jnp.float32)
            made[rows] = layer[part, rows].astype(jnp.float32) - step_size * change
        at = pl.ds(i * size, size)
        copies.append(pltpu.make_async_copy(made.at[at], out.at[part, at], sems.at[i]))
        copies[-1].start()
    for copy in copies:
        copy.wait()


def step(part, layer, gradient, *stepped):
    return pl.pallas_call(
        step_body,
        out_shape=jax.ShapeDtypeStruct(layer.shape, jnp.float32),
        in_specs=[pl.BlockSpec(memory_space=pltpu.SMEM), VMEM, VMEM]
        + [pl.BlockSpec(memory_space=pltpu.HBM)] * len(stepped),
        out_specs=pl.BlockSpec(memory_space=pltpu.HBM),
        scratch_shapes=[pltpu.VMEM(layer.shape[1:], jnp.float32), pltpu.SemaphoreType.DMA((4,))],
        input_output_aliases={3: 0} if stepped else {},
        compiler_params=pltpu.CompilerParams(vmem_limit_bytes=24 * 1024 * 1024),
    )(part.reshape(1).astype(jnp.int32), layer, gradient, *stepped)


def per_device(volume, probe_wave, amplitudes, offsets, column_starts, counts, angle_ids):
    layer = volume.reshape(volume.shape[0], *volume.shape[2:])
    tile_rows, columns = layer.shape[1:]
    width = amplitudes.shape[-1]
    slots = offsets.shape[3]
    angles, slabs, tiles = (lax.axis_size(axis) for axis in ("angle", "slab", "tile"))
    slab, angle = lax.axis_index("slab"), lax.axis_index("angle")
    f32, bf16 = jnp.float32, jnp.bfloat16
    tables = dft_tables(width)
    patterns = amplitudes.reshape(slots, width, width)

    core, place_z = angle % 2, angle // 2 % 4
    eight_groups = [[8 * f + i for i in range(8)] for f in range(angles // 8)]
    four_groups = [[8 * f + 2 * q + c for q in range(4)] for f in range(angles // 8) for c in range(2)]
    block_rows = tile_rows // 4

    def swap(value, by):
        return lax.ppermute(value, "angle", [(i, i ^ by) for i in range(angles)])

    def mirrored(value, by):
        pairs = [
            (a * tiles + t, (angles - 2 - (a - a % 2) + a % 2) * tiles + t + by)
            for a in range(angles)
            for t in range(tiles)
            if 0 <= t + by < tiles
        ]
        return lax.ppermute(value, ("angle", "tile"), pairs)

    def to_slab(value, by):
        return lax.ppermute(value, "slab", [(i, (i + by) % slabs) for i in range(slabs)])

    def to_eight(value):
        return lax.all_to_all(value, "angle", 0, 0, axis_index_groups=eight_groups, tiled=True)

    def to_four(value):
        return lax.all_to_all(value, "angle", 0, 0, axis_index_groups=four_groups, tiled=True)

    def to_slabs(value):
        return lax.all_to_all(value, "slab", 0, 0, tiled=True)

    def of_slabs(block):
        return [block] + [to_slab(block, k) for k in range(1, slabs)]

    def over_slabs(kept, *sent):
        return sum((to_slab(block, k + 1).astype(f32) for k, block in enumerate(sent)), kept)

    def live_to_eight(value, axis):
        def first(value):
            sent = to_eight(lax.slice_in_dim(value, 0, 1, axis=axis))
            return jnp.concatenate([sent, lax.slice_in_dim(value, 1, slots, axis=axis)], axis=axis)

        return lax.cond(more, to_eight, first, value)

    own_part = lax.dynamic_index_in_dim(layer, core, 0, keepdims=False)

    own_part = own_part.reshape(-1, FOUR, CHUNK, columns)

    def rows_of(place):
        return lax.dynamic_index_in_dim(own_part, place, 1, keepdims=False).reshape(block_rows, columns)

    after = mirrored(rows_of(3 - place_z), -1)
    own = rows_of(place_z)

    slot_rows, count = offsets.reshape(slots), counts.reshape(1)
    meta = facts_line(slot_rows, column_starts.reshape(slots), count, angle_ids)
    eight = to_eight(meta)
    facts = (eight, slab.reshape(1).astype(jnp.int32))
    more = jnp.max(eight[:, 5 : 3 * slots : 3]) > 0
    own = of_slabs(own)
    after, own = lax.optimization_barrier((after, own))
    own = cut_windows(facts, own, 8, slots, width)
    after = to_slabs(jnp.broadcast_to(after, (slabs, *after.shape)))
    after, own = lax.optimization_barrier((after, own))
    place = place_z.reshape(1).astype(jnp.int32)
    windows = live_to_eight(cut_rest(facts, place, after, own, tile_rows), 1)

    own, after = patch_gradients(slot_rows, count, windows, probe_wave, patterns, tables)
    after, own = lax.optimization_barrier((live_to_eight(after, 1), own))
    own = to_eight(own)
    spill = mirrored(over_slabs(*place_windows(facts, after, slabs, columns)).astype(bf16), 1)
    own = to_slabs(place_windows(facts, own, slabs, columns, together=True)[0])
    own = jnp.sum(own.astype(f32), axis=0)

    total = lax.optimization_barrier((own + spill.astype(f32)).astype(bf16))
    total = to_four(sum_copies([total, swap(total, 8)], 4))
    new = step(core, layer, total)
    return step(1 - core, layer, swap(total, 1), new).reshape(volume.shape)


def solution(mesh):
    in_specs = (
        P(None, "slab", "tile", None),
        P(),
        P("angle", "tile", "slab", None, None, None),
        P("angle", "tile", "slab", None),
        P("angle", "tile", "slab", None),
        P("angle", "tile", "slab"),
        P("angle"),
    )
    out_specs = P(None, "slab", "tile", None)
    return jax.shard_map(
        per_device, mesh=mesh, in_specs=in_specs, out_specs=out_specs, check_vma=False
    )
```

```python
import functools

import jax
import jax.numpy as jnp
import ml_dtypes
import numpy as np
from jax import lax
from jax.experimental import pallas as pl
from jax.experimental.pallas import tpu as pltpu
from jax.sharding import PartitionSpec as P

angle_center = 600
shear_divisor = 64
step_size = 0.03
floor_square = 0.25

LANE = 128
CHUNK = 16
FOUR = 4


def dft_tables(plane_width):
    index_line = np.arange(plane_width, dtype=np.int32)
    product_mod = np.mod(index_line[:, None] * index_line[None, :], plane_width)
    phase_table = product_mod.astype(np.float32) * np.float32(2.0 * 3.141592653589793 / plane_width)
    scale_factor = np.float32(plane_width ** (-0.5))
    table_real = (np.cos(phase_table) * scale_factor).astype(ml_dtypes.bfloat16)
    table_imag = (-np.sin(phase_table) * scale_factor).astype(ml_dtypes.bfloat16)
    return table_real, table_imag


def dot(left, right):
    return jnp.dot(left, right, preferred_element_type=jnp.float32)


def one_hot(rows, columns, down):
    row = lax.broadcasted_iota(jnp.int32, (rows, columns), 0)
    column = lax.broadcasted_iota(jnp.int32, (rows, columns), 1)
    return (row - column == down).astype(jnp.float32).astype(jnp.bfloat16)


VMEM = pl.BlockSpec(memory_space=pltpu.VMEM)


def call(body, out_shape, scratch, *args):
    smem = pl.BlockSpec(memory_space=pltpu.SMEM)
    return pl.pallas_call(
        body,
        out_shape=out_shape,
        in_specs=[smem if x.dtype == jnp.int32 else VMEM for x in args],
        out_specs=[VMEM] * len(out_shape),
        scratch_shapes=scratch,
        compiler_params=pltpu.CompilerParams(vmem_limit_bytes=24 * 1024 * 1024),
    )(*args)


def facts_body(rows_in, columns_in, count_in, index_in, out, rows_ref, columns_ref, count_ref, index_ref, sems):
    pairs = zip((rows_in, columns_in, count_in, index_in), (rows_ref, columns_ref, count_ref, index_ref))
    copies = [pltpu.make_async_copy(ref, to, sems.at[n]) for n, (ref, to) in enumerate(pairs)]
    for copy in copies:
        copy.start()
    for copy in copies:
        copy.wait()
    values = []
    for slot in range(rows_ref.shape[0]):
        values += [rows_ref[slot], columns_ref[slot], (slot < count_ref[0]).astype(jnp.int32)]
    lane = lax.broadcasted_iota(jnp.int32, out.shape, 1)
    line = jnp.zeros(out.shape, jnp.int32)
    for n, value in enumerate(values + [index_ref[0]]):
        line = jnp.where(lane == n, value, line)
    out[...] = line


def facts_line(*args):
    return pl.pallas_call(
        facts_body,
        out_shape=jax.ShapeDtypeStruct((8, LANE), jnp.int32),
        in_specs=[pl.BlockSpec(memory_space=pltpu.HBM)] * len(args),
        out_specs=VMEM,
        scratch_shapes=[pltpu.SMEM(x.shape, jnp.int32) for x in args] + [pltpu.SemaphoreType.DMA((len(args),))],
    )(*args)


class Facts:
    def __init__(self, ref, slab_ref, slots, slabs, columns):
        self.ref, self.slab, self.slots, self.slabs, self.columns = ref, slab_ref[0], slots, slabs, columns

    def slot(self, angle, slot):
        return tuple(self.ref[angle, 3 * slot + i] for i in range(3))

    def layer(self, step):
        layer = self.slab + step
        layer = jnp.where(layer < 0, layer + self.slabs, layer)
        return jnp.where(layer >= self.slabs, layer - self.slabs, layer)

    def columns_of(self, angle, slot, layer):
        index = self.ref[angle, 3 * self.slots]
        shift = ((index - angle_center) * (layer - self.slabs // 2)) >> (shear_divisor.bit_length() - 1)
        left = self.slot(angle, slot)[1] + shift
        left = jnp.where(left < 0, left + self.columns, left)
        left = jnp.where(left >= self.columns, left - self.columns, left)
        starts = []
        for i in range(3):
            start = (left & -LANE) + i * LANE
            start = jnp.where(start >= self.columns, start - self.columns, start)
            starts.append(pl.multiple_of(start, LANE))
        return starts, left & (LANE - 1)


def needed(row, chunk, width, tile_rows):
    first = chunk * CHUNK
    return first + CHUNK > row, first + tile_rows < row + width


def cut_body(absolute, put, angles, slots, facts_ref, slab_ref, *refs):
    blocks, out = refs[:-1], refs[-1]
    rows = blocks[0].shape[0]
    facts = Facts(facts_ref, slab_ref, slots, len(blocks), blocks[0].shape[1])
    lane = lax.broadcasted_iota(jnp.int32, (rows, LANE), 1)
    for slot in range(slots):
        for angle in range(angles):

            @pl.when(facts.slot(angle, slot)[2] > 0)
            def _():
                total = [jnp.zeros((rows, LANE), jnp.float32)] * 2
                for k, block in enumerate(blocks):
                    layer = k if absolute else facts.layer(-k)
                    starts, inside = facts.columns_of(angle, slot, layer)
                    turned = [
                        pltpu.roll(block[:, pl.ds(start, LANE)], (LANE - inside) & (LANE - 1), 1)
                        for start in starts
                    ]
                    here = lane < LANE - inside
                    total = [
                        t + jnp.where(here, turned[i], turned[i + 1]).astype(jnp.float32)
                        for i, t in enumerate(total)
                    ]
                put(out, angle, slot, jnp.concatenate(total, axis=1).astype(jnp.bfloat16))


def cut_windows(facts, blocks, angles, slots, width):
    out = jax.ShapeDtypeStruct((angles, slots, blocks[0].shape[0], width), jnp.bfloat16)

    def put(out, angle, slot, window):
        out[angle, slot] = window

    return call(functools.partial(cut_body, False, put, angles, slots), [out], [], *facts, *blocks)[0]


def cut_rest(facts, place_z, blocks, done, tile_rows):
    angles, slots, rows, width = done.shape
    chunks = rows // CHUNK
    out = jax.ShapeDtypeStruct((angles, slots, chunks + 2, CHUNK, width), jnp.bfloat16)

    def body(place_ref, facts_ref, slab_ref, blocks, done, out):
        facts = Facts(facts_ref, slab_ref, slots, blocks.shape[0], blocks.shape[2])

        def put(out, angle, slot, window):
            row = facts.slot(angle, slot)[0]
            extra = chunks
            for i in range(chunks):
                own, after = needed(row, place_ref[0] + FOUR * i, width, tile_rows)
                piece = window[i * CHUNK : (i + 1) * CHUNK]
                out[angle, slot, i] = done[angle, slot, i * CHUNK : (i + 1) * CHUNK]

                @pl.when(jnp.logical_not(own))
                def _():
                    out[angle, slot, i] = piece

                both = jnp.logical_and(own, after)

                @pl.when(both)
                def _():
                    out[angle, slot, extra] = piece

                extra = extra + both.astype(jnp.int32)

        cut_body(
            True, put, angles, slots, facts_ref, slab_ref, *(blocks.at[k] for k in range(blocks.shape[0])), out
        )

    return call(body, [out], [], place_z, *facts, blocks, done)[0]


def cos_sin(angle):
    turns = jnp.round(angle * 0.6366197723675814)
    rest = angle - turns * 1.5703125
    rest = rest - turns * 4.837512969970703e-4
    rest = rest - turns * 7.549789948768648e-8
    square = rest * rest
    sine = (-1.9515295891e-4 * square + 8.3321608736e-3) * square - 1.6666654611e-1
    sine = sine * square * rest + rest
    cosine = (2.443315711809948e-5 * square - 1.388731625493765e-3) * square + 4.166664568298827e-2
    cosine = cosine * square * square - 0.5 * square + 1.0
    quarter = turns.astype(jnp.int32)
    odd = (quarter & 1) == 1
    first, second = jnp.where(odd, sine, cosine), jnp.where(odd, cosine, sine)
    return (
        jnp.where(((quarter + 1) & 2) == 2, -first, first),
        jnp.where((quarter & 2) == 2, -second, second),
    )


def patch_body(row_ref, count_ref, windows, probe, patterns, wr_ref, wi_ref, own_out, next_out):
    angles, slots, chunks, _, width = windows.shape
    chunks = chunks - 2
    tile_rows = FOUR * chunks * CHUNK
    f32, bf16 = jnp.float32, jnp.bfloat16
    tall = 2 * tile_rows
    for slot in range(slots):
        row = row_ref[slot]

        @pl.when(slot < count_ref[0])
        def _():
            pick = one_hot(width, tall, -row)
            window = []
            after_at = [[None] * FOUR for _ in range(chunks)]
            for k in range(FOUR):
                extra = chunks
                for i in range(chunks):
                    own, after = needed(row, k + FOUR * i, width, tile_rows)
                    both = jnp.logical_and(own, after)
                    after_at[i][k] = jnp.where(both, extra, i)
                    extra = extra + both.astype(jnp.int32)
            for part in range(2):
                order = [(i, k) for i in range(chunks) for k in range(FOUR)]
                held = [windows[2 * k + part, slot, i] for i, k in order]
                held += [windows[2 * k + part, slot, after_at[i][k]] for i, k in order]
                window.append(dot(pick, jnp.concatenate(held, axis=0)))
            phase, absorption = window
            magnitude = jnp.exp(-absorption)
            cosine, sine = cos_sin(phase)
            trans_real = magnitude * cosine
            trans_imag = magnitude * sine
            probe_real, probe_imag = probe[0], probe[1]
            wr, wi = wr_ref[...], wi_ref[...]
            wave_real = (probe_real * trans_real - probe_imag * trans_imag).astype(bf16)
            wave_imag = (probe_real * trans_imag + probe_imag * trans_real).astype(bf16)
            left_real = (dot(wr, wave_real) - dot(wi, wave_imag)).astype(bf16)
            left_imag = (dot(wr, wave_imag) + dot(wi, wave_real)).astype(bf16)
            far_real = dot(left_real, wr) - dot(left_imag, wi)
            far_imag = dot(left_real, wi) + dot(left_imag, wr)
            power = far_real * far_real + far_imag * far_imag + floor_square
            keeping = 1.0 - patterns[slot].astype(f32) * lax.rsqrt(power)
            resid_real = (far_real * keeping).astype(bf16)
            resid_imag = (far_imag * keeping).astype(bf16)
            back_real = (dot(wr, resid_real) + dot(wi, resid_imag)).astype(bf16)
            back_imag = (dot(wr, resid_imag) - dot(wi, resid_real)).astype(bf16)
            exit_real = dot(back_real, wr) + dot(back_imag, wi)
            exit_imag = dot(back_imag, wr) - dot(back_real, wi)
            mixed_real = probe_real * exit_real + probe_imag * exit_imag
            mixed_imag = probe_real * exit_imag - probe_imag * exit_real
            final_real = trans_real * mixed_real + trans_imag * mixed_imag
            final_imag = trans_real * mixed_imag - trans_imag * mixed_real
            put = one_hot(tall, width, row)
            for part, value in enumerate((final_imag, -final_real)):
                placed = dot(put, value.astype(bf16)).astype(bf16)
                for i, k in order:
                    at, first = slice(i * CHUNK, (i + 1) * CHUNK), (FOUR * i + k) * CHUNK
                    own_out[2 * k + part, slot, at] = placed[first : first + CHUNK]
                    below = placed[tile_rows + first : tile_rows + first + CHUNK]
                    next_out[2 * (FOUR - 1 - k) + part, slot, at] = below


def patch_gradients(slot_rows, count, windows, probe_wave, patterns, tables):
    angles, slots, chunks, _, width = windows.shape
    out = jax.ShapeDtypeStruct((angles, slots, (chunks - 2) * CHUNK, width), jnp.bfloat16)
    return call(patch_body, [out, out], [], slot_rows, count, windows, probe_wave, patterns, *tables)


def place_body(facts_ref, slab_ref, windows, *refs):
    outs, total = refs[:-1], refs[-1]
    angles, slots, rows, width = windows.shape
    slabs = total.shape[0]
    facts = Facts(facts_ref, slab_ref, slots, slabs, total.shape[2])
    lane = lax.broadcasted_iota(jnp.int32, (rows, LANE), 1)
    total[...] = jnp.zeros_like(total)
    for slot in range(slots):
        for angle in range(angles):

            @pl.when(facts.slot(angle, slot)[2] > 0)
            def _():
                window = windows[angle, slot].astype(jnp.float32)
                for k in range(slabs):
                    layer = facts.layer(k) if len(outs) > 1 else k
                    starts, inside = facts.columns_of(angle, slot, layer)
                    first, second = (pltpu.roll(window[:, i * LANE : (i + 1) * LANE], inside, 1) for i in range(2))
                    there = lane < inside
                    total[k, :, pl.ds(starts[0], LANE)] += jnp.where(there, 0.0, first)
                    total[k, :, pl.ds(starts[1], LANE)] += jnp.where(there, first, second)
                    total[k, :, pl.ds(starts[2], LANE)] += jnp.where(there, second, 0.0)
    for k, out in enumerate(outs):
        out[...] = (total[k] if len(outs) > 1 else total[...]).astype(out.dtype)


def place_windows(facts, windows, slabs, columns, together=False):
    shape = (windows.shape[2], columns)
    outs = [jax.ShapeDtypeStruct(shape, jnp.bfloat16 if k else jnp.float32) for k in range(slabs)]
    if together:
        outs = [jax.ShapeDtypeStruct((slabs, *shape), jnp.bfloat16)]
    return call(place_body, outs, [pltpu.VMEM((slabs, *shape), jnp.float32)], *facts, windows)


def sum_body(*refs):
    *terms, out = refs
    total = terms[0][...]
    if len(terms) > 1:
        total = sum(term[...].astype(jnp.float32) for term in terms).astype(out.dtype)
    for k in range(out.shape[0]):
        out[k] = total


def sum_copies(terms, copies):
    out = jax.ShapeDtypeStruct((copies, *terms[0].shape), jnp.bfloat16)
    return call(sum_body, [out], [], *terms)[0]


def step_body(part_ref, layer, gradient, *refs):
    out, made, sems = refs[-3:]
    part = part_ref[0]
    chunks = gradient.shape[1] // CHUNK
    size = FOUR * CHUNK
    copies = []
    for i in range(chunks):
        for k in range(FOUR):
            rows = slice(i * size + k * CHUNK, i * size + (k + 1) * CHUNK)
            change = gradient[k, i * CHUNK : (i + 1) * CHUNK].astype(jnp.float32)
            made[rows] = layer[part, rows].astype(jnp.float32) - step_size * change
        at = pl.ds(i * size, size)
        copies.append(pltpu.make_async_copy(made.at[at], out.at[part, at], sems.at[i]))
        copies[-1].start()
    for copy in copies:
        copy.wait()


def step(part, layer, gradient, *stepped):
    return pl.pallas_call(
        step_body,
        out_shape=jax.ShapeDtypeStruct(layer.shape, jnp.float32),
        in_specs=[pl.BlockSpec(memory_space=pltpu.SMEM), VMEM, VMEM]
        + [pl.BlockSpec(memory_space=pltpu.HBM)] * len(stepped),
        out_specs=pl.BlockSpec(memory_space=pltpu.HBM),
        scratch_shapes=[pltpu.VMEM(layer.shape[1:], jnp.float32), pltpu.SemaphoreType.DMA((4,))],
        input_output_aliases={3: 0} if stepped else {},
        compiler_params=pltpu.CompilerParams(vmem_limit_bytes=24 * 1024 * 1024),
    )(part.reshape(1).astype(jnp.int32), layer, gradient, *stepped)


def per_device(volume, probe_wave, amplitudes, offsets, column_starts, counts, angle_ids):
    layer = volume.reshape(volume.shape[0], *volume.shape[2:])
    tile_rows, columns = layer.shape[1:]
    width = amplitudes.shape[-1]
    slots = offsets.shape[3]
    angles, slabs, tiles = (lax.axis_size(axis) for axis in ("angle", "slab", "tile"))
    slab, angle = lax.axis_index("slab"), lax.axis_index("angle")
    f32, bf16 = jnp.float32, jnp.bfloat16
    tables = dft_tables(width)
    patterns = amplitudes.reshape(slots, width, width)

    core, place_z = angle % 2, angle // 2 % 4
    eight_groups = [[8 * f + i for i in range(8)] for f in range(angles // 8)]
    four_groups = [[8 * f + 2 * q + c for q in range(4)] for f in range(angles // 8) for c in range(2)]
    block_rows = tile_rows // 4

    def swap(value, by):
        return lax.ppermute(value, "angle", [(i, i ^ by) for i in range(angles)])

    def mirrored(value, by):
        pairs = [
            (a * tiles + t, (angles - 2 - (a - a % 2) + a % 2) * tiles + t + by)
            for a in range(angles)
            for t in range(tiles)
            if 0 <= t + by < tiles
        ]
        return lax.ppermute(value, ("angle", "tile"), pairs)

    def to_slab(value, by):
        return lax.ppermute(value, "slab", [(i, (i + by) % slabs) for i in range(slabs)])

    def to_eight(value):
        return lax.all_to_all(value, "angle", 0, 0, axis_index_groups=eight_groups, tiled=True)

    def to_four(value):
        return lax.all_to_all(value, "angle", 0, 0, axis_index_groups=four_groups, tiled=True)

    def to_slabs(value):
        return lax.all_to_all(value, "slab", 0, 0, tiled=True)

    def of_slabs(block):
        return [block] + [to_slab(block, k) for k in range(1, slabs)]

    def over_slabs(kept, *sent):
        return sum((to_slab(block, k + 1).astype(f32) for k, block in enumerate(sent)), kept)

    def live_to_eight(value, axis):
        def first(value):
            sent = to_eight(lax.slice_in_dim(value, 0, 1, axis=axis))
            return jnp.concatenate([sent, lax.slice_in_dim(value, 1, slots, axis=axis)], axis=axis)

        return lax.cond(more, to_eight, first, value)

    own_part = lax.dynamic_index_in_dim(layer, core, 0, keepdims=False)

    own_part = own_part.reshape(-1, FOUR, CHUNK, columns)

    def rows_of(place):
        return lax.dynamic_index_in_dim(own_part, place, 1, keepdims=False).reshape(block_rows, columns)

    after = mirrored(rows_of(3 - place_z), -1)
    own = rows_of(place_z)

    slot_rows, count = offsets.reshape(slots), counts.reshape(1)
    meta = facts_line(slot_rows, column_starts.reshape(slots), count, angle_ids)
    eight = to_eight(meta)
    facts = (eight, slab.reshape(1).astype(jnp.int32))
    more = jnp.max(eight[:, 5 : 3 * slots : 3]) > 0
    own = of_slabs(own)
    after, own = lax.optimization_barrier((after, own))
    own = cut_windows(facts, own, 8, slots, width)
    after = to_slabs(sum_copies([after], slabs))
    after, own = lax.optimization_barrier((after, own))
    place = place_z.reshape(1).astype(jnp.int32)
    windows = live_to_eight(cut_rest(facts, place, after, own, tile_rows), 1)

    own, after = patch_gradients(slot_rows, count, windows, probe_wave, patterns, tables)
    after, own = lax.optimization_barrier((live_to_eight(after, 1), own))
    own = to_eight(own)
    spill = mirrored(over_slabs(*place_windows(facts, after, slabs, columns)).astype(bf16), 1)
    own = to_slabs(place_windows(facts, own, slabs, columns, together=True)[0])
    own = jnp.sum(own.astype(f32), axis=0)

    total = lax.optimization_barrier((own + spill.astype(f32)).astype(bf16))
    total = to_four(sum_copies([total, swap(total, 8)], 4))
    new = step(core, layer, total)
    return step(1 - core, layer, swap(total, 1), new).reshape(volume.shape)


def solution(mesh):
    in_specs = (
        P(None, "slab", "tile", None),
        P(),
        P("angle", "tile", "slab", None, None, None),
        P("angle", "tile", "slab", None),
        P("angle", "tile", "slab", None),
        P("angle", "tile", "slab"),
        P("angle"),
    )
    out_specs = P(None, "slab", "tile", None)
    return jax.shard_map(
        per_device, mesh=mesh, in_specs=in_specs, out_specs=out_specs, check_vma=False
    )
```

```python
import functools

import jax
import jax.numpy as jnp
import ml_dtypes
import numpy as np
from jax import lax
from jax.experimental import pallas as pl
from jax.experimental.pallas import tpu as pltpu
from jax.sharding import PartitionSpec as P

angle_center = 600
shear_divisor = 64
step_size = 0.03
floor_square = 0.25

LANE = 128
CHUNK = 16
FOUR = 4


def dft_tables(plane_width):
    index_line = np.arange(plane_width, dtype=np.int32)
    product_mod = np.mod(index_line[:, None] * index_line[None, :], plane_width)
    phase_table = product_mod.astype(np.float32) * np.float32(2.0 * 3.141592653589793 / plane_width)
    scale_factor = np.float32(plane_width ** (-0.5))
    table_real = (np.cos(phase_table) * scale_factor).astype(ml_dtypes.bfloat16)
    table_imag = (-np.sin(phase_table) * scale_factor).astype(ml_dtypes.bfloat16)
    return table_real, table_imag


def dot(left, right):
    return jnp.dot(left, right, preferred_element_type=jnp.float32)


def one_hot(rows, columns, down):
    row = lax.broadcasted_iota(jnp.int32, (rows, columns), 0)
    column = lax.broadcasted_iota(jnp.int32, (rows, columns), 1)
    return (row - column == down).astype(jnp.float32).astype(jnp.bfloat16)


VMEM = pl.BlockSpec(memory_space=pltpu.VMEM)


def call(body, out_shape, scratch, *args):
    smem = pl.BlockSpec(memory_space=pltpu.SMEM)
    return pl.pallas_call(
        body,
        out_shape=out_shape,
        in_specs=[smem if x.dtype == jnp.int32 else VMEM for x in args],
        out_specs=[VMEM] * len(out_shape),
        scratch_shapes=scratch,
        compiler_params=pltpu.CompilerParams(vmem_limit_bytes=24 * 1024 * 1024),
    )(*args)


def facts_body(rows_in, columns_in, count_in, index_in, out, rows_ref, columns_ref, count_ref, index_ref, sems):
    pairs = zip((rows_in, columns_in, count_in, index_in), (rows_ref, columns_ref, count_ref, index_ref))
    copies = [pltpu.make_async_copy(ref, to, sems.at[n]) for n, (ref, to) in enumerate(pairs)]
    for copy in copies:
        copy.start()
    for copy in copies:
        copy.wait()
    values = []
    for slot in range(rows_ref.shape[0]):
        values += [rows_ref[slot], columns_ref[slot], (slot < count_ref[0]).astype(jnp.int32)]
    lane = lax.broadcasted_iota(jnp.int32, out.shape, 1)
    line = jnp.zeros(out.shape, jnp.int32)
    for n, value in enumerate(values + [index_ref[0]]):
        line = jnp.where(lane == n, value, line)
    out[...] = line


def facts_line(*args):
    return pl.pallas_call(
        facts_body,
        out_shape=jax.ShapeDtypeStruct((8, LANE), jnp.int32),
        in_specs=[pl.BlockSpec(memory_space=pltpu.HBM)] * len(args),
        out_specs=VMEM,
        scratch_shapes=[pltpu.SMEM(x.shape, jnp.int32) for x in args] + [pltpu.SemaphoreType.DMA((len(args),))],
    )(*args)


class Facts:
    def __init__(self, ref, slab_ref, slots, slabs, columns):
        self.ref, self.slab, self.slots, self.slabs, self.columns = ref, slab_ref[0], slots, slabs, columns

    def slot(self, angle, slot):
        return tuple(self.ref[angle, 3 * slot + i] for i in range(3))

    def layer(self, step):
        layer = self.slab + step
        layer = jnp.where(layer < 0, layer + self.slabs, layer)
        return jnp.where(layer >= self.slabs, layer - self.slabs, layer)

    def columns_of(self, angle, slot, layer):
        index = self.ref[angle, 3 * self.slots]
        shift = ((index - angle_center) * (layer - self.slabs // 2)) >> (shear_divisor.bit_length() - 1)
        left = self.slot(angle, slot)[1] + shift
        left = jnp.where(left < 0, left + self.columns, left)
        left = jnp.where(left >= self.columns, left - self.columns, left)
        starts = []
        for i in range(3):
            start = (left & -LANE) + i * LANE
            start = jnp.where(start >= self.columns, start - self.columns, start)
            starts.append(pl.multiple_of(start, LANE))
        return starts, left & (LANE - 1)


def needed(row, chunk, width, tile_rows):
    first = chunk * CHUNK
    return first + CHUNK > row, first + tile_rows < row + width


def cut_body(absolute, put, angles, slots, facts_ref, slab_ref, *refs):
    blocks, out = refs[:-1], refs[-1]
    rows = blocks[0].shape[0]
    facts = Facts(facts_ref, slab_ref, slots, len(blocks), blocks[0].shape[1])
    lane = lax.broadcasted_iota(jnp.int32, (rows, LANE), 1)
    for slot in range(slots):
        for angle in range(angles):

            @pl.when(facts.slot(angle, slot)[2] > 0)
            def _():
                total = [jnp.zeros((rows, LANE), jnp.float32)] * 2
                for k, block in enumerate(blocks):
                    layer = k if absolute else facts.layer(-k)
                    starts, inside = facts.columns_of(angle, slot, layer)
                    turned = [
                        pltpu.roll(block[:, pl.ds(start, LANE)], (LANE - inside) & (LANE - 1), 1)
                        for start in starts
                    ]
                    here = lane < LANE - inside
                    total = [
                        t + jnp.where(here, turned[i], turned[i + 1]).astype(jnp.float32)
                        for i, t in enumerate(total)
                    ]
                put(out, angle, slot, jnp.concatenate(total, axis=1).astype(jnp.bfloat16))


def cut_windows(facts, blocks, angles, slots, width):
    out = jax.ShapeDtypeStruct((angles, slots, blocks[0].shape[0], width), jnp.bfloat16)

    def put(out, angle, slot, window):
        out[angle, slot] = window

    return call(functools.partial(cut_body, False, put, angles, slots), [out], [], *facts, *blocks)[0]


def cut_rest(facts, place_z, blocks, done, tile_rows):
    angles, slots, rows, width = done.shape
    chunks = rows // CHUNK
    out = jax.ShapeDtypeStruct((angles, slots, chunks + 2, CHUNK, width), jnp.bfloat16)

    def body(place_ref, facts_ref, slab_ref, blocks, done, out):
        facts = Facts(facts_ref, slab_ref, slots, blocks.shape[0], blocks.shape[2])

        def put(out, angle, slot, window):
            row = facts.slot(angle, slot)[0]
            extra = chunks
            for i in range(chunks):
                own, after = needed(row, place_ref[0] + FOUR * i, width, tile_rows)
                piece = window[i * CHUNK : (i + 1) * CHUNK]
                out[angle, slot, i] = done[angle, slot, i * CHUNK : (i + 1) * CHUNK]

                @pl.when(jnp.logical_not(own))
                def _():
                    out[angle, slot, i] = piece

                both = jnp.logical_and(own, after)

                @pl.when(both)
                def _():
                    out[angle, slot, extra] = piece

                extra = extra + both.astype(jnp.int32)

        cut_body(
            True, put, angles, slots, facts_ref, slab_ref, *(blocks.at[k] for k in range(blocks.shape[0])), out
        )

    return call(body, [out], [], place_z, *facts, blocks, done)[0]


def cos_sin(angle):
    turns = jnp.round(angle * 0.6366197723675814)
    rest = angle - turns * 1.5703125
    rest = rest - turns * 4.837512969970703e-4
    rest = rest - turns * 7.549789948768648e-8
    square = rest * rest
    sine = (-1.9515295891e-4 * square + 8.3321608736e-3) * square - 1.6666654611e-1
    sine = sine * square * rest + rest
    cosine = (2.443315711809948e-5 * square - 1.388731625493765e-3) * square + 4.166664568298827e-2
    cosine = cosine * square * square - 0.5 * square + 1.0
    quarter = turns.astype(jnp.int32)
    odd = (quarter & 1) == 1
    first, second = jnp.where(odd, sine, cosine), jnp.where(odd, cosine, sine)
    return (
        jnp.where(((quarter + 1) & 2) == 2, -first, first),
        jnp.where((quarter & 2) == 2, -second, second),
    )


def patch_body(row_ref, count_ref, windows, probe, patterns, wr_ref, wi_ref, own_out, next_out):
    angles, slots, chunks, _, width = windows.shape
    chunks = chunks - 2
    tile_rows = FOUR * chunks * CHUNK
    f32, bf16 = jnp.float32, jnp.bfloat16
    tall = 2 * tile_rows
    for slot in range(slots):
        row = row_ref[slot]

        @pl.when(slot < count_ref[0])
        def _():
            pick = one_hot(width, tall, -row)
            window = []
            after_at = [[None] * FOUR for _ in range(chunks)]
            for k in range(FOUR):
                extra = chunks
                for i in range(chunks):
                    own, after = needed(row, k + FOUR * i, width, tile_rows)
                    both = jnp.logical_and(own, after)
                    after_at[i][k] = jnp.where(both, extra, i)
                    extra = extra + both.astype(jnp.int32)
            for part in range(2):
                order = [(i, k) for i in range(chunks) for k in range(FOUR)]
                held = [windows[2 * k + part, slot, i] for i, k in order]
                held += [windows[2 * k + part, slot, after_at[i][k]] for i, k in order]
                window.append(dot(pick, jnp.concatenate(held, axis=0)))
            phase, absorption = window
            magnitude = jnp.exp(-absorption)
            cosine, sine = cos_sin(phase)
            trans_real = magnitude * cosine
            trans_imag = magnitude * sine
            probe_real, probe_imag = probe[0], probe[1]
            wr, wi = wr_ref[...], wi_ref[...]
            wave_real = (probe_real * trans_real - probe_imag * trans_imag).astype(bf16)
            wave_imag = (probe_real * trans_imag + probe_imag * trans_real).astype(bf16)
            left_real = (dot(wr, wave_real) - dot(wi, wave_imag)).astype(bf16)
            left_imag = (dot(wr, wave_imag) + dot(wi, wave_real)).astype(bf16)
            far_real = dot(left_real, wr) - dot(left_imag, wi)
            far_imag = dot(left_real, wi) + dot(left_imag, wr)
            power = far_real * far_real + far_imag * far_imag + floor_square
            keeping = 1.0 - patterns[slot].astype(f32) * lax.rsqrt(power)
            resid_real = (far_real * keeping).astype(bf16)
            resid_imag = (far_imag * keeping).astype(bf16)
            back_real = (dot(wr, resid_real) + dot(wi, resid_imag)).astype(bf16)
            back_imag = (dot(wr, resid_imag) - dot(wi, resid_real)).astype(bf16)
            exit_real = dot(back_real, wr) + dot(back_imag, wi)
            exit_imag = dot(back_imag, wr) - dot(back_real, wi)
            mixed_real = probe_real * exit_real + probe_imag * exit_imag
            mixed_imag = probe_real * exit_imag - probe_imag * exit_real
            final_real = trans_real * mixed_real + trans_imag * mixed_imag
            final_imag = trans_real * mixed_imag - trans_imag * mixed_real
            put = one_hot(tall, width, row)
            for part, value in enumerate((final_imag, -final_real)):
                placed = dot(put, value.astype(bf16)).astype(bf16)
                for i, k in order:
                    at, first = slice(i * CHUNK, (i + 1) * CHUNK), (FOUR * i + k) * CHUNK
                    own_out[2 * k + part, slot, at] = placed[first : first + CHUNK]
                    below = placed[tile_rows + first : tile_rows + first + CHUNK]
                    next_out[2 * (FOUR - 1 - k) + part, slot, at] = below


def patch_gradients(slot_rows, count, windows, probe_wave, patterns, tables):
    angles, slots, chunks, _, width = windows.shape
    out = jax.ShapeDtypeStruct((angles, slots, (chunks - 2) * CHUNK, width), jnp.bfloat16)
    return call(patch_body, [out, out], [], slot_rows, count, windows, probe_wave, patterns, *tables)


def place_body(facts_ref, slab_ref, windows, *refs):
    outs, total = refs[:-1], refs[-1]
    angles, slots, rows, width = windows.shape
    slabs = total.shape[0]
    facts = Facts(facts_ref, slab_ref, slots, slabs, total.shape[2])
    lane = lax.broadcasted_iota(jnp.int32, (rows, LANE), 1)
    total[...] = jnp.zeros_like(total)
    for slot in range(slots):
        for angle in range(angles):

            @pl.when(facts.slot(angle, slot)[2] > 0)
            def _():
                window = windows[angle, slot].astype(jnp.float32)
                for k in range(slabs):
                    layer = facts.layer(k) if len(outs) > 1 else k
                    starts, inside = facts.columns_of(angle, slot, layer)
                    first, second = (pltpu.roll(window[:, i * LANE : (i + 1) * LANE], inside, 1) for i in range(2))
                    there = lane < inside
                    total[k, :, pl.ds(starts[0], LANE)] += jnp.where(there, 0.0, first)
                    total[k, :, pl.ds(starts[1], LANE)] += jnp.where(there, first, second)
                    total[k, :, pl.ds(starts[2], LANE)] += jnp.where(there, second, 0.0)
    for k, out in enumerate(outs):
        out[...] = (total[k] if len(outs) > 1 else total[...]).astype(out.dtype)


def place_windows(facts, windows, slabs, columns, together=False):
    shape = (windows.shape[2], columns)
    outs = [jax.ShapeDtypeStruct(shape, jnp.bfloat16 if k else jnp.float32) for k in range(slabs)]
    if together:
        outs = [jax.ShapeDtypeStruct((slabs, *shape), jnp.bfloat16)]
    return call(place_body, outs, [pltpu.VMEM((slabs, *shape), jnp.float32)], *facts, windows)


def sum_body(*refs):
    *terms, out = refs
    total = terms[0][...]
    if len(terms) > 1:
        total = sum(term[...].astype(jnp.float32) for term in terms).astype(out.dtype)
    for k in range(out.shape[0]):
        out[k] = total


def sum_copies(terms, copies):
    out = jax.ShapeDtypeStruct((copies, *terms[0].shape), jnp.bfloat16)
    return call(sum_body, [out], [], *terms)[0]


def step_body(scalars, layer, *refs):
    blocks = refs[:FOUR]
    out, made, sems = refs[-3:]
    part, place = scalars[0], scalars[1]
    chunks = blocks[0].shape[0] // CHUNK
    size = FOUR * CHUNK
    copies = []
    for i in range(chunks):
        for k, block in enumerate(blocks):
            rows = pl.ds(pl.multiple_of(i * size + (place ^ k) * CHUNK, CHUNK), CHUNK)
            change = block[i * CHUNK : (i + 1) * CHUNK].astype(jnp.float32)
            made[rows] = layer[part, rows].astype(jnp.float32) - step_size * change
        at = pl.ds(i * size, size)
        copies.append(pltpu.make_async_copy(made.at[at], out.at[part, at], sems.at[i]))
        copies[-1].start()
    for copy in copies:
        copy.wait()


def step(part, place, layer, blocks, *stepped):
    return pl.pallas_call(
        step_body,
        out_shape=jax.ShapeDtypeStruct(layer.shape, jnp.float32),
        in_specs=[pl.BlockSpec(memory_space=pltpu.SMEM)] + [VMEM] * (1 + FOUR)
        + [pl.BlockSpec(memory_space=pltpu.HBM)] * len(stepped),
        out_specs=pl.BlockSpec(memory_space=pltpu.HBM),
        scratch_shapes=[pltpu.VMEM(layer.shape[1:], jnp.float32), pltpu.SemaphoreType.DMA((4,))],
        input_output_aliases={2 + FOUR: 0} if stepped else {},
        compiler_params=pltpu.CompilerParams(vmem_limit_bytes=24 * 1024 * 1024),
    )(jnp.stack([part, place]).astype(jnp.int32), layer, *blocks, *stepped)


def per_device(volume, probe_wave, amplitudes, offsets, column_starts, counts, angle_ids):
    layer = volume.reshape(volume.shape[0], *volume.shape[2:])
    tile_rows, columns = layer.shape[1:]
    width = amplitudes.shape[-1]
    slots = offsets.shape[3]
    angles, slabs, tiles = (lax.axis_size(axis) for axis in ("angle", "slab", "tile"))
    slab, angle = lax.axis_index("slab"), lax.axis_index("angle")
    f32, bf16 = jnp.float32, jnp.bfloat16
    tables = dft_tables(width)
    patterns = amplitudes.reshape(slots, width, width)

    core, place_z = angle % 2, angle // 2 % 4
    eight_groups = [[8 * f + i for i in range(8)] for f in range(angles // 8)]
    four_groups = [[8 * f + 2 * q + c for q in range(4)] for f in range(angles // 8) for c in range(2)]
    block_rows = tile_rows // 4

    def swap(value, by):
        return lax.ppermute(value, "angle", [(i, i ^ by) for i in range(angles)])

    def mirrored(value, by):
        pairs = [
            (a * tiles + t, (angles - 2 - (a - a % 2) + a % 2) * tiles + t + by)
            for a in range(angles)
            for t in range(tiles)
            if 0 <= t + by < tiles
        ]
        return lax.ppermute(value, ("angle", "tile"), pairs)

    def to_slab(value, by):
        return lax.ppermute(value, "slab", [(i, (i + by) % slabs) for i in range(slabs)])

    def to_eight(value):
        return lax.all_to_all(value, "angle", 0, 0, axis_index_groups=eight_groups, tiled=True)

    def to_four(value):
        return lax.all_to_all(value, "angle", 0, 0, axis_index_groups=four_groups, tiled=True)

    def to_slabs(value):
        return lax.all_to_all(value, "slab", 0, 0, tiled=True)

    def of_slabs(block):
        return [block] + [to_slab(block, k) for k in range(1, slabs)]

    def over_slabs(kept, *sent):
        return sum((to_slab(block, k + 1).astype(f32) for k, block in enumerate(sent)), kept)

    def live_to_eight(value, axis):
        def first(value):
            sent = to_eight(lax.slice_in_dim(value, 0, 1, axis=axis))
            return jnp.concatenate([sent, lax.slice_in_dim(value, 1, slots, axis=axis)], axis=axis)

        return lax.cond(more, to_eight, first, value)

    own_part = lax.dynamic_index_in_dim(layer, core, 0, keepdims=False)

    own_part = own_part.reshape(-1, FOUR, CHUNK, columns)

    def rows_of(place):
        return lax.dynamic_index_in_dim(own_part, place, 1, keepdims=False).reshape(block_rows, columns)

    after = mirrored(rows_of(3 - place_z), -1)
    own = rows_of(place_z)

    slot_rows, count = offsets.reshape(slots), counts.reshape(1)
    meta = facts_line(slot_rows, column_starts.reshape(slots), count, angle_ids)
    eight = to_eight(meta)
    facts = (eight, slab.reshape(1).astype(jnp.int32))
    more = jnp.max(eight[:, 5 : 3 * slots : 3]) > 0
    own = of_slabs(own)
    after, own = lax.optimization_barrier((after, own))
    own = cut_windows(facts, own, 8, slots, width)
    after = to_slabs(sum_copies([after], slabs))
    after, own = lax.optimization_barrier((after, own))
    place = place_z.reshape(1).astype(jnp.int32)
    windows = live_to_eight(cut_rest(facts, place, after, own, tile_rows), 1)

    own, after = patch_gradients(slot_rows, count, windows, probe_wave, patterns, tables)
    after, own = lax.optimization_barrier((live_to_eight(after, 1), own))
    own = to_eight(own)
    spill = mirrored(over_slabs(*place_windows(facts, after, slabs, columns)).astype(bf16), 1)
    own = to_slabs(place_windows(facts, own, slabs, columns, together=True)[0])
    own = jnp.sum(own.astype(f32), axis=0)

    total = lax.optimization_barrier((own + spill.astype(f32)).astype(bf16))
    total = sum_copies([total, swap(total, 8)], 1)[0]
    blocks = [total] + [swap(total, k << 1) for k in range(1, FOUR)]
    others = [swap(block, 1) for block in blocks]
    new = step(core, place_z, layer, blocks)
    return step(1 - core, place_z, layer, others, new).reshape(volume.shape)


def solution(mesh):
    in_specs = (
        P(None, "slab", "tile", None),
        P(),
        P("angle", "tile", "slab", None, None, None),
        P("angle", "tile", "slab", None),
        P("angle", "tile", "slab", None),
        P("angle", "tile", "slab"),
        P("angle"),
    )
    out_specs = P(None, "slab", "tile", None)
    return jax.shard_map(
        per_device, mesh=mesh, in_specs=in_specs, out_specs=out_specs, check_vma=False
    )
```

```python
import functools

import jax
import jax.numpy as jnp
import ml_dtypes
import numpy as np
from jax import lax
from jax.experimental import pallas as pl
from jax.experimental.pallas import tpu as pltpu
from jax.sharding import PartitionSpec as P

angle_center = 600
shear_divisor = 64
step_size = 0.03
floor_square = 0.25

LANE = 128
CHUNK = 16
FOUR = 4


def dft_tables(plane_width):
    index_line = np.arange(plane_width, dtype=np.int32)
    product_mod = np.mod(index_line[:, None] * index_line[None, :], plane_width)
    phase_table = product_mod.astype(np.float32) * np.float32(2.0 * 3.141592653589793 / plane_width)
    scale_factor = np.float32(plane_width ** (-0.5))
    table_real = (np.cos(phase_table) * scale_factor).astype(ml_dtypes.bfloat16)
    table_imag = (-np.sin(phase_table) * scale_factor).astype(ml_dtypes.bfloat16)
    return table_real, table_imag


def dot(left, right):
    return jnp.dot(left, right, preferred_element_type=jnp.float32)


def one_hot(rows, columns, down):
    row = lax.broadcasted_iota(jnp.int32, (rows, columns), 0)
    column = lax.broadcasted_iota(jnp.int32, (rows, columns), 1)
    return (row - column == down).astype(jnp.float32).astype(jnp.bfloat16)


VMEM = pl.BlockSpec(memory_space=pltpu.VMEM)


def call(body, out_shape, scratch, *args):
    smem = pl.BlockSpec(memory_space=pltpu.SMEM)
    return pl.pallas_call(
        body,
        out_shape=out_shape,
        in_specs=[smem if x.dtype == jnp.int32 else VMEM for x in args],
        out_specs=[VMEM] * len(out_shape),
        scratch_shapes=scratch,
        compiler_params=pltpu.CompilerParams(vmem_limit_bytes=24 * 1024 * 1024),
    )(*args)


def facts_body(rows_in, columns_in, count_in, index_in, out, rows_ref, columns_ref, count_ref, index_ref, sems):
    pairs = zip((rows_in, columns_in, count_in, index_in), (rows_ref, columns_ref, count_ref, index_ref))
    copies = [pltpu.make_async_copy(ref, to, sems.at[n]) for n, (ref, to) in enumerate(pairs)]
    for copy in copies:
        copy.start()
    for copy in copies:
        copy.wait()
    values = []
    for slot in range(rows_ref.shape[0]):
        values += [rows_ref[slot], columns_ref[slot], (slot < count_ref[0]).astype(jnp.int32)]
    lane = lax.broadcasted_iota(jnp.int32, out.shape, 1)
    line = jnp.zeros(out.shape, jnp.int32)
    for n, value in enumerate(values + [index_ref[0]]):
        line = jnp.where(lane == n, value, line)
    out[...] = line


def facts_line(*args):
    return pl.pallas_call(
        facts_body,
        out_shape=jax.ShapeDtypeStruct((8, LANE), jnp.int32),
        in_specs=[pl.BlockSpec(memory_space=pltpu.HBM)] * len(args),
        out_specs=VMEM,
        scratch_shapes=[pltpu.SMEM(x.shape, jnp.int32) for x in args] + [pltpu.SemaphoreType.DMA((len(args),))],
    )(*args)


class Facts:
    def __init__(self, ref, slab_ref, slots, slabs, columns):
        self.ref, self.slab, self.slots, self.slabs, self.columns = ref, slab_ref[0], slots, slabs, columns

    def slot(self, angle, slot):
        return tuple(self.ref[angle, 3 * slot + i] for i in range(3))

    def layer(self, step):
        layer = self.slab + step
        layer = jnp.where(layer < 0, layer + self.slabs, layer)
        return jnp.where(layer >= self.slabs, layer - self.slabs, layer)

    def columns_of(self, angle, slot, layer):
        index = self.ref[angle, 3 * self.slots]
        shift = ((index - angle_center) * (layer - self.slabs // 2)) >> (shear_divisor.bit_length() - 1)
        left = self.slot(angle, slot)[1] + shift
        left = jnp.where(left < 0, left + self.columns, left)
        left = jnp.where(left >= self.columns, left - self.columns, left)
        starts = []
        for i in range(3):
            start = (left & -LANE) + i * LANE
            start = jnp.where(start >= self.columns, start - self.columns, start)
            starts.append(pl.multiple_of(start, LANE))
        return starts, left & (LANE - 1)


def needed(row, chunk, width, tile_rows):
    first = chunk * CHUNK
    return first + CHUNK > row, first + tile_rows < row + width


def cut_body(absolute, put, angles, slots, facts_ref, slab_ref, *refs):
    blocks, out = refs[:-1], refs[-1]
    rows = blocks[0].shape[0]
    facts = Facts(facts_ref, slab_ref, slots, len(blocks), blocks[0].shape[1])
    lane = lax.broadcasted_iota(jnp.int32, (rows, LANE), 1)
    for slot in range(slots):
        for angle in range(angles):

            @pl.when(facts.slot(angle, slot)[2] > 0)
            def _():
                total = [jnp.zeros((rows, LANE), jnp.float32)] * 2
                for k, block in enumerate(blocks):
                    layer = k if absolute else facts.layer(-k)
                    starts, inside = facts.columns_of(angle, slot, layer)
                    turned = [
                        pltpu.roll(block[:, pl.ds(start, LANE)], (LANE - inside) & (LANE - 1), 1)
                        for start in starts
                    ]
                    here = lane < LANE - inside
                    total = [
                        t + jnp.where(here, turned[i], turned[i + 1]).astype(jnp.float32)
                        for i, t in enumerate(total)
                    ]
                put(out, angle, slot, jnp.concatenate(total, axis=1).astype(jnp.bfloat16))


def cut_windows(facts, blocks, angles, slots, width):
    out = jax.ShapeDtypeStruct((angles, slots, blocks[0].shape[0], width), jnp.bfloat16)

    def put(out, angle, slot, window):
        out[angle, slot] = window

    return call(functools.partial(cut_body, False, put, angles, slots), [out], [], *facts, *blocks)[0]


def cut_rest(facts, place_z, blocks, done, tile_rows):
    angles, slots, rows, width = done.shape
    chunks = rows // CHUNK
    out = jax.ShapeDtypeStruct((angles, slots, chunks + 2, CHUNK, width), jnp.bfloat16)

    def body(place_ref, facts_ref, slab_ref, blocks, done, out):
        facts = Facts(facts_ref, slab_ref, slots, blocks.shape[0], blocks.shape[2])

        def put(out, angle, slot, window):
            row = facts.slot(angle, slot)[0]
            extra = chunks
            for i in range(chunks):
                own, after = needed(row, place_ref[0] + FOUR * i, width, tile_rows)
                piece = window[i * CHUNK : (i + 1) * CHUNK]
                out[angle, slot, i] = done[angle, slot, i * CHUNK : (i + 1) * CHUNK]

                @pl.when(jnp.logical_not(own))
                def _():
                    out[angle, slot, i] = piece

                both = jnp.logical_and(own, after)

                @pl.when(both)
                def _():
                    out[angle, slot, extra] = piece

                extra = extra + both.astype(jnp.int32)

        cut_body(
            True, put, angles, slots, facts_ref, slab_ref, *(blocks.at[k] for k in range(blocks.shape[0])), out
        )

    return call(body, [out], [], place_z, *facts, blocks, done)[0]


def cos_sin(angle):
    turns = jnp.round(angle * 0.6366197723675814)
    rest = angle - turns * 1.5703125
    rest = rest - turns * 4.837512969970703e-4
    rest = rest - turns * 7.549789948768648e-8
    square = rest * rest
    sine = (-1.9515295891e-4 * square + 8.3321608736e-3) * square - 1.6666654611e-1
    sine = sine * square * rest + rest
    cosine = (2.443315711809948e-5 * square - 1.388731625493765e-3) * square + 4.166664568298827e-2
    cosine = cosine * square * square - 0.5 * square + 1.0
    quarter = turns.astype(jnp.int32)
    odd = (quarter & 1) == 1
    first, second = jnp.where(odd, sine, cosine), jnp.where(odd, cosine, sine)
    return (
        jnp.where(((quarter + 1) & 2) == 2, -first, first),
        jnp.where((quarter & 2) == 2, -second, second),
    )


def patch_body(row_ref, count_ref, windows, probe, patterns, wr_ref, wi_ref, own_out, next_out):
    angles, slots, chunks, _, width = windows.shape
    chunks = chunks - 2
    tile_rows = FOUR * chunks * CHUNK
    f32, bf16 = jnp.float32, jnp.bfloat16
    tall = 2 * tile_rows
    for slot in range(slots):
        row = row_ref[slot]

        @pl.when(slot < count_ref[0])
        def _():
            pick = one_hot(width, tall, -row)
            window = []
            after_at = [[None] * FOUR for _ in range(chunks)]
            for k in range(FOUR):
                extra = chunks
                for i in range(chunks):
                    own, after = needed(row, k + FOUR * i, width, tile_rows)
                    both = jnp.logical_and(own, after)
                    after_at[i][k] = jnp.where(both, extra, i)
                    extra = extra + both.astype(jnp.int32)
            for part in range(2):
                order = [(i, k) for i in range(chunks) for k in range(FOUR)]
                held = [windows[2 * k + part, slot, i] for i, k in order]
                held += [windows[2 * k + part, slot, after_at[i][k]] for i, k in order]
                window.append(dot(pick, jnp.concatenate(held, axis=0)))
            phase, absorption = window
            magnitude = jnp.exp(-absorption)
            cosine, sine = cos_sin(phase)
            trans_real = magnitude * cosine
            trans_imag = magnitude * sine
            probe_real, probe_imag = probe[0], probe[1]
            wr, wi = wr_ref[...], wi_ref[...]
            wave_real = (probe_real * trans_real - probe_imag * trans_imag).astype(bf16)
            wave_imag = (probe_real * trans_imag + probe_imag * trans_real).astype(bf16)
            left_real = (dot(wr, wave_real) - dot(wi, wave_imag)).astype(bf16)
            left_imag = (dot(wr, wave_imag) + dot(wi, wave_real)).astype(bf16)
            far_real = dot(left_real, wr) - dot(left_imag, wi)
            far_imag = dot(left_real, wi) + dot(left_imag, wr)
            power = far_real * far_real + far_imag * far_imag + floor_square
            keeping = 1.0 - patterns[slot].astype(f32) * lax.rsqrt(power)
            resid_real = (far_real * keeping).astype(bf16)
            resid_imag = (far_imag * keeping).astype(bf16)
            back_real = (dot(wr, resid_real) + dot(wi, resid_imag)).astype(bf16)
            back_imag = (dot(wr, resid_imag) - dot(wi, resid_real)).astype(bf16)
            exit_real = dot(back_real, wr) + dot(back_imag, wi)
            exit_imag = dot(back_imag, wr) - dot(back_real, wi)
            mixed_real = probe_real * exit_real + probe_imag * exit_imag
            mixed_imag = probe_real * exit_imag - probe_imag * exit_real
            final_real = trans_real * mixed_real + trans_imag * mixed_imag
            final_imag = trans_real * mixed_imag - trans_imag * mixed_real
            put = one_hot(tall, width, row)
            for part, value in enumerate((final_imag, -final_real)):
                placed = dot(put, value.astype(bf16)).astype(bf16)
                for i, k in order:
                    at, first = slice(i * CHUNK, (i + 1) * CHUNK), (FOUR * i + k) * CHUNK
                    own_out[2 * k + part, slot, at] = placed[first : first + CHUNK]
                    below = placed[tile_rows + first : tile_rows + first + CHUNK]
                    next_out[2 * (FOUR - 1 - k) + part, slot, at] = below


def patch_gradients(slot_rows, count, windows, probe_wave, patterns, tables):
    angles, slots, chunks, _, width = windows.shape
    out = jax.ShapeDtypeStruct((angles, slots, (chunks - 2) * CHUNK, width), jnp.bfloat16)
    return call(patch_body, [out, out], [], slot_rows, count, windows, probe_wave, patterns, *tables)


def place_body(facts_ref, slab_ref, windows, *refs):
    outs, total = refs[:-1], refs[-1]
    angles, slots, rows, width = windows.shape
    slabs = total.shape[0]
    facts = Facts(facts_ref, slab_ref, slots, slabs, total.shape[2])
    lane = lax.broadcasted_iota(jnp.int32, (rows, LANE), 1)
    total[...] = jnp.zeros_like(total)
    for slot in range(slots):
        for angle in range(angles):

            @pl.when(facts.slot(angle, slot)[2] > 0)
            def _():
                window = windows[angle, slot].astype(jnp.float32)
                for k in range(slabs):
                    layer = facts.layer(k) if len(outs) > 1 else k
                    starts, inside = facts.columns_of(angle, slot, layer)
                    first, second = (pltpu.roll(window[:, i * LANE : (i + 1) * LANE], inside, 1) for i in range(2))
                    there = lane < inside
                    total[k, :, pl.ds(starts[0], LANE)] += jnp.where(there, 0.0, first)
                    total[k, :, pl.ds(starts[1], LANE)] += jnp.where(there, first, second)
                    total[k, :, pl.ds(starts[2], LANE)] += jnp.where(there, second, 0.0)
    for k, out in enumerate(outs):
        out[...] = (total[k] if len(outs) > 1 else total[...]).astype(out.dtype)


def place_windows(facts, windows, slabs, columns, together=False):
    shape = (windows.shape[2], columns)
    outs = [jax.ShapeDtypeStruct(shape, jnp.bfloat16 if k else jnp.float32) for k in range(slabs)]
    if together:
        outs = [jax.ShapeDtypeStruct((slabs, *shape), jnp.bfloat16)]
    return call(place_body, outs, [pltpu.VMEM((slabs, *shape), jnp.float32)], *facts, windows)


def sum_body(*refs):
    *terms, out = refs
    total = terms[0][...]
    if len(terms) > 1:
        total = sum(term[...].astype(jnp.float32) for term in terms).astype(out.dtype)
    for k in range(out.shape[0]):
        out[k] = total


def sum_copies(terms, copies):
    out = jax.ShapeDtypeStruct((copies, *terms[0].shape), jnp.bfloat16)
    return call(sum_body, [out], [], *terms)[0]


def step_body(scalars, layer, *refs):
    blocks, (out, made, sems) = refs[:-3], refs[-3:]
    core, place = scalars[0], scalars[1]
    chunks = blocks[0].shape[0] // CHUNK
    size = FOUR * CHUNK
    copies = []
    for turn in range(2):
        part = core ^ turn
        for i in range(chunks):
            for k in range(FOUR):
                rows = pl.ds(pl.multiple_of(i * size + (place ^ k) * CHUNK, CHUNK), CHUNK)
                change = blocks[turn * FOUR + k][i * CHUNK : (i + 1) * CHUNK].astype(jnp.float32)
                made[turn, rows] = layer[part, rows].astype(jnp.float32) - step_size * change
            at = pl.ds(i * size, size)
            copies.append(pltpu.make_async_copy(made.at[turn, at], out.at[part, at], sems.at[turn, i]))
            copies[-1].start()
    for copy in copies:
        copy.wait()


def step(core, place, layer, blocks):
    return pl.pallas_call(
        step_body,
        out_shape=jax.ShapeDtypeStruct(layer.shape, jnp.float32),
        in_specs=[pl.BlockSpec(memory_space=pltpu.SMEM)] + [VMEM] * (1 + len(blocks)),
        out_specs=pl.BlockSpec(memory_space=pltpu.HBM),
        scratch_shapes=[pltpu.VMEM(layer.shape, jnp.float32), pltpu.SemaphoreType.DMA((2, 4))],
        compiler_params=pltpu.CompilerParams(vmem_limit_bytes=24 * 1024 * 1024),
    )(jnp.stack([core, place]).astype(jnp.int32), layer, *blocks)


def per_device(volume, probe_wave, amplitudes, offsets, column_starts, counts, angle_ids):
    layer = volume.reshape(volume.shape[0], *volume.shape[2:])
    tile_rows, columns = layer.shape[1:]
    width = amplitudes.shape[-1]
    slots = offsets.shape[3]
    angles, slabs, tiles = (lax.axis_size(axis) for axis in ("angle", "slab", "tile"))
    slab, angle = lax.axis_index("slab"), lax.axis_index("angle")
    f32, bf16 = jnp.float32, jnp.bfloat16
    tables = dft_tables(width)
    patterns = amplitudes.reshape(slots, width, width)

    core, place_z = angle % 2, angle // 2 % 4
    eight_groups = [[8 * f + i for i in range(8)] for f in range(angles // 8)]
    four_groups = [[8 * f + 2 * q + c for q in range(4)] for f in range(angles // 8) for c in range(2)]
    block_rows = tile_rows // 4

    def swap(value, by):
        return lax.ppermute(value, "angle", [(i, i ^ by) for i in range(angles)])

    def mirrored(value, by):
        pairs = [
            (a * tiles + t, (angles - 2 - (a - a % 2) + a % 2) * tiles + t + by)
            for a in range(angles)
            for t in range(tiles)
            if 0 <= t + by < tiles
        ]
        return lax.ppermute(value, ("angle", "tile"), pairs)

    def to_slab(value, by):
        return lax.ppermute(value, "slab", [(i, (i + by) % slabs) for i in range(slabs)])

    def to_eight(value):
        return lax.all_to_all(value, "angle", 0, 0, axis_index_groups=eight_groups, tiled=True)

    def to_four(value):
        return lax.all_to_all(value, "angle", 0, 0, axis_index_groups=four_groups, tiled=True)

    def to_slabs(value):
        return lax.all_to_all(value, "slab", 0, 0, tiled=True)

    def of_slabs(block):
        return [block] + [to_slab(block, k) for k in range(1, slabs)]

    def over_slabs(kept, *sent):
        return sum((to_slab(block, k + 1).astype(f32) for k, block in enumerate(sent)), kept)

    def live_to_eight(value, axis):
        def first(value):
            sent = to_eight(lax.slice_in_dim(value, 0, 1, axis=axis))
            return jnp.concatenate([sent, lax.slice_in_dim(value, 1, slots, axis=axis)], axis=axis)

        return lax.cond(more, to_eight, first, value)

    own_part = lax.dynamic_index_in_dim(layer, core, 0, keepdims=False)

    own_part = own_part.reshape(-1, FOUR, CHUNK, columns)

    def rows_of(place):
        return lax.dynamic_index_in_dim(own_part, place, 1, keepdims=False).reshape(block_rows, columns)

    after = mirrored(rows_of(3 - place_z), -1)
    own = rows_of(place_z)

    slot_rows, count = offsets.reshape(slots), counts.reshape(1)
    meta = facts_line(slot_rows, column_starts.reshape(slots), count, angle_ids)
    eight = to_eight(meta)
    facts = (eight, slab.reshape(1).astype(jnp.int32))
    more = jnp.max(eight[:, 5 : 3 * slots : 3]) > 0
    own = of_slabs(own)
    after, own = lax.optimization_barrier((after, own))
    own = cut_windows(facts, own, 8, slots, width)
    after = to_slabs(sum_copies([after], slabs))
    after, own = lax.optimization_barrier((after, own))
    place = place_z.reshape(1).astype(jnp.int32)
    windows = live_to_eight(cut_rest(facts, place, after, own, tile_rows), 1)

    own, after = patch_gradients(slot_rows, count, windows, probe_wave, patterns, tables)
    after, own = lax.optimization_barrier((live_to_eight(after, 1), own))
    own = to_eight(own)
    spill = mirrored(over_slabs(*place_windows(facts, after, slabs, columns)).astype(bf16), 1)
    own = to_slabs(place_windows(facts, own, slabs, columns, together=True)[0])
    own = jnp.sum(own.astype(f32), axis=0)

    total = lax.optimization_barrier((own + spill.astype(f32)).astype(bf16))
    total = sum_copies([total, swap(total, 8)], 1)[0]
    blocks = [total] + [swap(total, k << 1) for k in range(1, FOUR)]
    others = [swap(block, 1) for block in blocks]
    return step(core, place_z, layer, blocks + others).reshape(volume.shape)


def solution(mesh):
    in_specs = (
        P(None, "slab", "tile", None),
        P(),
        P("angle", "tile", "slab", None, None, None),
        P("angle", "tile", "slab", None),
        P("angle", "tile", "slab", None),
        P("angle", "tile", "slab"),
        P("angle"),
    )
    out_specs = P(None, "slab", "tile", None)
    return jax.shard_map(
        per_device, mesh=mesh, in_specs=in_specs, out_specs=out_specs, check_vma=False
    )
```
